32 devices in a mesh: fsdp: 32 (over z, y, x, core).
Axes of the slice: x: 2, y: 2, z: 4, core: 2. Of those that a mesh axis runs over, the one named last changes fastest.
Arguments:
- layer_in: bfloat16 [64, 416, 768], P('fsdp'), may hold values from -24 to 24
- pair_ids: int32 [64, 416], P('fsdp'), may hold values from 0 to 2, as said below
- pair_lengths: int32 [64, 3, 2], P('fsdp'), may hold values from 1 to 273, as said below
- attn_shard: bfloat16 [2363392], P('fsdp'), may hold values from -2 to 2
- ffn_shard: bfloat16 [4726784], P('fsdp'), may hold values from -2 to 2
- out_grad: bfloat16 [64, 416, 768], P('fsdp'), may hold values from -8 to 8
Outputs:
- layer_out: bfloat16 [64, 416, 768], P('fsdp')
- in_grad: float32 [64, 416, 768], P('fsdp')
- attn_grad: float32 [2363392], P('fsdp')
- ffn_grad: float32 [4726784], P('fsdp')
- out_bias_grad: float32 [768], replicated
The draws below stay inside these ranges and needn't reach their ends.
Inputs may be any that keep to these rules, and one draw needn't show every extreme that they name: `pair_ids`: ids never decrease along a row, and every id of 0 to 2 occupies a run of slots in every row. `pair_lengths`: [.., 0] counts text slots and [.., 1] region slots; their sum is at most the pair's run of slots, and the live slots are the first ones of the run.
All inputs are finite; a program needn't handle non-finite values.
Results may differ from the reference program's by a relative error of at most 0.014.
The reference program's roundings to bfloat16 on the way count: a program that leaves them out, or rounds other values in their place, can miss the bound.
Values may be sent and summed in bfloat16 or wider, within the bound.
A program may use at most 192 MiB of HBM per device.

```python
import math
import jax
import jax.numpy as jnp
from jax import lax

D = 768
HEADS = 12
HEAD_DIM = 64
FF = 3072
SLOTS = 416
PAIRS = 3
ROWS = 64
ATT_PAD = 2363392
FFN_PAD = 4726784


def chosen_row(key):
    return jax.random.randint(jax.random.fold_in(key, 7), (), 0, ROWS, dtype=jnp.int32)


def row_cuts(key):
    first_key, second_key = jax.random.split(key)
    lowest = SLOTS // 8
    highest = 3 * SLOTS // 8 + 1
    cut_first = jax.random.randint(first_key, (ROWS, 1), lowest, highest, dtype=jnp.int32)
    cut_second = cut_first + jax.random.randint(second_key, (ROWS, 1), lowest, highest, dtype=jnp.int32)
    picked = jnp.arange(ROWS, dtype=jnp.int32)[:, None] == chosen_row(key)
    cut_first = jnp.where(picked, lowest, cut_first)
    cut_second = jnp.where(picked, 2 * lowest, cut_second)
    return (cut_first, cut_second)


def draw_pair_ids(key, part):
    cut_first, cut_second = row_cuts(key)
    places = jnp.arange(SLOTS, dtype=jnp.int32)[None, :]
    return (places >= cut_first).astype(jnp.int32) + (places >= cut_second).astype(jnp.int32)


def draw_pair_lengths(key, part):
    cut_first, cut_second = row_cuts(key)
    picked_row = jnp.arange(ROWS, dtype=jnp.int32)[:, None] == chosen_row(key)
    picked_pair = picked_row & (jnp.arange(PAIRS, dtype=jnp.int32)[None, :] == PAIRS - 1)
    key = jax.random.fold_in(key, 5)
    text_key, fill_key, region_key = jax.random.split(key, 3)
    pair_spans = jnp.concatenate([cut_first, cut_second - cut_first, SLOTS - cut_second], axis=1)
    text_least = jnp.maximum(pair_spans // 8, 1)
    text_len = jax.random.randint(text_key, (ROWS, PAIRS), text_least, pair_spans // 2 + 1, dtype=jnp.int32)
    text_len = jnp.where(picked_pair, text_least, text_len)
    fill_level = jax.random.randint(fill_key, (ROWS, 1), 2, 5, dtype=jnp.int32)
    fill_level = jnp.where(picked_row, 4, fill_level)
    region_top = (pair_spans - text_len) * fill_level // 4
    region = jax.random.randint(region_key, (ROWS, PAIRS), jnp.maximum(region_top // 2, 1), region_top + 1, dtype=jnp.int32)
    region = jnp.where(picked_pair, region_top, region)
    return jnp.stack([text_len, region], axis=-1)


def draw_layer_in(key, part):
    key = jax.random.fold_in(key, 11)
    column_key, row_key, base_key = jax.random.split(key, 3)
    columns = jnp.exp(jax.random.uniform(column_key, (1, 1, D), jnp.float32, math.log(0.3), math.log(3.0)))
    rows_scale = jnp.exp(jax.random.uniform(row_key, (ROWS, 1, 1), jnp.float32, math.log(0.5), math.log(2.0)))
    base_draw = jax.random.truncated_normal(base_key, -4.0, 4.0, (ROWS, SLOTS, D), jnp.float32)
    return (base_draw * columns * rows_scale).astype(jnp.bfloat16)


def draw_out_grad(key, part):
    key = jax.random.fold_in(key, 13)
    scale_key, base_key = jax.random.split(key)
    row_scale = jnp.exp(jax.random.uniform(scale_key, (ROWS, SLOTS, 1), jnp.float32, math.log(0.5), math.log(2.0)))
    base_draw = jax.random.truncated_normal(base_key, -4.0, 4.0, (ROWS, SLOTS, D), jnp.float32)
    return (base_draw * row_scale).astype(jnp.bfloat16)


def flat_draw(key, pieces, total):
    scales = jnp.concatenate([jnp.full((amount,), spread, jnp.float32) for amount, spread, centre in pieces])
    centres = jnp.concatenate([jnp.full((amount,), centre, jnp.float32) for amount, spread, centre in pieces])
    base_draw = jax.random.truncated_normal(key, -4.0, 4.0, (total,), jnp.float32)
    return (base_draw * scales + centres).astype(jnp.bfloat16)


def draw_attn_shard(key, part):
    key = jax.random.fold_in(key, 17)
    out_fan = 4 * D // SLOTS
    pieces = [(3 * D * D, D ** (-0.5), 0.0), (D * D, out_fan ** (-0.5), 0.0), (D, 0.2, 0.0), (D, 0.2, 0.0), (D, 0.2, 0.0), (D, 0.1, 1.0), (D, 0.2, 0.0), (ATT_PAD - 4 * D * D - 5 * D, 0.1, 0.0)]
    return flat_draw(key, pieces, ATT_PAD)


def draw_ffn_shard(key, part):
    key = jax.random.fold_in(key, 19)
    pieces = [(D * FF, D ** (-0.5), 0.0), (FF, 0.2, 0.0), (FF * D, FF ** (-0.5), 0.0), (D, 0.2, 0.0), (D, 0.1, 1.0), (D, 0.2, 0.0), (FFN_PAD - 2 * D * FF - FF - 3 * D, 0.1, 0.0)]
    return flat_draw(key, pieces, FFN_PAD)


def setup_inputs(seed: int = 0) -> dict:
    key_list = jax.random.split(jax.random.key(seed), 7)
    return {
        "layer_in": draw_layer_in(jax.random.fold_in(key_list[6], 71), 0),
        "pair_ids": draw_pair_ids(jax.random.fold_in(key_list[6], 71), 0),
        "pair_lengths": draw_pair_lengths(jax.random.fold_in(key_list[6], 71), 0),
        "attn_shard": draw_attn_shard(jax.random.fold_in(key_list[6], 71), 0),
        "ffn_shard": draw_ffn_shard(jax.random.fold_in(key_list[6], 71), 0),
        "out_grad": draw_out_grad(jax.random.fold_in(key_list[6], 71), 0),
    }


@jax.custom_vjp
def low(v):
    return lax.optimization_barrier(v.astype(jnp.bfloat16)).astype(jnp.float32)

@jax.custom_vjp
def low_back(v):
    return v

def low_keep(v):
    return (low(v), None)

def low_pass(kept, grad):
    return (grad,)

def back_keep(v):
    return (v, None)

def back_low(kept, grad):
    return (low(grad),)
low.defvjp(low_keep, low_pass)
low_back.defvjp(back_keep, back_low)
NORM_EPS = 1e-12
EXACTLY = lax.Precision.HIGHEST

def unpack_attention(flattened):
    offset = 3 * D * D
    weight_joint = flattened[:offset].reshape(D, 3 * D)
    weight_out = flattened[offset:offset + D * D].reshape(D, D)
    offset = offset + D * D
    vectors = flattened[offset:offset + 5 * D].reshape(5, D)
    return (weight_joint, weight_out, vectors[0], vectors[1], vectors[2], vectors[3], vectors[4])

def unpack_feedforward(flattened):
    offset = D * FF
    weight_in = flattened[:offset].reshape(D, FF)
    bias_in = flattened[offset:offset + FF]
    offset = offset + FF
    weight_back = flattened[offset:offset + FF * D].reshape(FF, D)
    offset = offset + FF * D
    vectors = flattened[offset:offset + 3 * D].reshape(3, D)
    return (weight_in, bias_in, weight_back, vectors[0], vectors[1], vectors[2])

def layer_norm(values, gain_vec, shift_vec):
    row_mean = lax.optimization_barrier(jnp.mean(values, axis=-1, keepdims=True))
    centred = values - row_mean
    row_var = lax.optimization_barrier(jnp.mean(centred * centred, axis=-1, keepdims=True))
    return centred * lax.rsqrt(row_var + NORM_EPS) * gain_vec + shift_vec

def key_mask(pair_ids, pair_lengths):
    labels = jnp.arange(PAIRS, dtype=jnp.int32)
    member = pair_ids[:, :, None] == labels[None, None, :]
    starts = lax.optimization_barrier(jnp.sum((pair_ids[:, :, None] < labels[None, None, :]).astype(jnp.int32), axis=1))
    live_len = pair_lengths[:, :, 0] + pair_lengths[:, :, 1]
    slot_start = lax.optimization_barrier(jnp.sum(jnp.where(member, starts[:, None, :], 0), axis=-1))
    slot_len = lax.optimization_barrier(jnp.sum(jnp.where(member, live_len[:, None, :], 0), axis=-1))
    places = jnp.arange(pair_ids.shape[1], dtype=jnp.int32)[None, :]
    is_live = places - slot_start < slot_len
    return (pair_ids[:, :, None] == pair_ids[:, None, :]) & is_live[:, None, :]

def forward(inputs, attention, feedforward, key_ok):
    weight_joint, weight_out, bias_query, bias_value, bias_out, gain_first, shift_first = unpack_attention(attention)
    weight_in, bias_in, weight_back, bias_back, gain_second, shift_second = unpack_feedforward(feedforward)
    row_count = inputs.shape[0]
    flat_in = inputs.reshape(row_count * SLOTS, D)
    bias_joint = jnp.concatenate([bias_query, jnp.zeros_like(bias_query), bias_value])
    projected = low(low_back(jnp.dot(flat_in, weight_joint, precision=EXACTLY) + bias_joint))
    projected = projected.reshape(row_count, SLOTS, 3, HEADS, HEAD_DIM)
    scores = jnp.einsum('gqhd,gkhd->ghqk', projected[:, :, 0], projected[:, :, 1], precision=EXACTLY) * HEAD_DIM ** (-0.5)
    scores = jnp.where(key_ok[:, None], low_back(scores), -1e+30)
    row_max = lax.optimization_barrier(jnp.max(scores, axis=-1, keepdims=True))
    raised = jnp.exp(scores - row_max)
    shares = raised / lax.optimization_barrier(jnp.sum(raised, axis=-1, keepdims=True))
    context = jnp.einsum('ghqk,gkhd->gqhd', low(shares), projected[:, :, 2], precision=EXACTLY)
    context = low(low_back(context)).reshape(row_count * SLOTS, D)
    attn_out = low_back(jnp.dot(context, weight_out, precision=EXACTLY) + bias_out)
    norm_first = layer_norm(flat_in + attn_out, gain_first, shift_first)
    hidden = low_back(jnp.dot(low(norm_first), weight_in, precision=EXACTLY) + bias_in)
    active = low(jax.nn.gelu(hidden, approximate=False))
    ffn_out = low_back(jnp.dot(active, weight_back, precision=EXACTLY) + bias_back)
    return layer_norm(norm_first + ffn_out, gain_second, shift_second).reshape(row_count, SLOTS, D)

def reference(layer_in, pair_ids, pair_lengths, attn_shard, ffn_shard, out_grad):
    attention = attn_shard.astype(jnp.float32)
    feedforward = ffn_shard.astype(jnp.float32)
    group_rows = 8 if ROWS % 8 == 0 else ROWS
    step_count = ROWS // group_rows
    blocks = (layer_in.reshape(step_count, group_rows, SLOTS, D), pair_ids.reshape(step_count, group_rows, SLOTS), pair_lengths.reshape(step_count, group_rows, PAIRS, 2), out_grad.reshape(step_count, group_rows, SLOTS, D))

    def advance(totals, block_data):
        inputs, ids_block, length_block, cotangent = block_data
        key_ok = key_mask(ids_block, length_block)
        output, pullback = jax.vjp(lambda a, b, c: forward(a, b, c, key_ok), inputs.astype(jnp.float32), attention, feedforward)
        grad_inputs, grad_attention, grad_feed = pullback(cotangent.astype(jnp.float32))
        return ((totals[0] + grad_attention, totals[1] + grad_feed), (output.astype(jnp.bfloat16), grad_inputs))
    initial = (jnp.zeros_like(attention), jnp.zeros_like(feedforward))
    (grad_attention, grad_feed), (outputs, grad_inputs) = lax.scan(advance, initial, blocks)
    bias_start = 4 * D * D + 2 * D
    out_bias_grad = grad_attention[bias_start:bias_start + D]
    return (outputs.reshape(ROWS, SLOTS, D), grad_inputs.reshape(ROWS, SLOTS, D), grad_attention, grad_feed, out_bias_grad)
```

```python
import functools

import jax
import jax.numpy as jnp
from jax import lax
from jax.experimental import pallas as pl
from jax.experimental.pallas import tpu as pltpu
from jax.sharding import PartitionSpec as P

D = 768
HEADS = 12
HEAD_DIM = 64
FF = 3072
SLOTS = 416
PAIRS = 3
LANES = 128
NORM_EPS = 1e-12
F32 = jnp.float32
BF16 = jnp.bfloat16
MESH = pl.DeviceIdType.MESH
VMEM_LIMIT = 62 << 20


def dot_nn(a, b):
    return lax.dot_general(a, b, (((1,), (0,)), ((), ())), preferred_element_type=F32)


def dot_nt(a, b):
    return lax.dot_general(a, b, (((1,), (1,)), ((), ())), preferred_element_type=F32)


def dot_tn(a, b):
    return lax.dot_general(a, b, (((0,), (0,)), ((), ())), preferred_element_type=F32)


def row_mean(v):
    return jnp.sum(v, axis=1, keepdims=True) * (1.0 / D)


def col_sum(v):
    return jnp.sum(v, axis=0, keepdims=True)


class Plan:
    def __init__(self, n, attn_shard_len, ffn_shard_len, row_count):
        self.n = n
        self.nz = n // 8
        self.rows = row_count
        self.tokens = row_count * SLOTS
        self.unit_a = attn_shard_len // LANES
        self.unit_f = ffn_shard_len // LANES
        self.block_a = 4 * D * D // LANES // n
        self.block_f = 2 * D * FF // LANES // n
        self.rows_a = 4 * D // n
        self.rows_f = 2 * FF // n
        self.joint_rows = self.rows_a // 3
        self.joint_src = 3 * n // 4
        self.in_rows = self.rows_f // 4
        self.in_src = n // 2
        self.late_a = 16
        self.late_f = 48
        self.half_a = 32
        self.half_f = 64
        self.gap = FF // LANES
        self.at_attn_vec = divmod(4 * D * D // LANES, self.unit_a)
        self.at_bias_in = divmod(D * FF // LANES, self.unit_f)
        self.at_ffn_vec = divmod(2 * D * FF // LANES + self.gap, self.unit_f)

    def shift_a(self, me):
        return me * (self.unit_a - self.block_a)

    def shift_f(self, me):
        return me * (self.unit_f - self.block_f) - jnp.where(me >= self.in_src, self.gap, 0)

    def fits(self):
        n = self.n
        if n < 16 or n & (n - 1) or 4 * D % n or self.rows_a % 48 or self.rows_f % 64:
            return False
        last_a = (n - 1) * (self.unit_a - self.block_a)
        step_f = self.unit_f - self.block_f
        last_f = max((self.in_src - 1) * step_f, (n - 1) * step_f - self.gap)
        first_f = self.in_src * step_f - self.gap
        self.tail_a = -(-(last_a + 1) // 8) * 8
        self.tail_f = -(-(last_f + 2) // 8) * 8
        vec_a, vec_f = 5 * D // LANES, 3 * D // LANES
        return (
            step_f >= 0
            and self.unit_a >= self.block_a
            and first_f >= 0
            and self.tail_a <= self.block_a
            and self.tail_f <= self.block_f
            and self.at_attn_vec[0] == n - 1
            and self.at_ffn_vec[0] == n - 1
            and self.at_bias_in[0] == self.in_src - 1
            and self.unit_a - self.at_attn_vec[1] <= self.tail_a
            and self.unit_f - self.at_ffn_vec[1] <= self.tail_f
            and self.at_attn_vec[1] + vec_a <= self.unit_a
            and self.at_ffn_vec[1] + vec_f <= self.unit_f
            and self.at_bias_in[1] + self.gap <= self.unit_f
            and self.at_bias_in[1] == self.block_f - (self.in_src - 1) * step_f
            and self.rows_a > self.late_a + self.half_a
            and self.rows_f > self.late_f + self.half_f
        )


class Place:
    def __init__(self, plan):
        self.n, self.nz = plan.n, plan.nz
        me = lax.axis_index("fsdp")
        self.me = me
        self.core = lax.rem(me, 2)
        self.x = lax.rem(me // 2, 2)
        self.y = lax.rem(me // 4, 2)
        self.z = me // 8
        self.sib = me + 1 - 2 * self.core
        self.xn = me + 2 - 4 * self.x
        self.yn = me + 4 - 8 * self.y

    def block(self, column, z, other_core=False):
        x = self.x if column in (0, 2) else 1 - self.x
        y = self.y if column in (0, 1) else 1 - self.y
        core = 1 - self.core if other_core else self.core
        return ((z * 2 + y) * 2 + x) * 2 + core

    def level(self, distance, fn):
        if distance == 0:
            fn(self.z)
            return
        pl.when(self.z >= distance)(lambda: fn(self.z - distance))
        pl.when(self.z + distance < self.nz)(lambda: fn(self.z + distance))

    def onward(self, z, fn):
        pl.when((z <= self.z) & (self.z < self.nz - 1))(lambda: fn(self.me + 8))
        pl.when((z >= self.z) & (self.z > 0))(lambda: fn(self.me - 8))

    def bits(self):
        out = []
        bit = 1
        while bit < self.n:
            out.append(self.me + bit - 2 * bit * lax.rem(self.me // bit, 2))
            bit *= 2
        return out

    def barrier(self):
        sem = pltpu.get_barrier_semaphore()

        def tell(partner):
            pl.semaphore_signal(sem, inc=1, device_id=(partner,), device_id_type=MESH)

        fixed = self.bits()
        for partner in fixed:
            tell(partner)
        z_odd = lax.rem(self.z, 2)
        far_z = (self.z > 0) & (self.z < self.nz - 1)
        far = (self.me > 0) & (self.me < self.n - 1)
        pl.when(far_z)(lambda: tell(self.me - 8 + 16 * z_odd))
        pl.when(far)(lambda: tell(self.me - 1 + 2 * self.core))
        pl.semaphore_wait(sem, len(fixed) + far_z.astype(jnp.int32) + far.astype(jnp.int32))


class Wire:
    def __init__(self, send, recv):
        self.send, self.recv = send, recv
        self.sent = []

    def copy(self, src, dst, number, partner):
        return pltpu.make_async_remote_copy(
            src_ref=src,
            dst_ref=dst,
            send_sem=self.send.at[number],
            recv_sem=self.recv.at[number],
            device_id=(partner,),
            device_id_type=MESH,
        )


def add_over_all(place, wire, base, own, held):
    partners = place.bits()

    def send(s):
        wire.copy(own.at[s], held.at[s], base + s, partners[s]).start()

    def take(s):
        wire.copy(own.at[s], held.at[s], base + s, partners[s]).wait()
        own[s + 1] = own[s] + held[s]

    steps = [lambda: send(0)]
    for s in range(len(partners)):

        def step(s=s):
            take(s)
            if s + 1 < len(partners):
                send(s + 1)

        steps.append(step)
    return steps


def gather_count(nz):
    return 17 * nz + 3


class Gather:
    def __init__(self, place, wire, base, ref, rows, late, half):
        self.p, self.w, self.ref = place, wire, ref
        nz = place.nz
        self.early = (0, rows - late)
        self.late = (rows - late, late)
        self.first = (0, half)
        self.second = (half, rows - late - half)
        self.all = (0, rows)
        at = [base]

        def take(count):
            at[0] += count
            return at[0] - count

        self.line, self.xs, self.ys, self.d1, self.d2 = (take(nz) for _ in range(5))
        self.sib, self.late_line, self.late_sib = (take(4 * nz) for _ in range(3))
        self.px, self.py, self.pd = (take(1) for _ in range(3))

    def at(self, column, z, part):
        return self.ref.at[self.p.block(column, z), pl.ds(*part)]

    def move(self, column, z, part, number, partner):
        ref = self.at(column, z, part)
        return self.w.copy(ref, ref, number, partner)

    def send(self, *args):
        self.move(*args).start()

    def wait(self, column, z, part, number):
        self.move(column, z, part, number, self.p.sib).wait_recv()

    def to_sib(self, column, z):
        self.send(column, z, self.early, self.sib + column * self.p.nz + z, self.p.sib)

    def to_sib_late(self, column, z):
        self.send(column, z, self.late, self.late_sib + column * self.p.nz + z, self.p.sib)

    def spread(self, z):
        p = self.p
        p.onward(z, lambda partner: self.send(0, z, self.early, self.line + z, partner))
        self.send(0, z, self.early, self.xs + z, p.xn)
        self.send(0, z, self.early, self.ys + z, p.yn)
        self.to_sib(0, z)

    def spread_late(self, column, z):
        number = self.late_line + column * self.p.nz + z
        self.p.onward(z, lambda partner: self.send(column, z, self.late, number, partner))
        self.to_sib_late(column, z)

    def take_line(self, z):
        self.wait(0, z, self.early, self.line + z)
        self.spread(z)

    def take_plane(self, z):
        self.wait(1, z, self.early, self.xs + z)
        self.send(1, z, self.first, self.d1 + z, self.p.yn)
        self.to_sib(1, z)
        self.wait(2, z, self.early, self.ys + z)
        self.send(2, z, self.second, self.d2 + z, self.p.xn)
        self.to_sib(2, z)

    def take_corner(self, z):
        self.wait(3, z, self.first, self.d1 + z)
        self.wait(3, z, self.second, self.d2 + z)
        self.to_sib(3, z)

    def take_late(self, z):
        for column in range(4):
            self.wait(column, z, self.late, self.late_line + column * self.p.nz + z)
            self.spread_late(column, z)

    def begin(self):
        p = self.p
        z = p.z
        self.send(0, z, self.late, self.px, p.xn)
        self.send(0, z, self.late, self.py, p.yn)
        self.spread(z)

    def begin_late(self):
        p = self.p
        z = p.z
        self.wait(1, z, self.late, self.px)
        self.send(1, z, self.late, self.pd, p.yn)
        self.spread_late(0, z)
        self.spread_late(1, z)
        self.wait(2, z, self.late, self.py)
        self.spread_late(2, z)

    def corner_late(self):
        self.wait(3, self.p.z, self.late, self.pd)
        self.spread_late(3, self.p.z)

    def steps(self):
        p, nz = self.p, self.p.nz
        out = [self.begin, self.begin_late]
        for d in range(1, nz + 2):
            if d < nz:
                out.append(lambda d=d: p.level(d, self.take_line))
            if d - 1 < nz:
                out.append(lambda d=d: p.level(d - 1, self.take_plane))
            if d == 1:
                out.append(self.corner_late)
            if 0 <= d - 2 < nz:
                out.append(lambda d=d: p.level(d - 2, self.take_corner))
            if 1 <= d - 1 < nz:
                out.append(lambda d=d: p.level(d - 1, self.take_late))
        out.append(self.finish)
        return out

    def finish(self):
        p = self.p
        nz = p.nz

        def one(j, carry):
            for column in range(4):
                ref = self.ref.at[p.block(column, j, True)]
                for part, base in ((self.early, self.sib), (self.late, self.late_sib)):
                    r = ref.at[pl.ds(*part)]
                    self.w.copy(r, r, base + column * nz + j, p.sib).wait_recv()
            return carry

        lax.fori_loop(0, nz, one, 0)

    def drain(self):
        p = self.p
        nz = p.nz

        def sent(column, z, part, number):
            self.move(column, z, part, number, p.sib).wait_send()

        sent(0, p.z, self.late, self.px)
        sent(0, p.z, self.late, self.py)
        sent(1, p.z, self.late, self.pd)

        def one(z, carry):
            p.onward(z, lambda partner: sent(0, z, self.early, self.line + z))
            sent(0, z, self.early, self.xs + z)
            sent(0, z, self.early, self.ys + z)
            sent(1, z, self.first, self.d1 + z)
            sent(2, z, self.second, self.d2 + z)
            for column in range(4):
                number = column * nz + z
                sent(column, z, self.early, self.sib + number)
                sent(column, z, self.late, self.late_sib + number)
                p.onward(z, lambda partner: sent(column, z, self.late, self.late_line + number))
            return carry

        lax.fori_loop(0, nz, one, 0)


class Scatter:
    def __init__(self, place, wire, base, src, rows, late, half, total, room, loaded):
        self.p, self.w, self.src, self.total, self.loaded = place, wire, src, total, loaded
        nz = place.nz
        self.early = (0, rows - late)
        self.late = (rows - late, late)
        self.first = (0, half)
        self.second = (half, rows - late - half)
        (self.side, self.in_first, self.in_second, self.in_x, self.in_y, self.in_line, self.in_late,
         self.in_plane) = room
        at = [base]

        def take(count):
            at[0] += count
            return at[0] - count

        self.sib = take(4 * nz)
        self.d1, self.d2, self.xs, self.ys = (take(nz) for _ in range(4))
        self.line = take(nz + 1)
        self.late_line = take(4 * (nz + 1))
        self.plane = take(3)

    @staticmethod
    def rooms(nz, rows, late, half):
        def room(count, size):
            return pltpu.VMEM((count, size, D), BF16)

        early = rows - late
        return [
            room(4 * nz, rows), room(4 * nz, rows), room(nz, half), room(nz, early - half), room(nz, early),
            room(nz, early), room(nz + 1, early), room(4 * (nz + 1), late), room(3, late),
        ]

    def slot(self, column, z):
        return column * self.p.nz + z

    def sum_of(self, column, z, part):
        return self.total.at[self.slot(column, z), pl.ds(*part)]

    def add(self, target, *terms):
        self.store_sum(target, target, *terms)

    def store_sum(self, target, *terms):
        count = target.shape[0]
        step = count if count <= 48 else next(s for s in (48, 40, 32, 16) if count % s == 0 and s % 16 == 0)

        def some(i, carry):
            rs = pl.ds(pl.multiple_of(i * step, 16), step)
            acc = terms[0][rs, :].astype(F32)
            for term in terms[1:]:
                acc = acc + term[rs, :].astype(F32)
            target[rs, :] = acc.astype(BF16)
            return carry

        lax.fori_loop(0, count // step, some, 0)

    def send_sib(self, z):
        p = self.p
        for column in (3, 1, 2, 0):
            k = self.slot(column, z)
            self.w.copy(
                self.src.at[p.block(column, z, True)], self.side.at[k], self.sib + k, p.sib
            ).start()

    def take_sib(self, column, z):
        k = self.slot(column, z)
        side = self.side.at[k]
        self.w.copy(side, side, self.sib + k, self.p.sib).wait_recv()
        own = self.total.at[k] if self.loaded else self.src.at[self.p.block(column, z)]
        self.store_sum(self.total.at[k], own, side)

    def corner(self, z):
        p = self.p
        self.take_sib(3, z)
        self.w.copy(self.sum_of(3, z, self.first), self.in_first.at[z], self.d1 + z, p.yn).start()
        self.w.copy(self.sum_of(3, z, self.second), self.in_second.at[z], self.d2 + z, p.xn).start()

    def take_rest(self, z):
        for column in (1, 2, 0):
            self.take_sib(column, z)

    def got(self, ref, number):
        self.w.copy(ref, ref, number, self.p.sib).wait_recv()
        return ref

    def sides(self, z):
        p = self.p
        self.add(self.sum_of(1, z, self.first), self.got(self.in_first.at[z], self.d1 + z))
        self.w.copy(self.sum_of(1, z, self.early), self.in_x.at[z], self.xs + z, p.xn).start()
        self.add(self.sum_of(2, z, self.second), self.got(self.in_second.at[z], self.d2 + z))
        self.w.copy(self.sum_of(2, z, self.early), self.in_y.at[z], self.ys + z, p.yn).start()

    def own(self, z):
        self.add(
            self.sum_of(0, z, self.early),
            self.got(self.in_x.at[z], self.xs + z),
            self.got(self.in_y.at[z], self.ys + z),
        )
        self.along(z, self.sum_of(0, z, self.early), self.in_line, self.line, 0)

    def own_late(self, z):
        for column in range(4):
            self.along(z, self.sum_of(column, z, self.late), self.in_late, self.late_line,
                       column * (self.p.nz + 1))

    def along(self, z, ref, room, number, at):
        p, nz = self.p, self.p.nz
        below, above = p.z > 0, p.z < nz - 1

        def take(slot):
            self.add(ref, self.got(room.at[at + slot], number + at + slot))

        pl.when((z >= p.z) & below)(lambda: take(z))
        pl.when((z < p.z) & above)(lambda: take(z))
        pl.when((z == p.z) & above)(lambda: take(nz))

        def send(slot, partner):
            self.w.copy(ref, room.at[at + slot], number + at + slot, partner).start()

        pl.when(z > p.z)(lambda: send(z, p.me + 8))
        pl.when(z < p.z)(lambda: send(jnp.where(z == p.z - 1, nz, z), p.me - 8))

    def plane_corner(self):
        p = self.p
        self.w.copy(self.sum_of(3, p.z, self.late), self.in_plane.at[0], self.plane, p.yn).start()

    def plane_sides(self):
        p = self.p
        self.w.copy(self.sum_of(2, p.z, self.late), self.in_plane.at[2], self.plane + 2, p.yn).start()
        ref = self.sum_of(1, p.z, self.late)
        self.add(ref, self.got(self.in_plane.at[0], self.plane))
        self.w.copy(ref, self.in_plane.at[1], self.plane + 1, p.xn).start()

    def plane_own(self):
        self.add(
            self.sum_of(0, self.p.z, self.late),
            self.got(self.in_plane.at[1], self.plane + 1),
            self.got(self.in_plane.at[2], self.plane + 2),
        )

    def steps(self):
        p, nz = self.p, self.p.nz
        out = []

        def begin():
            for d in range(nz - 1, -1, -1):
                p.level(d, self.send_sib)

        out.append(begin)
        for t in range(nz + 2):
            d = nz - 1 - t
            if d >= 0:
                out.append(lambda d=d: p.level(d, self.corner))
            if 0 <= d + 1 < nz:
                out.append(lambda d=d: p.level(d + 1, self.sides))
            if d >= 0:
                out.append(lambda d=d: p.level(d, self.take_rest))
                out.append(lambda d=d: p.level(d, self.own_late))
            if d == 0:
                out.append(self.plane_corner)
            if d == -1:
                out.append(self.plane_sides)
            if 0 <= d + 2 < nz:
                out.append(lambda d=d: p.level(d + 2, self.own))
        out.append(self.plane_own)
        return out

    def drain(self):
        p, nz = self.p, self.p.nz

        def sent(ref, number):
            self.w.copy(ref, ref, number, p.sib).wait_send()

        for i in range(3):
            sent(self.in_plane.at[i], self.plane + i)

        def one(z, carry):
            for column in range(4):
                k = self.slot(column, z)
                sent(self.side.at[k], self.sib + k)
            sent(self.in_first.at[z], self.d1 + z)
            sent(self.in_second.at[z], self.d2 + z)
            sent(self.in_x.at[z], self.xs + z)
            sent(self.in_y.at[z], self.ys + z)

            def lines(slot):
                sent(self.in_line.at[slot], self.line + slot)
                for column in range(4):
                    at = column * (nz + 1) + slot
                    sent(self.in_late.at[at], self.late_line + at)

            pl.when(z > p.z)(lambda: lines(z))
            pl.when(z < p.z)(lambda: lines(jnp.where(z == p.z - 1, nz, z)))
            return carry

        lax.fori_loop(0, nz, one, 0)


def scatter_count(nz):
    return 4 * nz + 4 * nz + nz + 1 + 4 * (nz + 1) + 3


def build_masks(plan, ids_ref, len_ref, key_add, query_one):
    for r in range(plan.rows):
        ids = jnp.broadcast_to(ids_ref[r : r + 1, :], (LANES, SLOTS))
        label = lax.broadcasted_iota(jnp.int32, (LANES, SLOTS), 0)
        place = lax.broadcasted_iota(jnp.int32, (LANES, SLOTS), 1)
        start = jnp.sum((ids < label).astype(F32), axis=1, keepdims=True)
        live = jnp.zeros((LANES, SLOTS), jnp.int32)
        for j in range(PAIRS):
            live = jnp.where(label == j, len_ref[r, j, 0] + len_ref[r, j, 1], live)
        same = ids == label
        ok = same & (place.astype(F32) - start < live.astype(F32))
        rs = pl.ds(r * SLOTS, SLOTS)
        key_add[rs, :] = jnp.where(ok | (label >= PAIRS), 0.0, -1e30).T.astype(BF16)
        query_one[rs, :] = same.astype(F32).T.astype(BF16)


def split_heads(v):
    lane = lax.broadcasted_iota(jnp.int32, v.shape, 1)
    zero = jnp.zeros_like(v)
    return jnp.concatenate(
        [jnp.where(lane < HEAD_DIM, v, zero), jnp.where(lane < HEAD_DIM, zero, v)], axis=0
    )


def join_heads(v):
    lane = lax.broadcasted_iota(jnp.int32, (SLOTS, LANES), 1)
    return jnp.where(lane < HEAD_DIM, v[:SLOTS], v[SLOTS:])


def head_pair(i):
    pairs = HEADS // 2
    r, p = i // pairs, lax.rem(i, pairs)
    return (
        pl.ds(pl.multiple_of(r * SLOTS, 16), SLOTS),
        pl.ds(pl.multiple_of(p * LANES, LANES), LANES),
    )


def scores_of(rs, cs, qkv, key_add, query_one):
    q, k, one = qkv[0, rs, cs], qkv[1, rs, cs], query_one[rs, :]
    q_side = jnp.concatenate([split_heads(q), jnp.concatenate([one, one], axis=0)], axis=1)
    k_side = jnp.concatenate([k, key_add[rs, :]], axis=1)
    return dot_nt(k_side, q_side), q, k


def attend(i, qkv, key_add, query_one, context, log_totals):
    rs, cs = head_pair(i)
    scores, _, _ = scores_of(rs, cs, qkv, key_add, query_one)
    top = jnp.max(scores, axis=0, keepdims=True)
    raised = jnp.exp(scores - top)
    total = jnp.sum(raised, axis=0, keepdims=True)
    shares = (raised * (1.0 / total)).astype(BF16)
    log_totals[i] = top + jnp.log(total)
    context[rs, cs] = join_heads(dot_tn(shares, qkv[2, rs, cs])).astype(BF16)


def attend_back(i, qkv, key_add, query_one, log_totals, grad_context, grad_qkv):
    rs, cs = head_pair(i)
    scores, q, k = scores_of(rs, cs, qkv, key_add, query_one)
    shares = jnp.exp(scores - log_totals[i])
    grad = split_heads(grad_context[rs, cs])
    grad_shares = dot_nt(qkv[2, rs, cs], grad)
    inner = jnp.sum(shares * grad_shares, axis=0, keepdims=True)
    grad_scores = (shares * (grad_shares - inner)).astype(BF16)
    grad_qkv[2, rs, cs] = dot_nn(shares.astype(BF16), grad).astype(BF16)
    grad_qkv[1, rs, cs] = dot_nn(grad_scores, split_heads(q)).astype(BF16)
    grad_qkv[0, rs, cs] = (join_heads(dot_tn(grad_scores, k)) * 0.125).astype(BF16)


def run_beside(count, body, steps):
    def turn(i, carry):
        body(i)
        for j, some in enumerate(steps):
            if some:

                @pl.when(i == j)
                def _(some=some):
                    for step in some:
                        step()

        return carry

    lax.fori_loop(0, count, turn, 0)


def deal(steps, count):
    out = [[] for _ in range(count)]
    for j, step in enumerate(steps):
        out[j * count // len(steps)].append(step)
    return out


def joint_weight(plan, ref, b):
    jr = plan.joint_rows
    return ref[0 : plan.joint_src, b * jr : (b + 1) * jr, :].reshape(D, D)


def out_weight(plan, ref):
    return ref[plan.joint_src : plan.n].reshape(D, D)


def in_weight(plan, ref, c):
    ir = plan.in_rows
    return ref[0 : plan.in_src, c * ir : (c + 1) * ir, :].reshape(D, D)


def back_weight(plan, ref, c):
    return ref[back_blocks(plan, c)].reshape(D, D)


def back_blocks(plan, c):
    per = (plan.n - plan.in_src) // 4
    return pl.ds(plan.in_src + c * per, per)


def token_tiles(plan, size, fn):
    def one(t, carry):
        fn(pl.ds(pl.multiple_of(t * size, 16), size))
        return carry

    lax.fori_loop(0, plan.tokens // size, one, 0)


def first_kernel(plan, *refs):
    (x, ids, lens, shard_a, shard_f) = refs[:5]
    (all_a, all_f, qkv_out, context_out, log_totals, xhat_out, rstd_out, vec) = refs[5:13]
    (params, qkv, context, xhat, joined_a, joined_f, halo_a, halo_f, end_a, end_f, block_f, vec_own, vec_held,
     key_add, query_one, send, recv, local) = refs[13:]
    n, nz = plan.n, plan.nz
    place = Place(plan)
    me = place.me
    wire = Wire(send, recv)
    tail_a, tail_f = plan.tail_a, plan.tail_f
    halo_number = 0
    vec_base = 2
    bits = n.bit_length() - 1
    a_base = vec_base + bits
    f_base = a_base + gather_count(nz)

    end_a[...] = shard_a[plan.unit_a - tail_a : plan.unit_a, :]
    end_f[...] = shard_f[plan.unit_f - tail_f : plan.unit_f, :]
    joined_a[tail_a : tail_a + plan.unit_a, :] = shard_a[...]
    joined_f[tail_f : tail_f + plan.unit_f, :] = shard_f[...]
    vec_own[0] = jnp.zeros(vec_own.shape[1:], F32)
    va, vf = 5 * D // LANES, 3 * D // LANES

    @pl.when(me == plan.at_attn_vec[0])
    def _():
        vec_own[0, 0:va, :] = shard_a[plan.at_attn_vec[1] : plan.at_attn_vec[1] + va, :]
        vec_own[0, va + plan.gap : va + plan.gap + vf, :] = shard_f[
            plan.at_ffn_vec[1] : plan.at_ffn_vec[1] + vf, :
        ]

    @pl.when(me == plan.at_bias_in[0])
    def _():
        vec_own[0, va : va + plan.gap, :] = shard_f[
            plan.at_bias_in[1] : plan.at_bias_in[1] + plan.gap, :
        ]

    place.barrier()

    @pl.when(me < n - 1)
    def _():
        wire.copy(end_a, halo_a, halo_number, me + 1).start()
        wire.copy(end_f, halo_f, halo_number + 1, me + 1).start()

    vec_steps = add_over_all(place, wire, vec_base, vec_own, vec_held)
    vec_steps[0]()

    @pl.when(me > 0)
    def _():
        wire.copy(end_a, halo_a, halo_number, me - 1).wait_recv()
        joined_a[0:tail_a, :] = halo_a[...]

    start = tail_a - plan.shift_a(me)
    jr = plan.joint_rows
    mine = params.at[me]
    cols = [pl.ds(u * LANES, LANES) for u in range(6)]

    @pl.when(me < plan.joint_src)
    def _():
        for b in range(3):
            for u in range(6):
                mine[b * jr : (b + 1) * jr, cols[u]] = joined_a[
                    pl.ds(start + 6 * b + u, jr, stride=18), :
                ].astype(BF16)

    @pl.when(me >= plan.joint_src)
    def _():
        for u in range(6):
            mine[:, cols[u]] = joined_a[pl.ds(start + u, plan.rows_a, stride=6), :].astype(BF16)

    gather_a = Gather(place, wire, a_base, params, plan.rows_a, plan.late_a, plan.half_a)
    gather_f = Gather(place, wire, f_base, all_f, plan.rows_f, plan.late_f, plan.half_f)
    steps_a = gather_a.steps()
    steps_f = gather_f.steps()
    steps_a[0]()

    @pl.when(me > 0)
    def _():
        wire.copy(end_f, halo_f, halo_number + 1, me - 1).wait_recv()
        joined_f[0:tail_f, :] = halo_f[...]

    start_f = tail_f - plan.shift_f(me)
    ir = plan.in_rows

    @pl.when(me < plan.in_src)
    def _():
        for c in range(4):
            for u in range(6):
                block_f[c * ir : (c + 1) * ir, cols[u]] = joined_f[
                    pl.ds(start_f + 6 * c + u, ir, stride=24), :
                ].astype(BF16)

    @pl.when(me >= plan.in_src)
    def _():
        for u in range(6):
            block_f[:, cols[u]] = joined_f[pl.ds(start_f + u, plan.rows_f, stride=6), :].astype(BF16)

    own_f = pltpu.make_async_copy(block_f, all_f.at[me], local.at[0])
    own_f.start()

    def begin_f():
        own_f.wait()
        steps_f[0]()

    build_masks(plan, ids, lens, key_add, query_one)

    def finish_vec():
        whole = vec_own.at[bits]
        vec[...] = jnp.zeros_like(vec)
        count = (va + plan.gap + vf) // 6
        for u in range(6):
            vec[0:count, cols[u]] = whole[pl.ds(u, count, stride=6), :]

    order = steps_a[1:]
    at = len(order) - 4
    order.insert(at, begin_f)
    for j, step in enumerate(vec_steps[1:] + [finish_vec]):
        order.insert(2 * j + 1, step)
    for step in order:
        step()

    keep_a = pltpu.make_async_copy(params, all_a, local.at[1])
    keep_a.start()
    deals = deal(steps_f[1:-1], 3 + HEADS // 2 * plan.rows + 1)
    for b in range(3):
        bias = vec[0:1, :] if b == 0 else vec[1:2, :] if b == 2 else None
        got = dot_nn(x[...], joint_weight(plan, params, b))
        if bias is not None:
            got = got + bias
        got = got.astype(BF16)
        if b == 0:
            got = got * jnp.asarray(HEAD_DIM ** (-0.5), BF16)
        qkv[b] = got
        for step in deals[b]:
            step()
    keep_qkv = pltpu.make_async_copy(qkv, qkv_out, local.at[2])
    keep_qkv.start()
    count = HEADS // 2 * plan.rows
    run_beside(
        count, lambda i: attend(i, qkv, key_add, query_one, context, log_totals), deals[3 : 3 + count]
    )
    keep_context = pltpu.make_async_copy(context, context_out, local.at[3])
    keep_context.start()

    def norm(rs):
        v = x[rs, :].astype(F32) + (dot_nn(context[rs, :], out_weight(plan, params)) + vec[2:3, :])
        centred = v - row_mean(v)
        rstd = lax.rsqrt(row_mean(centred * centred) + NORM_EPS)
        xhat[rs, :] = centred * rstd
        rstd_out[rs, :] = jnp.broadcast_to(rstd, (rstd.shape[0], LANES))

    token_tiles(plan, SLOTS, norm)
    keep_xhat = pltpu.make_async_copy(xhat, xhat_out, local.at[4])
    keep_xhat.start()
    for step in deals[-1] + steps_f[-1:]:
        step()
    for copy in (keep_a, keep_qkv, keep_context, keep_xhat):
        copy.wait()
    gather_a.drain()
    gather_f.drain()

    @pl.when(me < n - 1)
    def _():
        wire.copy(end_a, halo_a, halo_number, me + 1).wait_send()
        wire.copy(end_f, halo_f, halo_number + 1, me + 1).wait_send()


def vmem_spec():
    return pl.BlockSpec(memory_space=pltpu.VMEM)


def any_spec():
    return pl.BlockSpec(memory_space=pl.ANY)


def first_call(plan, x, ids, lens, shard_a, shard_f):
    n, t = plan.n, plan.tokens
    shape = jax.ShapeDtypeStruct
    turns = HEADS // 2 * plan.rows
    bits = n.bit_length() - 1
    units = 80
    sems = 2 + bits + 2 * gather_count(plan.nz)
    return pl.pallas_call(
        functools.partial(first_kernel, plan),
        name="gather_attend",
        out_shape=[
            shape((n, plan.rows_a, D), BF16),
            shape((n, plan.rows_f, D), BF16),
            shape((3, t, D), BF16),
            shape((t, D), BF16),
            shape((turns, 1, 2 * SLOTS), F32),
            shape((t, D), F32),
            shape((t, LANES), F32),
            shape((16, D), F32),
        ],
        in_specs=[vmem_spec(), vmem_spec(), pl.BlockSpec(memory_space=pltpu.SMEM), vmem_spec(), vmem_spec()],
        out_specs=[
            any_spec(), any_spec(), any_spec(), any_spec(), vmem_spec(), any_spec(), vmem_spec(), vmem_spec(),
        ],
        scratch_shapes=[
            pltpu.VMEM((n, plan.rows_a, D), BF16),
            pltpu.VMEM((3, t, D), BF16),
            pltpu.VMEM((t, D), BF16),
            pltpu.VMEM((t, D), F32),
            pltpu.VMEM((plan.tail_a + -(-plan.unit_a // 8) * 8 + 8, LANES), F32),
            pltpu.VMEM((plan.tail_f + -(-plan.unit_f // 8) * 8 + 8, LANES), F32),
            pltpu.VMEM((plan.tail_a, LANES), F32),
            pltpu.VMEM((plan.tail_f, LANES), F32),
            pltpu.VMEM((plan.tail_a, LANES), F32),
            pltpu.VMEM((plan.tail_f, LANES), F32),
            pltpu.VMEM((plan.rows_f, D), BF16),
            pltpu.VMEM((bits + 1, units, LANES), F32),
            pltpu.VMEM((bits, units, LANES), F32),
            pltpu.VMEM((t, LANES), BF16),
            pltpu.VMEM((t, LANES), BF16),
            pltpu.SemaphoreType.DMA((sems,)),
            pltpu.SemaphoreType.DMA((sems,)),
            pltpu.SemaphoreType.DMA((5,)),
        ],
        compiler_params=pltpu.CompilerParams(
            collective_id=0, has_side_effects=True, vmem_limit_bytes=VMEM_LIMIT
        ),
    )(x, ids, lens, shard_a, shard_f)


def gelu_with_slope(h):
    cdf = 0.5 * (1.0 + lax.erf(h * 0.7071067811865476))
    return h * cdf, cdf + h * jnp.exp(-0.5 * h * h) * 0.3989422804014327


def norm_back(grad, xhat, rstd):
    return rstd * (grad - row_mean(grad) - xhat * row_mean(grad * xhat))


def middle_kernel(plan, *refs):
    (xhat1, rstd1, vec, out_grad, all_f) = refs[:5]
    (layer_out, grad_first, terms_f, vec_grad) = refs[5:9]
    (weights, norm_b, active, slope, grad_hidden, acc, grad_ffn, terms, loaded, stored) = refs[9:]
    per = (plan.n - plan.in_src) // 4
    ir = plan.in_rows

    def in_part(ref, c):
        return ref.at[0 : plan.in_src, pl.ds(pl.multiple_of(c * ir, 16), ir), :]

    def back_part(ref, c):
        return ref.at[pl.ds(plan.in_src + c * per, per)]

    loads = []
    for c in range(4):
        loads.append(pltpu.make_async_copy(in_part(all_f, c), in_part(weights, c), loaded.at[2 * c]))
        loads.append(pltpu.make_async_copy(back_part(all_f, c), back_part(weights, c), loaded.at[2 * c + 1]))
    for load in loads:
        load.start()
    gain_first, shift_first = vec[3:4, :], vec[4:5, :]
    bias_back, gain_second, shift_second = vec[9:10, :], vec[10:11, :], vec[11:12, :]
    vec_grad[...] = jnp.zeros_like(vec_grad)

    def enter(rs):
        v = xhat1[rs, :] * gain_first + shift_first
        norm_b[rs, :] = v.astype(BF16)
        acc[rs, :] = v + bias_back

    token_tiles(plan, SLOTS, enter)

    def up(c, carry):
        pltpu.make_async_copy(in_part(all_f, c), in_part(weights, c), loaded.at[2 * c]).wait()
        pltpu.make_async_copy(back_part(all_f, c), back_part(weights, c), loaded.at[2 * c + 1]).wait()
        w_in = in_part(weights, c)[...].reshape(D, D)
        w_back = back_part(weights, c)[...].reshape(D, D)

        def tile(rs):
            hidden = dot_nn(norm_b[rs, :], w_in) + vec[pl.ds(5 + c, 1), :]
            value, incline = gelu_with_slope(hidden)
            value = value.astype(BF16)
            active[c, rs, :] = value
            slope[c, rs, :] = incline.astype(BF16)
            acc[rs, :] += dot_nn(value, w_back)

        token_tiles(plan, SLOTS, tile)
        return carry

    lax.fori_loop(0, 4, up, 0)

    def turn(rs):
        v = acc[rs, :]
        centred = v - row_mean(v)
        rstd = lax.rsqrt(row_mean(centred * centred) + NORM_EPS)
        xhat = centred * rstd
        layer_out[rs, :] = (xhat * gain_second + shift_second).astype(BF16)
        cot = out_grad[rs, :].astype(F32)
        vec_grad[10:11, :] += col_sum(cot * xhat)
        vec_grad[11:12, :] += col_sum(cot)
        grad = norm_back(cot * gain_second, xhat, rstd)
        acc[rs, :] = grad
        low = grad.astype(BF16)
        grad_ffn[rs, :] = low
        vec_grad[9:10, :] += col_sum(low.astype(F32))

    token_tiles(plan, SLOTS, turn)

    def store(part, c, k):
        return pltpu.make_async_copy(part(terms, c), part(terms_f, c), stored.at[2 * c + k])

    def down(c, carry):
        back_part(terms, c)[...] = dot_tn(active[c], grad_ffn[...]).astype(BF16).reshape(per, plan.rows_f, D)
        store(back_part, c, 0).start()
        w_in = in_part(weights, c)[...].reshape(D, D)
        w_back = back_part(weights, c)[...].reshape(D, D)

        def tile(rs):
            grad = (slope[c, rs, :].astype(F32) * dot_nt(grad_ffn[rs, :], w_back)).astype(BF16)
            grad_hidden[rs, :] = grad
            vec_grad[pl.ds(5 + c, 1), :] += col_sum(grad.astype(F32))
            acc[rs, :] += dot_nt(grad, w_in)

        token_tiles(plan, SLOTS, tile)
        in_part(terms, c)[...] = dot_tn(norm_b[...], grad_hidden[...]).astype(BF16).reshape(plan.in_src, ir, D)
        store(in_part, c, 1).start()
        return carry

    lax.fori_loop(0, 4, down, 0)

    def leave(rs):
        grad, xhat = acc[rs, :], xhat1[rs, :]
        vec_grad[3:4, :] += col_sum(grad * xhat)
        vec_grad[4:5, :] += col_sum(grad)
        grad = norm_back(grad * gain_first, xhat, rstd1[rs, 0:1])
        grad_first[rs, :] = grad
        vec_grad[2:3, :] += col_sum(grad.astype(BF16).astype(F32))

    token_tiles(plan, SLOTS, leave)
    for c in range(4):
        store(back_part, c, 0).wait()
        store(in_part, c, 1).wait()


def middle_call(plan, xhat, rstd, vec, out_grad, all_f):
    n, t = plan.n, plan.tokens
    shape = jax.ShapeDtypeStruct
    return pl.pallas_call(
        functools.partial(middle_kernel, plan),
        name="feed_forward",
        out_shape=[
            shape((t, D), BF16), shape((t, D), F32), shape((n, plan.rows_f, D), BF16), shape((16, D), F32),
        ],
        in_specs=[vmem_spec(), vmem_spec(), vmem_spec(), vmem_spec(), any_spec()],
        out_specs=[vmem_spec(), vmem_spec(), any_spec(), vmem_spec()],
        scratch_shapes=[
            pltpu.VMEM((n, plan.rows_f, D), BF16),
            pltpu.VMEM((t, D), BF16),
            pltpu.VMEM((4, t, D), BF16),
            pltpu.VMEM((4, t, D), BF16),
            pltpu.VMEM((t, D), BF16),
            pltpu.VMEM((t, D), F32),
            pltpu.VMEM((t, D), BF16),
            pltpu.VMEM((n, plan.rows_f, D), BF16),
            pltpu.SemaphoreType.DMA((8,)),
            pltpu.SemaphoreType.DMA((8,)),
        ],
        compiler_params=pltpu.CompilerParams(vmem_limit_bytes=VMEM_LIMIT),
    )(xhat, rstd, vec, out_grad, all_f)


def last_kernel(plan, *refs):
    (terms_f, all_a, qkv_in, context_in, x_in, grad_first_in, log_totals, ids, lens, vec_grad) = refs[:10]
    (in_grad, attn_grad, ffn_grad, bias_grad) = refs[10:14]
    (params, qkv, context, x, grad_first, grad_attn, grad_context, grad_qkv, terms_a, key_add, query_one,
     vec_own, vec_held, joined_a, joined_f, halo_a, halo_f, send, recv, local, local_f) = refs[14:35]
    room_f, room_a = refs[35:44], refs[44:53]
    n, nz = plan.n, plan.nz
    place = Place(plan)
    me = place.me
    wire = Wire(send, recv)
    bits = n.bit_length() - 1
    vec_base = 2
    f_base = vec_base + bits
    a_base = f_base + scatter_count(nz)
    total_f, total_a = room_f[0], room_a[0]
    scatter_f = Scatter(place, wire, f_base, terms_f, plan.rows_f, plan.late_f, plan.half_f, total_f,
                        room_f[1:], True)
    scatter_a = Scatter(place, wire, a_base, terms_a, plan.rows_a, plan.late_a, plan.half_a, total_a,
                        room_a[1:], False)

    pairs = ((all_a, params), (grad_first_in, grad_first), (context_in, context), (qkv_in, qkv), (x_in, x))
    loads = [pltpu.make_async_copy(a, b, local.at[j]) for j, (a, b) in enumerate(pairs)]
    own_loads = []
    for z in range(nz):
        for column in range(4):
            k = column * nz + z
            own_loads.append(
                pltpu.make_async_copy(terms_f.at[place.block(column, z)], total_f.at[k], local_f.at[k])
            )
    for load in loads[:2] + own_loads + loads[2:]:
        load.start()
    place.barrier()
    steps_f = scatter_f.steps()
    steps_a = scatter_a.steps()
    steps_f[0]()
    loads[0].wait()
    loads[1].wait()

    def low(rs):
        grad_attn[rs, :] = grad_first[rs, :].astype(BF16)
        grad_context[rs, :] = dot_nt(grad_attn[rs, :], out_weight(plan, params)).astype(BF16)

    token_tiles(plan, SLOTS, low)
    loads[2].wait()
    terms_a[plan.joint_src : n] = (
        dot_tn(context[...], grad_attn[...]).astype(BF16).reshape(n - plan.joint_src, plan.rows_a, D)
    )
    build_masks(plan, ids, lens, key_add, query_one)
    loads[3].wait()
    for load in own_loads:
        load.wait()
    count = HEADS // 2 * plan.rows
    run_beside(
        count,
        lambda i: attend_back(i, qkv, key_add, query_one, log_totals, grad_context, grad_qkv),
        deal(steps_f[1:], count),
    )
    vec_own[0] = vec_grad[...]
    vec_own[0, 0:1, :] = col_sum(grad_qkv[0].astype(F32))
    vec_own[0, 1:2, :] = col_sum(grad_qkv[2].astype(F32))
    vec_steps = add_over_all(place, wire, vec_base, vec_own, vec_held)
    vec_steps[0]()
    loads[4].wait()
    jr = plan.joint_rows
    for b in range(3):
        terms_a[0 : plan.joint_src, b * jr : (b + 1) * jr, :] = (
            dot_tn(x[...], grad_qkv[b]).astype(BF16).reshape(plan.joint_src, jr, D)
        )
    cols = [pl.ds(u * LANES, LANES) for u in range(6)]
    whole = vec_own.at[bits]

    def lay_f():
        total = total_f.at[place.z]
        ir = plan.in_rows

        @pl.when(me < plan.in_src)
        def _():
            for c in range(4):
                for u in range(6):
                    joined_f[pl.ds(6 * c + u, ir, stride=24), :] = total[
                        c * ir : (c + 1) * ir, cols[u]
                    ].astype(F32)

        @pl.when(me >= plan.in_src)
        def _():
            for u in range(6):
                joined_f[pl.ds(u, plan.rows_f, stride=6), :] = total[:, cols[u]].astype(F32)

        @pl.when(me > 0)
        def _():
            wire.copy(joined_f.at[0 : plan.tail_f], halo_f, 1, me - 1).start()

    def lay_a():
        total = total_a.at[place.z]

        @pl.when(me < plan.joint_src)
        def _():
            for b in range(3):
                for u in range(6):
                    joined_a[pl.ds(6 * b + u, jr, stride=18), :] = total[
                        b * jr : (b + 1) * jr, cols[u]
                    ].astype(F32)

        @pl.when(me >= plan.joint_src)
        def _():
            for u in range(6):
                joined_a[pl.ds(u, plan.rows_a, stride=6), :] = total[:, cols[u]].astype(F32)

        @pl.when(me > 0)
        def _():
            wire.copy(joined_a.at[0 : plan.tail_a], halo_a, 0, me - 1).start()

    def input_grad(rs):
        got = grad_first[rs, :]
        for b in range(3):
            got = got + dot_nt(grad_qkv[b, rs, :], joint_weight(plan, params, b))
        in_grad[rs, :] = got

    def join_f():
        @pl.when(me < n - 1)
        def _():
            wire.copy(halo_f, halo_f, 1, me + 1).wait_recv()
            joined_f[plan.block_f : plan.block_f + plan.tail_f, :] = halo_f[...]

        @pl.when(me == plan.at_bias_in[0])
        def _():
            for u in range(6):
                joined_f[pl.ds(plan.block_f + u, 4, stride=6), :] = whole[5:9, cols[u]]
            rest = plan.tail_f - plan.gap
            joined_f[plan.block_f + plan.gap : plan.block_f + plan.tail_f, :] = halo_f[0:rest, :]

        @pl.when(me == n - 1)
        def _():
            joined_f[plan.block_f : plan.block_f + plan.tail_f, :] = jnp.zeros((plan.tail_f, LANES), F32)
            for u in range(6):
                joined_f[pl.ds(plan.block_f + u, 3, stride=6), :] = whole[9:12, cols[u]]

        ffn_grad[...] = joined_f[pl.ds(plan.shift_f(me), plan.unit_f), :]

    def join_a():
        @pl.when(me < n - 1)
        def _():
            wire.copy(halo_a, halo_a, 0, me + 1).wait_recv()
            joined_a[plan.block_a : plan.block_a + plan.tail_a, :] = halo_a[...]

        @pl.when(me == n - 1)
        def _():
            joined_a[plan.block_a : plan.block_a + plan.tail_a, :] = jnp.zeros((plan.tail_a, LANES), F32)
            for u in range(6):
                joined_a[pl.ds(plan.block_a + u, 5, stride=6), :] = whole[0:5, cols[u]]

        attn_grad[...] = joined_a[pl.ds(plan.shift_a(me), plan.unit_a), :]

    steps_a[0]()
    lay_f()
    order = steps_a[1:]
    for j, step in enumerate(vec_steps[1:]):
        order.insert(2 * j + 1, step)
    quarter = plan.tokens // 4
    for j in range(4):
        order.insert(3 * j + 1, lambda j=j: input_grad(pl.ds(j * quarter, quarter)))
    for step in order:
        step()
    lay_a()
    join_f()
    join_a()
    bias_grad[...] = whole[2:3, :]
    scatter_f.drain()
    scatter_a.drain()

    @pl.when(me > 0)
    def _():
        wire.copy(halo_f, halo_f, 1, me - 1).wait_send()
        wire.copy(halo_a, halo_a, 0, me - 1).wait_send()


def last_call(plan, terms_f, all_a, qkv, context, x, grad_first, log_totals, ids, lens, vec_grad):
    n, t, nz = plan.n, plan.tokens, plan.nz
    shape = jax.ShapeDtypeStruct
    bits = n.bit_length() - 1
    sems = 2 + bits + 2 * scatter_count(nz)
    smem = pl.BlockSpec(memory_space=pltpu.SMEM)
    return pl.pallas_call(
        functools.partial(last_kernel, plan),
        name="attend_back_reduce",
        out_shape=[
            shape((t, D), F32), shape((plan.unit_a, LANES), F32), shape((plan.unit_f, LANES), F32),
            shape((1, D), F32),
        ],
        in_specs=[any_spec()] * 6 + [vmem_spec(), vmem_spec(), smem, vmem_spec()],
        out_specs=[vmem_spec()] * 4,
        scratch_shapes=[
            pltpu.VMEM((n, plan.rows_a, D), BF16),
            pltpu.VMEM((3, t, D), BF16),
            pltpu.VMEM((t, D), BF16),
            pltpu.VMEM((t, D), BF16),
            pltpu.VMEM((t, D), F32),
            pltpu.VMEM((t, D), BF16),
            pltpu.VMEM((t, D), BF16),
            pltpu.VMEM((3, t, D), BF16),
            pltpu.VMEM((n, plan.rows_a, D), BF16),
            pltpu.VMEM((t, LANES), BF16),
            pltpu.VMEM((t, LANES), BF16),
            pltpu.VMEM((bits + 1, 16, D), F32),
            pltpu.VMEM((bits, 16, D), F32),
            pltpu.VMEM((plan.block_a + plan.tail_a + 8, LANES), F32),
            pltpu.VMEM((plan.block_f + plan.tail_f + 8, LANES), F32),
            pltpu.VMEM((plan.tail_a, LANES), F32),
            pltpu.VMEM((plan.tail_f, LANES), F32),
            pltpu.SemaphoreType.DMA((sems,)),
            pltpu.SemaphoreType.DMA((sems,)),
            pltpu.SemaphoreType.DMA((5,)),
            pltpu.SemaphoreType.DMA((4 * nz,)),
        ]
        + Scatter.rooms(nz, plan.rows_f, plan.late_f, plan.half_f)
        + Scatter.rooms(nz, plan.rows_a, plan.late_a, plan.half_a),
        compiler_params=pltpu.CompilerParams(
            collective_id=1, has_side_effects=True, vmem_limit_bytes=VMEM_LIMIT
        ),
    )(terms_f, all_a, qkv, context, x, grad_first, log_totals, ids, lens, vec_grad)


def fused_body(plan, layer_in, pair_ids, pair_lengths, attn_shard, ffn_shard, out_grad):
    t = plan.tokens
    x = layer_in.reshape(t, D)
    shard_a = attn_shard.astype(F32).reshape(plan.unit_a, LANES)
    shard_f = ffn_shard.astype(F32).reshape(plan.unit_f, LANES)
    all_a, all_f, qkv, context, log_totals, xhat, rstd, vec = first_call(
        plan, x, pair_ids, pair_lengths, shard_a, shard_f
    )
    layer_out, grad_first, terms_f, vec_grad = middle_call(
        plan, xhat, rstd, vec, out_grad.reshape(t, D), all_f
    )
    in_grad, attn_grad, ffn_grad, bias_grad = last_call(
        plan, terms_f, all_a, qkv, context, x, grad_first, log_totals, pair_ids, pair_lengths, vec_grad
    )
    return (
        layer_out.reshape(layer_in.shape),
        in_grad.reshape(layer_in.shape),
        attn_grad.reshape(-1),
        ffn_grad.reshape(-1),
        bias_grad.reshape(-1),
    )


def unpack_attention(flattened):
    offset = 3 * D * D
    weight_joint = flattened[:offset].reshape(D, 3 * D)
    weight_out = flattened[offset : offset + D * D].reshape(D, D)
    offset = offset + D * D
    vectors = flattened[offset : offset + 5 * D].reshape(5, D)
    return (weight_joint, weight_out, vectors[0], vectors[1], vectors[2], vectors[3], vectors[4])


def unpack_feedforward(flattened):
    offset = D * FF
    weight_in = flattened[:offset].reshape(D, FF)
    bias_in = flattened[offset : offset + FF]
    offset = offset + FF
    weight_back = flattened[offset : offset + FF * D].reshape(FF, D)
    offset = offset + FF * D
    vectors = flattened[offset : offset + 3 * D].reshape(3, D)
    return (weight_in, bias_in, weight_back, vectors[0], vectors[1], vectors[2])


def layer_norm(values, gain_vec, shift_vec):
    row_mean = jnp.mean(values, axis=-1, keepdims=True)
    centred = values - row_mean
    row_var = jnp.mean(centred * centred, axis=-1, keepdims=True)
    return centred * lax.rsqrt(row_var + NORM_EPS) * gain_vec + shift_vec


def exact_gelu(values):
    return jax.nn.gelu(values, approximate=False)


def key_mask(pair_ids, pair_lengths):
    labels = jnp.arange(PAIRS, dtype=jnp.int32)
    member = pair_ids[:, :, None] == labels[None, None, :]
    starts = jnp.sum((pair_ids[:, :, None] < labels[None, None, :]).astype(jnp.int32), axis=1)
    live_len = pair_lengths[:, :, 0] + pair_lengths[:, :, 1]
    slot_start = jnp.sum(jnp.where(member, starts[:, None, :], 0), axis=-1)
    slot_len = jnp.sum(jnp.where(member, live_len[:, None, :], 0), axis=-1)
    places = jnp.arange(pair_ids.shape[1], dtype=jnp.int32)[None, :]
    is_live = places - slot_start < slot_len
    return (pair_ids[:, :, None] == pair_ids[:, None, :]) & is_live[:, None, :]


def contract_rows(one_side, other_side):
    return lax.dot_general(
        one_side, other_side, (((0,), (0,)), ((), ())), preferred_element_type=jnp.float32
    )


def contract_cols(one_side, other_side):
    return lax.dot_general(
        one_side, other_side, (((1,), (1,)), ((), ())), preferred_element_type=jnp.float32
    )


def attend_forward(queries, key_rows, value_rows, key_ok, score_scale):

    def head_block(block_index):
        head_start = block_index * 4
        query_b = lax.dynamic_slice_in_dim(queries, head_start, 4, 2)
        key_b = lax.dynamic_slice_in_dim(key_rows, head_start, 4, 2)
        value_b = lax.dynamic_slice_in_dim(value_rows, head_start, 4, 2)
        scores = (
            jnp.einsum("rqhd,rkhd->rhqk", query_b, key_b, preferred_element_type=jnp.float32)
            * score_scale
        )
        scores = jnp.where(key_ok[:, None], scores, -1e30)
        row_max = jnp.max(scores, axis=-1, keepdims=True)
        raised = jnp.exp(scores - row_max)
        totals = jnp.sum(raised, axis=-1, keepdims=True)
        shares = (raised / totals).astype(jnp.bfloat16)
        context = jnp.einsum("rhqk,rkhd->rqhd", shares, value_b, preferred_element_type=jnp.float32)
        return (context, row_max + jnp.log(totals))

    return lax.map(head_block, jnp.arange(HEADS // 4))


def attend_backward(queries, key_rows, value_rows, grad_context, log_totals, key_ok, score_scale):

    def head_block(operands):
        block_index, log_total = operands
        head_start = block_index * 4
        query_b = lax.dynamic_slice_in_dim(queries, head_start, 4, 2)
        key_b = lax.dynamic_slice_in_dim(key_rows, head_start, 4, 2)
        value_b = lax.dynamic_slice_in_dim(value_rows, head_start, 4, 2)
        grad_block = lax.dynamic_slice_in_dim(grad_context, head_start, 4, 2)
        scores = (
            jnp.einsum("rqhd,rkhd->rhqk", query_b, key_b, preferred_element_type=jnp.float32)
            * score_scale
        )
        shares = jnp.where(key_ok[:, None], jnp.exp(scores - log_total), 0.0)
        grad_shares = jnp.einsum(
            "rqhd,rkhd->rhqk", grad_block, value_b, preferred_element_type=jnp.float32
        )
        inner_sum = jnp.sum(shares * grad_shares, axis=-1, keepdims=True)
        grad_scores = (shares * (grad_shares - inner_sum)).astype(jnp.bfloat16)
        grad_query = (
            jnp.einsum("rhqk,rkhd->rqhd", grad_scores, key_b, preferred_element_type=jnp.float32)
            * score_scale
        )
        grad_key = (
            jnp.einsum("rhqk,rqhd->rkhd", grad_scores, query_b, preferred_element_type=jnp.float32)
            * score_scale
        )
        grad_value = jnp.einsum(
            "rhqk,rqhd->rkhd",
            shares.astype(jnp.bfloat16),
            grad_block,
            preferred_element_type=jnp.float32,
        )
        return (grad_query, grad_key, grad_value)

    gradients = lax.map(head_block, (jnp.arange(HEADS // 4), log_totals))
    return [jnp.moveaxis(piece, 0, 2).reshape(-1, D) for piece in gradients]


def plain_body(layer_in, pair_ids, pair_lengths, attn_shard, ffn_shard, out_grad):
    row_count = layer_in.shape[0]
    tokens = row_count * SLOTS
    score_scale = HEAD_DIM ** (-0.5)
    key_ok = key_mask(pair_ids, pair_lengths)
    att_whole = lax.all_gather(attn_shard, "fsdp", axis=0, tiled=True)
    weight_joint, weight_out, bias_query, bias_value, bias_out, gain_first, shift_first = (
        unpack_attention(att_whole)
    )
    inputs = layer_in.reshape(tokens, D)
    bias_joint = jnp.concatenate([bias_query, jnp.zeros_like(bias_query), bias_value]).astype(
        jnp.float32
    )
    projected = (
        jnp.dot(inputs, weight_joint, preferred_element_type=jnp.float32) + bias_joint
    ).astype(jnp.bfloat16)
    projected = projected.reshape(row_count, SLOTS, 3, HEADS, HEAD_DIM)
    queries = projected[:, :, 0]
    key_rows = projected[:, :, 1]
    value_rows = projected[:, :, 2]
    contexts, log_totals = attend_forward(queries, key_rows, value_rows, key_ok, score_scale)
    context = jnp.moveaxis(contexts, 0, 2).reshape(tokens, D).astype(jnp.bfloat16)
    attn_out = jnp.dot(context, weight_out, preferred_element_type=jnp.float32) + bias_out.astype(
        jnp.float32
    )
    norm_first, first_pull = jax.vjp(
        layer_norm,
        inputs.astype(jnp.float32) + attn_out,
        gain_first.astype(jnp.float32),
        shift_first.astype(jnp.float32),
    )
    norm_first_b = norm_first.astype(jnp.bfloat16)
    feed_whole = lax.all_gather(ffn_shard, "fsdp", axis=0, tiled=True)
    weight_in, bias_in, weight_back, bias_back, gain_second, shift_second = unpack_feedforward(
        feed_whole
    )
    hidden = jnp.dot(norm_first_b, weight_in, preferred_element_type=jnp.float32) + bias_in.astype(
        jnp.float32
    )
    active, gelu_pull = jax.vjp(exact_gelu, hidden)
    active_b = active.astype(jnp.bfloat16)
    ffn_out = jnp.dot(active_b, weight_back, preferred_element_type=jnp.float32) + bias_back.astype(
        jnp.float32
    )
    result, second_pull = jax.vjp(
        layer_norm,
        norm_first + ffn_out,
        gain_second.astype(jnp.float32),
        shift_second.astype(jnp.float32),
    )
    layer_out = result.astype(jnp.bfloat16).reshape(row_count, SLOTS, D)
    feed_back = lax.all_gather(ffn_shard, "fsdp", axis=0, tiled=True)
    weight_in, bias_in, weight_back, bias_back, gain_second, shift_second = unpack_feedforward(
        feed_back
    )
    cotangent = out_grad.reshape(tokens, D).astype(jnp.float32)
    grad_sum_second, grad_gain_second, grad_shift_second = second_pull(cotangent)
    grad_ffn = grad_sum_second.astype(jnp.bfloat16)
    grad_bias_back = jnp.sum(grad_ffn.astype(jnp.float32), axis=0)
    grad_weight_back = contract_rows(active_b, grad_ffn)
    (grad_hidden,) = gelu_pull(contract_cols(grad_ffn, weight_back))
    grad_hidden = grad_hidden.astype(jnp.bfloat16)
    grad_bias_in = jnp.sum(grad_hidden.astype(jnp.float32), axis=0)
    grad_weight_in = contract_rows(norm_first_b, grad_hidden)
    grad_norm_first = grad_sum_second + contract_cols(grad_hidden, weight_in)
    grad_sum_first, grad_gain_first, grad_shift_first = first_pull(grad_norm_first)
    feed_pad = feed_back.shape[0] - (2 * D * FF + FF + 3 * D)
    feed_full = jnp.concatenate(
        [
            grad_weight_in.reshape(-1),
            grad_bias_in,
            grad_weight_back.reshape(-1),
            grad_bias_back,
            grad_gain_second,
            grad_shift_second,
            jnp.zeros((feed_pad,), jnp.float32),
        ]
    )
    ffn_grad = lax.psum_scatter(feed_full, "fsdp", scatter_dimension=0, tiled=True)
    att_back = lax.all_gather(attn_shard, "fsdp", axis=0, tiled=True)
    weight_joint, weight_out, bias_query, bias_value, bias_out, gain_first, shift_first = (
        unpack_attention(att_back)
    )
    grad_attn = grad_sum_first.astype(jnp.bfloat16)
    grad_bias_out = jnp.sum(grad_attn.astype(jnp.float32), axis=0)
    out_bias_grad = lax.psum(grad_bias_out, "fsdp")
    grad_weight_out = contract_rows(context, grad_attn)
    grad_context = (
        contract_cols(grad_attn, weight_out)
        .astype(jnp.bfloat16)
        .reshape(row_count, SLOTS, HEADS, HEAD_DIM)
    )
    grad_query, grad_key, grad_value = attend_backward(
        queries, key_rows, value_rows, grad_context, log_totals, key_ok, score_scale
    )
    grad_projected = jnp.concatenate([grad_query, grad_key, grad_value], axis=-1).astype(
        jnp.bfloat16
    )
    column_sums = jnp.sum(grad_projected.astype(jnp.float32), axis=0)
    grad_weight_joint = contract_rows(inputs, grad_projected)
    in_grad = grad_sum_first + contract_cols(grad_projected, weight_joint)
    att_pad = att_back.shape[0] - (4 * D * D + 5 * D)
    attn_full = jnp.concatenate(
        [
            grad_weight_joint.reshape(-1),
            grad_weight_out.reshape(-1),
            column_sums[:D],
            column_sums[2 * D :],
            grad_bias_out,
            grad_gain_first,
            grad_shift_first,
            jnp.zeros((att_pad,), jnp.float32),
        ]
    )
    attn_grad = lax.psum_scatter(attn_full, "fsdp", scatter_dimension=0, tiled=True)
    return (layer_out, in_grad.reshape(row_count, SLOTS, D), attn_grad, ffn_grad, out_bias_grad)


def body(layer_in, pair_ids, pair_lengths, attn_shard, ffn_shard, out_grad, devices):
    plan = Plan(devices, attn_shard.shape[0], ffn_shard.shape[0], layer_in.shape[0])
    run = functools.partial(fused_body, plan) if plan.fits() else plain_body
    return run(layer_in, pair_ids, pair_lengths, attn_shard, ffn_shard, out_grad)


def solution(mesh):
    placed = (
        P("fsdp", None, None),
        P("fsdp", None),
        P("fsdp", None, None),
        P("fsdp"),
        P("fsdp"),
        P("fsdp", None, None),
    )
    return jax.shard_map(
        functools.partial(body, devices=mesh.shape["fsdp"]),
        mesh=mesh,
        in_specs=placed,
        out_specs=(P("fsdp", None, None), P("fsdp", None, None), P("fsdp"), P("fsdp"), P()),
        check_vma=False,
    )
```

```python
import functools

import jax
import jax.numpy as jnp
from jax import lax
from jax.experimental import pallas as pl
from jax.experimental.pallas import tpu as pltpu
from jax.sharding import PartitionSpec as P

D = 768
HEADS = 12
HEAD_DIM = 64
FF = 3072
SLOTS = 416
PAIRS = 3
LANES = 128
NORM_EPS = 1e-12
F32 = jnp.float32
BF16 = jnp.bfloat16
MESH = pl.DeviceIdType.MESH
VMEM_LIMIT = 62 << 20
FINISH = 11
RELAY, PROJECT, ATTEND, NORM, UP, DOWN, TURN, BACK_WEIGHT, HIDDEN, LEAVE, ATTEND_BACK, JOINT, INPUT_GRAD = range(
    0, 1300, 100
)


def dot_nn(a, b):
    return lax.dot_general(a, b, (((1,), (0,)), ((), ())), preferred_element_type=F32)


def dot_nt(a, b):
    return lax.dot_general(a, b, (((1,), (1,)), ((), ())), preferred_element_type=F32)


def dot_tn(a, b):
    return lax.dot_general(a, b, (((0,), (0,)), ((), ())), preferred_element_type=F32)


def row_mean(v):
    return jnp.sum(v, axis=1, keepdims=True) * (1.0 / D)


def col_sum(v):
    return jnp.sum(v, axis=0, keepdims=True)


class Plan:
    def __init__(self, n, attn_shard_len, ffn_shard_len, row_count):
        self.n = n
        self.nz = n // 8
        self.rows = row_count
        self.tokens = row_count * SLOTS
        self.unit_a = attn_shard_len // LANES
        self.unit_f = ffn_shard_len // LANES
        self.block_a = 4 * D * D // LANES // n
        self.block_f = 2 * D * FF // LANES // n
        self.rows_a = 4 * D // n
        self.rows_f = 2 * FF // n
        self.joint_rows = self.rows_a // 3
        self.joint_src = 3 * n // 4
        self.in_rows = self.rows_f // 4
        self.in_src = n // 2
        self.part_a = (0, self.rows_a, 16, 32)
        self.part_f = (0, self.rows_f, 48, 64)
        self.gap = FF // LANES
        self.at_attn_vec = divmod(4 * D * D // LANES, self.unit_a)
        self.at_bias_in = divmod(D * FF // LANES, self.unit_f)
        self.at_ffn_vec = divmod(2 * D * FF // LANES + self.gap, self.unit_f)

    def shift_a(self, me):
        return me * (self.unit_a - self.block_a)

    def shift_f(self, me):
        return me * (self.unit_f - self.block_f) - jnp.where(me >= self.in_src, self.gap, 0)

    def fits(self):
        n = self.n
        if self.nz != 4 or n % 8 or self.rows_a % 48 or self.rows_f % 64:
            return False
        last_a = (n - 1) * (self.unit_a - self.block_a)
        step_f = self.unit_f - self.block_f
        last_f = max((self.in_src - 1) * step_f, (n - 1) * step_f - self.gap)
        first_f = self.in_src * step_f - self.gap
        self.tail_a = -(-(last_a + 1) // 8) * 8
        self.tail_f = -(-(last_f + 2) // 8) * 8
        vec_a, vec_f = 5 * D // LANES, 3 * D // LANES
        return (
            step_f >= 0
            and self.unit_a >= self.block_a
            and first_f >= 0
            and self.tail_a <= self.block_a
            and self.tail_f <= self.block_f
            and self.at_attn_vec[0] == n - 1
            and self.at_ffn_vec[0] == n - 1
            and self.at_bias_in[0] == self.in_src - 1
            and self.unit_a - self.at_attn_vec[1] <= self.tail_a
            and self.unit_f - self.at_ffn_vec[1] <= self.tail_f
            and self.at_attn_vec[1] + vec_a <= self.unit_a
            and self.at_ffn_vec[1] + vec_f <= self.unit_f
            and self.at_bias_in[1] + self.gap <= self.unit_f
            and self.at_bias_in[1] == self.block_f - (self.in_src - 1) * step_f
        )


class Place:
    def __init__(self, plan):
        self.n, self.nz = plan.n, plan.nz
        me = lax.axis_index("fsdp")
        self.me = me
        self.core = lax.rem(me, 2)
        self.x = lax.rem(me // 2, 2)
        self.y = lax.rem(me // 4, 2)
        self.z = me // 8
        self.sib = me + 1 - 2 * self.core
        self.xn = me + 2 - 4 * self.x
        self.yn = me + 4 - 8 * self.y

    def block(self, column, z, other_core=False):
        x = self.x if column in (0, 2) else 1 - self.x
        y = self.y if column in (0, 1) else 1 - self.y
        core = 1 - self.core if other_core else self.core
        return ((z * 2 + y) * 2 + x) * 2 + core

    def level(self, distance, fn):
        if distance == 0:
            fn(self.z)
            return
        pl.when(self.z >= distance)(lambda: fn(self.z - distance))
        pl.when(self.z + distance < self.nz)(lambda: fn(self.z + distance))

    def onward(self, z, fn):
        pl.when((z <= self.z) & (self.z < self.nz - 1))(lambda: fn(self.me + 8))
        pl.when((z >= self.z) & (self.z > 0))(lambda: fn(self.me - 8))

    def bits(self):
        out = []
        bit = 1
        while bit < self.n:
            out.append(self.me + bit - 2 * bit * lax.rem(self.me // bit, 2))
            bit *= 2
        return out

    def barrier(self, halo=1, hubs=()):
        sem = pltpu.get_barrier_semaphore()

        def tell(partner):
            pl.semaphore_signal(sem, inc=1, device_id=(partner,), device_id_type=MESH)

        fixed = self.bits()
        for partner in fixed:
            tell(partner)
        z_odd = lax.rem(self.z, 2)
        far_z = (self.z > 0) & (self.z < self.nz - 1)
        far = (self.me > 0) & (self.me < self.n - 1)
        pl.when(far_z)(lambda: tell(self.me - 8 + 16 * z_odd))
        pl.when(far)(lambda: tell(self.me - 1 + 2 * self.core))
        count = len(fixed) + far_z.astype(jnp.int32) + far.astype(jnp.int32)
        for hub in hubs:
            pl.when(self.me != hub)(lambda: tell(hub))
            count = count + jnp.where(self.me == hub, self.n - 1, 0)
        pl.semaphore_wait(sem, count)


class Wire:
    def __init__(self, send, recv):
        self.send, self.recv = send, recv
        self.sent = []

    def copy(self, src, dst, number, partner):
        return pltpu.make_async_remote_copy(
            src_ref=src,
            dst_ref=dst,
            send_sem=self.send.at[number],
            recv_sem=self.recv.at[number],
            device_id=(partner,),
            device_id_type=MESH,
        )


def add_over_all(place, wire, base, own, held):
    partners = place.bits()

    def send(s):
        wire.copy(own.at[s], held.at[s], base + s, partners[s]).start()

    def take(s):
        wire.copy(own.at[s], held.at[s], base + s, partners[s]).wait()
        own[s + 1] = own[s] + held[s]

    steps = [lambda: send(0)]
    for s in range(len(partners)):

        def step(s=s):
            take(s)
            if s + 1 < len(partners):
                send(s + 1)

        steps.append(step)
    return steps


def gather_count(nz):
    return 17 * nz + 3


class Gather:
    def __init__(self, place, wire, base, ref, top, rows, late, half):
        self.p, self.w, self.ref = place, wire, ref
        nz = place.nz
        self.early = (top, rows - late)
        self.late = (top + rows - late, late)
        self.first = (top, half)
        self.second = (top + half, rows - late - half)
        at = [base]

        def take(count):
            at[0] += count
            return at[0] - count

        self.line, self.xs, self.ys, self.d1, self.d2 = (take(nz) for _ in range(5))
        self.sib, self.late_line, self.late_sib = (take(4 * nz) for _ in range(3))
        self.px, self.py, self.pd = (take(1) for _ in range(3))

    def move(self, column, z, part, number, partner):
        ref = self.ref.at[self.p.block(column, z), pl.ds(*part)]
        return self.w.copy(ref, ref, number, partner)

    def send(self, *args):
        self.move(*args).start()

    def wait(self, column, z, part, number):
        self.move(column, z, part, number, self.p.sib).wait_recv()

    def to_sib(self, column, z):
        self.send(column, z, self.early, self.sib + column * self.p.nz + z, self.p.sib)

    def spread(self, z):
        p = self.p
        p.onward(z, lambda partner: self.send(0, z, self.early, self.line + z, partner))
        self.send(0, z, self.early, self.xs + z, p.xn)
        self.send(0, z, self.early, self.ys + z, p.yn)
        self.to_sib(0, z)

    def spread_late(self, column, z):
        number = column * self.p.nz + z
        self.p.onward(
            z, lambda partner: self.send(column, z, self.late, self.late_line + number, partner)
        )
        self.send(column, z, self.late, self.late_sib + number, self.p.sib)

    def take_line(self, z):
        self.wait(0, z, self.early, self.line + z)
        self.spread(z)

    def take_x(self, z):
        self.wait(1, z, self.early, self.xs + z)
        self.send(1, z, self.first, self.d1 + z, self.p.yn)
        self.to_sib(1, z)

    def take_y(self, z):
        self.wait(2, z, self.early, self.ys + z)
        self.send(2, z, self.second, self.d2 + z, self.p.xn)
        self.to_sib(2, z)

    def take_corner(self, z):
        self.wait(3, z, self.first, self.d1 + z)
        self.wait(3, z, self.second, self.d2 + z)
        self.to_sib(3, z)

    def take_late(self, z):
        for column in range(4):
            self.wait(column, z, self.late, self.late_line + column * self.p.nz + z)
            self.spread_late(column, z)

    def begin(self):
        self.spread(self.p.z)

    def begin_late(self):
        p = self.p
        self.send(0, p.z, self.late, self.px, p.xn)
        self.send(0, p.z, self.late, self.py, p.yn)

    def late_x(self):
        self.wait(1, self.p.z, self.late, self.px)
        self.send(1, self.p.z, self.late, self.pd, self.p.yn)

    def late_y(self):
        self.wait(2, self.p.z, self.late, self.py)

    def late_corner(self):
        self.wait(3, self.p.z, self.late, self.pd)

    def step(self, kind, number, by_plane):
        p, nz = self.p, self.p.nz
        plane, digit = number // 10, number % 10
        starts = (self.begin, self.begin_late, self.late_x, self.late_y, self.late_corner,
                  lambda: self.spread_late(digit, p.z))
        takes = (self.take_line, self.take_x, self.take_y, self.take_corner, self.take_late)
        if kind == FINISH:
            planes = range(nz) if not by_plane else range(digit * nz // 2, (digit + 1) * nz // 2)
            return lambda: self.finish(planes)
        if kind < len(starts):
            return (lambda: pl.when(p.z == plane)(starts[kind])) if by_plane else starts[kind]
        take = takes[kind - len(starts)]
        if not by_plane:
            return lambda: p.level(digit, take)
        if digit:
            return lambda: pl.when((p.z == plane - digit) | (p.z == plane + digit))(lambda: take(plane))
        return lambda: take(plane)

    def finish(self, planes):
        p, nz = self.p, self.p.nz

        def one(j, carry):
            for column in range(4):
                ref = self.ref.at[p.block(column, j, True)]
                for part, base in ((self.early, self.sib), (self.late, self.late_sib)):
                    r = ref.at[pl.ds(*part)]
                    self.w.copy(r, r, base + column * nz + j, p.sib).wait_recv()
            return carry

        lax.fori_loop(planes[0], planes[-1] + 1, one, 0)

    def drain(self):
        p, nz = self.p, self.p.nz

        def sent(column, z, part, number):
            self.move(column, z, part, number, p.sib).wait_send()

        sent(0, p.z, self.late, self.px)
        sent(0, p.z, self.late, self.py)
        sent(1, p.z, self.late, self.pd)

        def one(z, carry):
            p.onward(z, lambda partner: sent(0, z, self.early, self.line + z))
            sent(0, z, self.early, self.xs + z)
            sent(0, z, self.early, self.ys + z)
            sent(1, z, self.first, self.d1 + z)
            sent(2, z, self.second, self.d2 + z)
            for column in range(4):
                number = column * nz + z
                sent(column, z, self.early, self.sib + number)
                sent(column, z, self.late, self.late_sib + number)
                p.onward(z, lambda partner: sent(column, z, self.late, self.late_line + number))
            return carry

        lax.fori_loop(0, nz, one, 0)


def gather_count(nz):
    return 17 * nz + 3


ORDER = (
    10000, 0, 10100, 20030, 20130, 20010, 20020, 20000, 20100, 10200, 10601, 20530, 20200, 10300, 10500,
    10502, 10501, 20330, 10400, 10503, 10602, 20300, 20502, 10800, 20230, 20501, 11001, 20500, 20400, 10801,
    20503, 10603, 20531, 10701, 11002, 10702, 10802, 10700, 20120, 10803, 20430, 20533, 20110, 20601, 10703,
    20631, 20621, 21001, 20611, 10901, 10900, 11003, 10902, 20320, 20522, 20602, 20532, 10903, 20510, 20310,
    20512, 20220, 20612, 20521, 11100, 100, 20210, 20632, 20622, 101, 102, 200, 20511, 21031, 21002, 20603,
    201, 202, 20633, 203, 204, 20410, 20513, 205, 206, 20710, 21011, 20810, 207, 208, 20700, 20800, 20820,
    21032, 209, 20520, 20720, 20420, 210, 20523, 21003, 20910, 211, 300, 21012, 20900, 301, 20730, 21100,
    400, 21033, 21021, 20830, 401, 402, 403, 404, 405, 20920, 21022, 406, 20930, 407, 21101, 500, 501, 502,
    503, 504, 505, 506, 507, 600, 700, 30030, 701, 30020, 30130, 30230, 30633, 800, 30120, 801, 30430,
    30330, 802, 30632, 30220, 30622, 803, 804, 30533, 805, 30621, 30631, 30320, 30420, 806, 807, 30000,
    30532, 900, 30522, 30010, 30100, 30620, 30630, 30730, 30720, 30200, 30603, 901, 902, 30110, 30531,
    30210, 30830, 30820, 30521, 30612, 30300, 1000, 1001, 30602, 30400, 1002, 1003, 30930, 30920, 30530,
    30520, 30410, 1004, 30310, 1005, 30503, 1101, 40003, 30611, 40001, 1006, 30601, 40002, 1007, 40102,
    30512, 40103, 40202, 40201, 30502, 40101, 1008, 1009, 40301, 40203, 40603, 40303, 30610, 40403, 30710,
    40302, 40401, 1010, 40602, 30511, 30600, 30700, 1011, 30810, 30501, 1102, 50003, 30800, 40503, 60000,
    50002, 50103, 40402, 50203, 50603, 40601, 60001, 50001, 50102, 1200, 40000, 30910, 50303, 50403, 50101,
    50202, 50602, 40100, 30900, 30510, 60002, 40502, 30500, 50000, 40200, 50302, 50402, 50503, 50201, 50100,
    50601, 50401, 50301, 60003, 40300, 40600, 50200, 50502, 40501, 40700, 50600, 50700, 40400, 1201, 60004,
    50300, 50400, 50501, 40800, 50800, 1202, 1203, 40500, 40900, 50900, 60005, 50500,
)

class Scatter:
    def __init__(self, place, wire, base, terms, columns, top, rows, late, half, room):
        self.p, self.w, self.terms, self.columns = place, wire, terms, columns
        nz = place.nz
        self.whole = (top, rows)
        self.early = (top, rows - late)
        self.late = (top + rows - late, late)
        self.first = (top, half)
        self.second = (top + half, rows - late - half)
        (self.side, self.in_first, self.in_second, self.in_x, self.in_y, self.in_line, self.in_late,
         self.in_plane) = room
        at = [base]

        def take(count):
            at[0] += count
            return at[0] - count

        self.sib = take(4 * nz)
        self.d1, self.d2, self.xs, self.ys = (take(nz) for _ in range(4))
        self.line = take(nz + 1)
        self.late_line = take(4 * (nz + 1))
        self.plane = take(3)

    @staticmethod
    def rooms(nz, columns, top, rows, late, half):
        def room(count, size):
            return pltpu.VMEM((count, size, columns), BF16)

        early = rows - late
        return [
            room(4 * nz, rows), room(nz, half), room(nz, early - half), room(nz, early), room(nz, early),
            room(nz + 1, early), room(4 * (nz + 1), late), room(3, late),
        ]

    def slot(self, column, z):
        return column * self.p.nz + z

    def term(self, column, z, part, other_core=False):
        return self.terms.at[self.p.block(column, z, other_core), pl.ds(*part), pl.ds(*self.columns)]

    def add(self, target, term):
        count = target.shape[0]
        step = count if count <= 48 else next(s for s in (48, 32, 16) if count % s == 0)

        def some(i, carry):
            rs = pl.ds(pl.multiple_of(i * step, 16), step)
            target[rs, :] = target[rs, :] + term[rs, :]
            return carry

        lax.fori_loop(0, count // step, some, 0)

    def got(self, ref, number):
        self.w.copy(ref, ref, number, self.p.sib).wait_recv()
        return ref

    def send_sib(self, z):
        p = self.p
        for column in (3, 1, 2, 0):
            k = self.slot(column, z)
            self.w.copy(self.term(column, z, self.whole, True), self.side.at[k], self.sib + k, p.sib).start()

    def take_sib(self, column, z):
        k = self.slot(column, z)
        self.add(self.term(column, z, self.whole), self.got(self.side.at[k], self.sib + k))

    def corner(self, z):
        p = self.p
        self.take_sib(3, z)
        self.w.copy(self.term(3, z, self.first), self.in_first.at[z], self.d1 + z, p.yn).start()
        self.w.copy(self.term(3, z, self.second), self.in_second.at[z], self.d2 + z, p.xn).start()

    def take_rest(self, z):
        for column in (1, 2, 0):
            self.take_sib(column, z)

    def side_x(self, z):
        p = self.p
        self.add(self.term(1, z, self.first), self.got(self.in_first.at[z], self.d1 + z))
        self.w.copy(self.term(1, z, self.early), self.in_x.at[z], self.xs + z, p.xn).start()

    def side_y(self, z):
        p = self.p
        self.add(self.term(2, z, self.second), self.got(self.in_second.at[z], self.d2 + z))
        self.w.copy(self.term(2, z, self.early), self.in_y.at[z], self.ys + z, p.yn).start()

    def own(self, z):
        ref = self.term(0, z, self.early)
        self.add(ref, self.got(self.in_x.at[z], self.xs + z))
        self.add(ref, self.got(self.in_y.at[z], self.ys + z))
        self.along(z, ref, self.in_line, self.line, 0)

    def own_late(self, z):
        for column in range(4):
            self.along(z, self.term(column, z, self.late), self.in_late, self.late_line,
                       column * (self.p.nz + 1))

    def along(self, z, ref, room, number, at):
        p, nz = self.p, self.p.nz
        below, above = p.z > 0, p.z < nz - 1

        def take(slot):
            self.add(ref, self.got(room.at[at + slot], number + at + slot))

        def send(slot, partner):
            self.w.copy(ref, room.at[at + slot], number + at + slot, partner).start()

        pl.when((z >= p.z) & below)(lambda: take(z))
        pl.when((z < p.z) & above)(lambda: take(z))
        pl.when((z == p.z) & above)(lambda: take(nz))
        pl.when(z > p.z)(lambda: send(z, p.me + 8))
        pl.when(z < p.z)(lambda: send(jnp.where(z == p.z - 1, nz, z), p.me - 8))

    def plane_corner(self):
        p = self.p
        self.w.copy(self.term(3, p.z, self.late), self.in_plane.at[0], self.plane, p.yn).start()

    def plane_sides(self):
        p = self.p
        self.w.copy(self.term(2, p.z, self.late), self.in_plane.at[2], self.plane + 2, p.yn).start()
        ref = self.term(1, p.z, self.late)
        self.add(ref, self.got(self.in_plane.at[0], self.plane))
        self.w.copy(ref, self.in_plane.at[1], self.plane + 1, p.xn).start()

    def plane_own(self):
        ref = self.term(0, self.p.z, self.late)
        self.add(ref, self.got(self.in_plane.at[1], self.plane + 1))
        self.add(ref, self.got(self.in_plane.at[2], self.plane + 2))

    def step(self, kind, number, by_plane):
        p = self.p
        plane, digit = number // 10, number % 10
        takes = (self.send_sib, self.corner, self.take_rest, self.side_x, self.side_y, self.own, self.own_late)
        ends = (self.plane_corner, self.plane_sides, self.plane_own)
        if kind >= len(takes):
            end = ends[kind - len(takes)]
            return (lambda: pl.when(p.z == plane)(end)) if by_plane else end
        take = takes[kind]
        if not by_plane:
            return lambda: p.level(digit, take)
        if take in (self.own, self.own_late):
            return lambda: pl.when((p.z == plane - digit) | (p.z == plane + digit))(lambda: take(plane))
        return lambda: take(plane)

    def drain(self):
        p, nz = self.p, self.p.nz

        def sent(ref, number):
            self.w.copy(ref, ref, number, p.sib).wait_send()

        for i in range(3):
            sent(self.in_plane.at[i], self.plane + i)

        def one(z, carry):
            for column in range(4):
                k = self.slot(column, z)
                sent(self.side.at[k], self.sib + k)
            sent(self.in_first.at[z], self.d1 + z)
            sent(self.in_second.at[z], self.d2 + z)
            sent(self.in_x.at[z], self.xs + z)
            sent(self.in_y.at[z], self.ys + z)

            def lines(slot):
                sent(self.in_line.at[slot], self.line + slot)
                for column in range(4):
                    at = column * (nz + 1) + slot
                    sent(self.in_late.at[at], self.late_line + at)

            pl.when(z > p.z)(lambda: lines(z))
            pl.when(z < p.z)(lambda: lines(jnp.where(z == p.z - 1, nz, z)))
            return carry

        lax.fori_loop(0, nz, one, 0)


def scatter_count(nz):
    return 4 * nz + 4 * nz + nz + 1 + 4 * (nz + 1) + 3


def build_masks(plan, ids_ref, len_ref, key_add, query_one):
    for r in range(plan.rows):
        ids = jnp.broadcast_to(ids_ref[r : r + 1, :], (LANES, SLOTS))
        label = lax.broadcasted_iota(jnp.int32, (LANES, SLOTS), 0)
        place = lax.broadcasted_iota(jnp.int32, (LANES, SLOTS), 1)
        start = jnp.sum((ids < label).astype(F32), axis=1, keepdims=True)
        lengths = len_ref[r]
        lengths = lengths[0:1, :] + lengths[1:2, :]
        live = jnp.zeros((LANES, SLOTS), jnp.int32)
        for j in range(PAIRS):
            live = jnp.where(label == j, lengths[:, j : j + 1], live)
        same = ids == label
        ok = same & (place.astype(F32) - start < live.astype(F32))
        rs = pl.ds(r * SLOTS, SLOTS)
        key_add[rs, :] = jnp.where(ok | (label >= PAIRS), 0.0, -1e30).T.astype(BF16)
        query_one[rs, :] = same.astype(F32).T.astype(BF16)


def split_heads(v):
    lane = lax.broadcasted_iota(jnp.int32, v.shape, 1)
    zero = jnp.zeros_like(v)
    return jnp.concatenate(
        [jnp.where(lane < HEAD_DIM, v, zero), jnp.where(lane < HEAD_DIM, zero, v)], axis=0
    )


def join_heads(v):
    lane = lax.broadcasted_iota(jnp.int32, (SLOTS, LANES), 1)
    return jnp.where(lane < HEAD_DIM, v[:SLOTS], v[SLOTS:])


def head_pair(i, rows):
    r, p = lax.rem(i, rows), i // rows
    return (
        pl.ds(pl.multiple_of(r * SLOTS, 16), SLOTS),
        pl.ds(pl.multiple_of(p * LANES, LANES), LANES),
    )


def scores_of(rs, cs, qkv, key_add, query_one):
    q, k, one = qkv[0, rs, cs], qkv[1, rs, cs], query_one[rs, :]
    q_side = jnp.concatenate([split_heads(q), jnp.concatenate([one, one], axis=0)], axis=1)
    k_side = jnp.concatenate([k, key_add[rs, :]], axis=1)
    return dot_nt(k_side, q_side), q, k


def attend(i, rows, qkv, key_add, query_one, context, log_totals):
    rs, cs = head_pair(i, rows)
    scores, _, _ = scores_of(rs, cs, qkv, key_add, query_one)
    top = jnp.max(scores, axis=0, keepdims=True)
    raised = jnp.exp(scores - top)
    total = jnp.sum(raised, axis=0, keepdims=True)
    shares = (raised * (1.0 / total)).astype(BF16)
    log_totals[i] = top + jnp.log(total)
    context[rs, cs] = join_heads(dot_tn(shares, qkv[2, rs, cs])).astype(BF16)


def attend_back(i, rows, qkv, key_add, query_one, log_totals, grad_context, grad_qkv):
    rs, cs = head_pair(i, rows)
    scores, q, k = scores_of(rs, cs, qkv, key_add, query_one)
    shares = jnp.exp(scores - log_totals[i])
    grad = split_heads(grad_context[rs, cs])
    grad_shares = dot_nt(qkv[2, rs, cs], grad)
    inner = jnp.sum(shares * grad_shares, axis=0, keepdims=True)
    grad_scores = (shares * (grad_shares - inner)).astype(BF16)
    grad_qkv[2, rs, cs] = dot_nn(shares.astype(BF16), grad).astype(BF16)
    grad_qkv[1, rs, cs] = dot_nn(grad_scores, split_heads(q)).astype(BF16)
    grad_qkv[0, rs, cs] = (join_heads(dot_tn(grad_scores, k)) * 0.125).astype(BF16)


def run_beside(count, body, steps):
    def turn(i, carry):
        body(i)
        for j, some in enumerate(steps):
            if some:

                @pl.when(i == j)
                def _(some=some):
                    for step in some:
                        step()

        return carry

    lax.fori_loop(0, count, turn, 0)


def after(code, steps):
    at = ORDER.index(code) + 1
    out = []
    while at < len(ORDER) and ORDER[at] >= 10000:
        out.append(steps[ORDER[at]])
        at += 1
    return out


def beside(kind, count, steps):
    return [after(kind + i, steps) for i in range(count)]


def run(steps):
    for step in steps:
        step()


def joint_weight(plan, ref, b):
    jr = plan.joint_rows
    return ref[0 : plan.joint_src, b * jr : (b + 1) * jr, :].reshape(D, D)


def out_weight(plan, ref):
    return ref[plan.joint_src : plan.n].reshape(D, D)


def in_weight(plan, ref, c):
    ir = plan.in_rows
    return ref[0 : plan.in_src, pl.ds(pl.multiple_of(c * ir, 16), ir), :].reshape(D, D)


def back_weight(plan, ref, c):
    return ref[back_blocks(plan, c)].reshape(D, D)


def back_blocks(plan, c):
    per = (plan.n - plan.in_src) // 4
    return pl.ds(plan.in_src + c * per, per)


def row_slots(r):
    return pl.ds(pl.multiple_of(r * SLOTS, 16), SLOTS)


def token_tiles(plan, size, fn):
    def one(t, carry):
        fn(pl.ds(pl.multiple_of(t * size, 16), size))
        return carry

    lax.fori_loop(0, plan.tokens // size, one, 0)


def gelu_with_slope(h):
    cdf = 0.5 * (1.0 + lax.erf(h * 0.7071067811865476))
    return h * cdf, cdf + h * jnp.exp(-0.5 * h * h) * 0.3989422804014327


def norm_parts(v):
    centred = v - row_mean(v)
    rstd = lax.rsqrt(row_mean(centred * centred) + NORM_EPS)
    return centred * rstd, rstd


def norm_back(grad, xhat, rstd):
    return rstd * (grad - row_mean(grad) - xhat * row_mean(grad * xhat))


def layer_kernel(plan, *refs):
    (x_in, ids, lens, shard_a, shard_f, out_grad_in) = refs[:6]
    (layer_out, in_grad, attn_grad, ffn_grad, bias_grad, params_far, qkv_far, context_far) = refs[6:14]
    (x, weights, active, slope, terms_f, norm_b, grad_hidden, grad_low, acc, xhat, rstd_first, log_totals, key_add,
     query_one, vec, vec_own, vec_held, joined_a, joined_f, halo_a, halo_f, end_a, end_f, vec_a, vec_b, got_a, got_b,
     got, out_a, out_f, send, recv, vec_send, vec_recv, local) = refs[14:49]
    room_f, room_1, room_2 = refs[49:57], refs[57:65], refs[65:73]
    n, nz, rows = plan.n, plan.nz, plan.rows
    place = Place(plan)
    me = place.me
    wire = Wire(send, recv)
    tail_a, tail_f = plan.tail_a, plan.tail_f
    hub_a, hub_b = plan.at_attn_vec[0], plan.at_bias_in[0]
    va, vf, gap = 5 * D // LANES, 3 * D // LANES, plan.gap
    bits = n.bit_length() - 1
    ra, half = plan.rows_a, D // 2
    jr, ir = plan.joint_rows, plan.in_rows
    per = (n - plan.in_src) // 4
    turns = HEADS // 2 * rows
    cols = [pl.ds(u * LANES, LANES) for u in range(6)]
    params = terms_f.at[:, 0:ra, :]
    qkv, context = slope.at[0:3], slope.at[3]
    out_grad = grad_hidden
    params_back = weights.at[:, 0:ra, :]
    terms_a = weights.at[:, ra : 2 * ra, :]
    qkv_back, context_back = active.at[0:3], active.at[3]
    grad_qkv, grad_context = slope.at[0:3], slope.at[3]

    base = [0]

    def numbers(count):
        base[0] += count
        return base[0] - count

    halo_in, halo_out = numbers(2), numbers(2)
    gather_a = Gather(place, wire, numbers(gather_count(nz)), params, *plan.part_a)
    gather_f = Gather(place, wire, numbers(gather_count(nz)), weights, *plan.part_f)
    scatter_f = Scatter(place, wire, numbers(scatter_count(nz)), terms_f, (0, D), *plan.part_f, room_f)
    scatter_1 = Scatter(place, wire, numbers(scatter_count(nz)), weights, (0, half), ra, *plan.part_a[1:], room_1)
    scatter_2 = Scatter(place, wire, numbers(scatter_count(nz)), weights, (half, half), ra, *plan.part_a[1:], room_2)
    vec_steps = add_over_all(place, wire, numbers(bits), vec_own, vec_held)
    movers = (None, (gather_a, False), (gather_f, True), (scatter_f, True), (scatter_1, False), (scatter_2, False))
    steps = {}
    for code in ORDER:
        family, kind, number = code // 10000, code // 100 % 100, code % 100
        if family == 6:
            steps[code] = vec_steps[number]
        elif family:
            mover, by_plane = movers[family]
            steps[code] = mover.step(kind, number, by_plane)

    copies = {}

    def copy_here(name, src, dst):
        copies[name] = pltpu.make_async_copy(src, dst, local.at[len(copies)])

    copy_here("x", x_in, x)
    copy_here("out_grad", out_grad_in, out_grad)
    copy_here("params", params, params_far)
    copy_here("qkv", qkv, qkv_far)
    copy_here("context", context, context_far)
    copy_here("result", out_grad, layer_out)
    copy_here("params_back", params_far, params_back)
    copy_here("qkv_back", qkv_far, qkv_back)
    copy_here("context_back", context_far, context_back)
    copy_here("in_grad", acc, in_grad)
    copies["x"].start()
    copies["out_grad"].start()

    joined_a[tail_a : tail_a + plan.unit_a, :] = shard_a[...].astype(F32)
    joined_f[tail_f : tail_f + plan.unit_f, :] = shard_f[...].astype(F32)
    end_a[...] = joined_a[plan.unit_a : plan.unit_a + tail_a, :]
    end_f[...] = joined_f[plan.unit_f : plan.unit_f + tail_f, :]
    at = tail_a + plan.at_attn_vec[1]
    vec_a[0:va, :] = joined_a[at : at + va, :].astype(BF16)
    at = tail_f + plan.at_ffn_vec[1]
    vec_a[va : va + vf, :] = joined_f[at : at + vf, :].astype(BF16)
    at = tail_f + plan.at_bias_in[1]
    vec_b[...] = jnp.zeros_like(vec_b)
    vec_b[0:gap, :] = joined_f[at : at + gap, :].astype(BF16)
    place.barrier(hubs=(hub_a, hub_b))

    @pl.when(me < n - 1)
    def _():
        wire.copy(end_a, halo_a, halo_in, me + 1).start()
        wire.copy(end_f, halo_f, halo_in + 1, me + 1).start()

    def vec_copy(src, dst, which, partner):
        return pltpu.make_async_remote_copy(
            src_ref=src, dst_ref=dst, send_sem=vec_send.at[partner], recv_sem=vec_recv.at[which],
            device_id=(partner,), device_id_type=MESH,
        )

    def to_all(src, dst, which, fn):
        @pl.when(me == (hub_a, hub_b)[which])
        def _():
            def one(j, carry):
                pl.when(j != me)(lambda: fn(vec_copy(src, dst, which, j)))
                return carry

            lax.fori_loop(0, n, one, 0)

    to_all(vec_a, got_a, 0, lambda copy: copy.start())
    to_all(vec_b, got_b, 1, lambda copy: copy.start())

    @pl.when(me > 0)
    def _():
        wire.copy(end_a, halo_a, halo_in, me - 1).wait_recv()
        joined_a[0:tail_a, :] = halo_a[...]

    start = tail_a - plan.shift_a(me)
    mine = params.at[me]

    @pl.when(me < plan.joint_src)
    def _():
        for b in range(3):
            for u in range(6):
                mine[b * jr : (b + 1) * jr, cols[u]] = joined_a[
                    pl.ds(start + 6 * b + u, jr, stride=18), :
                ].astype(BF16)

    @pl.when(me >= plan.joint_src)
    def _():
        for u in range(6):
            mine[:, cols[u]] = joined_a[pl.ds(start + u, ra, stride=6), :].astype(BF16)

    run([steps[code] for code in ORDER[: ORDER.index(RELAY)]])

    @pl.when(me > 0)
    def _():
        wire.copy(end_f, halo_f, halo_in + 1, me - 1).wait_recv()
        joined_f[0:tail_f, :] = halo_f[...]

    start_f = tail_f - plan.shift_f(me)
    mine_f = weights.at[me]

    @pl.when(me < plan.in_src)
    def _():
        for c in range(4):
            for u in range(6):
                mine_f[c * ir : (c + 1) * ir, cols[u]] = joined_f[
                    pl.ds(start_f + 6 * c + u, ir, stride=24), :
                ].astype(BF16)

    @pl.when(me >= plan.in_src)
    def _():
        for u in range(6):
            mine_f[:, cols[u]] = joined_f[pl.ds(start_f + u, plan.rows_f, stride=6), :].astype(BF16)

    build_masks(plan, ids, lens, key_add, query_one)
    run(after(RELAY, steps))

    @pl.when(me == hub_a)
    def _():
        got_a[...] = vec_a[...]

    @pl.when(me == hub_b)
    def _():
        got_b[...] = vec_b[...]

    @pl.when(me != hub_a)
    def _():
        vec_copy(vec_a, got_a, 0, hub_a).wait_recv()

    @pl.when(me != hub_b)
    def _():
        vec_copy(vec_b, got_b, 1, hub_b).wait_recv()

    got[0 : va + vf, :] = got_a[0 : va + vf, :].astype(F32)
    got[va + vf : va + vf + gap, :] = got_b[0:gap, :].astype(F32)
    vec[...] = jnp.zeros_like(vec)
    for u in range(6):
        vec[0:5, cols[u]] = got[pl.ds(u, 5, stride=6), :]
        vec[9:12, cols[u]] = got[pl.ds(va + u, 3, stride=6), :]
        vec[5:9, cols[u]] = got[pl.ds(va + vf + u, 4, stride=6), :]

    copies["params"].start()
    copies["x"].wait()
    for b in range(3):
        now = dot_nn(x[...], joint_weight(plan, params, b))
        if b == 0:
            now = (now + vec[0:1, :]).astype(BF16) * jnp.asarray(HEAD_DIM ** (-0.5), BF16)
        elif b == 2:
            now = now + vec[1:2, :]
        qkv[b] = now.astype(BF16)
        run(after(PROJECT + b, steps))
    copies["qkv"].start()
    run_beside(
        turns,
        lambda i: attend(i, rows, qkv, key_add, query_one, context, log_totals),
        beside(ATTEND, turns, steps),
    )
    copies["context"].start()
    gain_first, shift_first, bias_back = vec[3:4, :], vec[4:5, :], vec[9:10, :]
    gain_second, shift_second = vec[10:11, :], vec[11:12, :]

    def norm(t):
        rs = row_slots(t)
        v = x[rs, :].astype(F32) + (dot_nn(context[rs, :], out_weight(plan, params)) + vec[2:3, :])
        now, rstd = norm_parts(v)
        xhat[rs, :] = now
        rstd_first[rs, :] = jnp.broadcast_to(rstd, (rstd.shape[0], LANES))
        v = now * gain_first + shift_first
        norm_b[rs, :] = v.astype(BF16)
        acc[rs, :] = v + bias_back

    run_beside(rows, norm, beside(NORM, rows, steps))

    copies["qkv"].wait()
    copies["context"].wait()

    def up(i):
        c, rs = i // rows, row_slots(lax.rem(i, rows))
        hidden = dot_nn(norm_b[rs, :], in_weight(plan, weights, c)) + vec[pl.ds(5 + c, 1), :]
        value, incline = gelu_with_slope(hidden)
        active[c, rs, :] = value.astype(BF16)
        slope[c, rs, :] = incline.astype(BF16)

    run_beside(4 * rows, up, beside(UP, 4 * rows, steps))

    def down(i):
        c, rs = i // rows, row_slots(lax.rem(i, rows))
        acc[rs, :] += dot_nn(active[c, rs, :], back_weight(plan, weights, c))

    run_beside(4 * rows, down, beside(DOWN, 4 * rows, steps))
    copies["out_grad"].wait()
    grads = vec_own.at[0]
    grads[...] = jnp.zeros(grads.shape, F32)

    def turn(rs):
        now, rstd = norm_parts(acc[rs, :])
        cot = out_grad[rs, :].astype(F32)
        out_grad[rs, :] = (now * gain_second + shift_second).astype(BF16)
        grads[10:11, :] += col_sum(cot * now)
        grads[11:12, :] += col_sum(cot)
        grad = norm_back(cot * gain_second, now, rstd)
        acc[rs, :] = grad
        low = grad.astype(BF16)
        grad_low[rs, :] = low
        grads[9:10, :] += col_sum(low.astype(F32))

    token_tiles(plan, SLOTS, turn)
    copies["result"].start()
    copies["params"].wait()
    gather_a.drain()

    back_order = (2, 3, 0, 1)
    for c in back_order:
        terms_f[back_blocks(plan, c)] = (
            dot_tn(active[c], grad_low[...]).astype(BF16).reshape(per, plan.rows_f, D)
        )
        if c == back_order[1]:
            run(after(BACK_WEIGHT, steps))
    run(after(BACK_WEIGHT + 1, steps))
    copies["context_back"].start()
    copies["qkv_back"].start()
    copies["result"].wait()

    def hidden_back(i):
        c, t = i // rows, lax.rem(i, rows)
        rs = row_slots(t)
        grad = (slope[c, rs, :].astype(F32) * dot_nt(grad_low[rs, :], back_weight(plan, weights, c))).astype(BF16)
        grad_hidden[rs, :] = grad
        grads[pl.ds(5 + c, 1), :] += col_sum(grad.astype(F32))
        acc[rs, :] += dot_nt(grad, in_weight(plan, weights, c))

        @pl.when(t == rows - 1)
        def _():
            in_rows = pl.ds(pl.multiple_of(c * ir, 16), ir)
            terms_f[0 : plan.in_src, in_rows, :] = (
                dot_tn(norm_b[...], grad_hidden[...]).astype(BF16).reshape(plan.in_src, ir, D)
            )

    run_beside(4 * rows, hidden_back, beside(HIDDEN, 4 * rows, steps))
    gather_f.drain()
    copies["params_back"].start()

    def leave(rs):
        grad, now = acc[rs, :], xhat[rs, :]
        grads[3:4, :] += col_sum(grad * now)
        grads[4:5, :] += col_sum(grad)
        grad = norm_back(grad * gain_first, now, rstd_first[rs, 0:1])
        acc[rs, :] = grad
        grad = grad.astype(BF16)
        grad_low[rs, :] = grad
        grads[2:3, :] += col_sum(grad.astype(F32))

    token_tiles(plan, SLOTS, leave)
    run(after(LEAVE, steps))
    copies["params_back"].wait()

    def into_context(rs):
        grad_context[rs, :] = dot_nt(grad_low[rs, :], out_weight(plan, params_back)).astype(BF16)

    token_tiles(plan, SLOTS, into_context)
    run(after(LEAVE + 1, steps))
    copies["context_back"].wait()
    terms_a[plan.joint_src : n] = (
        dot_tn(context_back[...], grad_low[...]).astype(BF16).reshape(n - plan.joint_src, ra, D)
    )
    copies["qkv_back"].wait()
    run(after(LEAVE + 2, steps))

    def joint_terms(first):
        for b in range(3):
            terms_a[0 : plan.joint_src, b * jr : (b + 1) * jr, first : first + half] = (
                dot_tn(x[...], grad_qkv[b, :, first : first + half]).astype(BF16).reshape(plan.joint_src, jr, half)
            )

    def back(i):
        attend_back(i, rows, qkv_back, key_add, query_one, log_totals, grad_context, grad_qkv)

    beside_back = beside(ATTEND_BACK, turns, steps)
    beside_back[turns // 2 - 1] += [lambda: joint_terms(0)] + after(JOINT + 1, steps)
    run_beside(turns, back, beside_back)
    joint_terms(half)
    grads[0:1, :] = col_sum(grad_qkv[0].astype(F32))
    grads[1:2, :] = col_sum(grad_qkv[2].astype(F32))
    run(after(JOINT + 2, steps))

    def input_grad(rs):
        now = acc[rs, :]
        for b in range(3):
            now = now + dot_nt(grad_qkv[b, rs, :], joint_weight(plan, params_back, b))
        acc[rs, :] = now

    size = plan.tokens // 4
    for j in range(4):
        input_grad(pl.ds(j * size, size))
        if j == 3:
            copies["in_grad"].start()
        run(after(INPUT_GRAD + j, steps))

    summed = vec_own.at[bits]
    total_f, total_a = terms_f.at[me], terms_a.at[me]

    @pl.when(me < plan.in_src)
    def _():
        for c in range(4):
            for u in range(6):
                joined_f[pl.ds(6 * c + u, ir, stride=24), :] = total_f[c * ir : (c + 1) * ir, cols[u]].astype(F32)

    @pl.when(me >= plan.in_src)
    def _():
        for u in range(6):
            joined_f[pl.ds(u, plan.rows_f, stride=6), :] = total_f[:, cols[u]].astype(F32)

    @pl.when(me < plan.joint_src)
    def _():
        for b in range(3):
            for u in range(6):
                joined_a[pl.ds(6 * b + u, jr, stride=18), :] = total_a[b * jr : (b + 1) * jr, cols[u]].astype(F32)

    @pl.when(me >= plan.joint_src)
    def _():
        for u in range(6):
            joined_a[pl.ds(u, ra, stride=6), :] = total_a[:, cols[u]].astype(F32)

    head_a, head_f = joined_a.at[0:tail_a], joined_f.at[0:tail_f]

    @pl.when(me > 0)
    def _():
        wire.copy(head_f, out_f, halo_out + 1, me - 1).start()
        wire.copy(head_a, out_a, halo_out, me - 1).start()

    rest_a = pl.ds(plan.block_a, tail_a)
    rest_f = pl.ds(plan.block_f, tail_f)

    @pl.when(me < n - 1)
    def _():
        wire.copy(head_f, out_f, halo_out + 1, me + 1).wait_recv()
        wire.copy(head_a, out_a, halo_out, me + 1).wait_recv()
        joined_f[rest_f, :] = out_f[...]
        joined_a[rest_a, :] = out_a[...]

    @pl.when(me == hub_b)
    def _():
        for u in range(6):
            joined_f[pl.ds(plan.block_f + u, 4, stride=6), :] = summed[5:9, cols[u]]
        joined_f[plan.block_f + gap : plan.block_f + tail_f, :] = out_f[0 : tail_f - gap, :]

    @pl.when(me == n - 1)
    def _():
        joined_f[rest_f, :] = jnp.zeros((tail_f, LANES), F32)
        joined_a[rest_a, :] = jnp.zeros((tail_a, LANES), F32)
        for u in range(6):
            joined_f[pl.ds(plan.block_f + u, 3, stride=6), :] = summed[9:12, cols[u]]
            joined_a[pl.ds(plan.block_a + u, 5, stride=6), :] = summed[0:5, cols[u]]

    ffn_grad[...] = joined_f[pl.ds(plan.shift_f(me), plan.unit_f), :]
    attn_grad[...] = joined_a[pl.ds(plan.shift_a(me), plan.unit_a), :]
    for u in range(6):
        bias_grad[u : u + 1, :] = summed[2:3, cols[u]]
    copies["in_grad"].wait()
    for mover in (scatter_f, scatter_1, scatter_2):
        mover.drain()
    to_all(vec_a, got_a, 0, lambda copy: copy.wait_send())
    to_all(vec_b, got_b, 1, lambda copy: copy.wait_send())

    @pl.when(me < n - 1)
    def _():
        wire.copy(end_a, halo_a, halo_in, me + 1).wait_send()
        wire.copy(end_f, halo_f, halo_in + 1, me + 1).wait_send()

    @pl.when(me > 0)
    def _():
        wire.copy(head_f, out_f, halo_out + 1, me - 1).wait_send()
        wire.copy(head_a, out_a, halo_out, me - 1).wait_send()


def fused_body(plan, layer_in, pair_ids, pair_lengths, attn_shard, ffn_shard, out_grad):
    n, t, nz = plan.n, plan.tokens, plan.nz
    shape = jax.ShapeDtypeStruct
    bits = n.bit_length() - 1
    turns = HEADS // 2 * plan.rows
    sems = 4 + bits + 2 * gather_count(nz) + 3 * scatter_count(nz)
    low, full = pltpu.VMEM((t, D), BF16), pltpu.VMEM((t, D), F32)
    blocks = pltpu.VMEM((n, plan.rows_f, D), BF16)
    wide = pltpu.VMEM((4, t, D), BF16)
    side = pltpu.VMEM((t, LANES), BF16)
    vmem, far = pl.BlockSpec(memory_space=pltpu.VMEM), pl.BlockSpec(memory_space=pl.ANY)

    def units(count):
        return pltpu.VMEM((count, LANES), F32)

    def low_units(count):
        return pltpu.VMEM((count, LANES), BF16)

    layer_out, in_grad, attn_grad, ffn_grad, bias_grad = pl.pallas_call(
        functools.partial(layer_kernel, plan),
        name="layer",
        out_shape=[
            shape((t, D), BF16),
            shape((t, D), F32),
            shape((plan.unit_a, LANES), F32),
            shape((plan.unit_f, LANES), F32),
            shape((D // LANES, LANES), F32),
            shape((n, plan.rows_a, D), BF16),
            shape((3, t, D), BF16),
            shape((t, D), BF16),
        ],
        in_specs=[far] + [vmem] * 4 + [far],
        out_specs=[far] * 2 + [vmem] * 3 + [far] * 3,
        scratch_shapes=[
            low, blocks, wide, wide, blocks, low, low, low, full, full,
            pltpu.VMEM((t, LANES), F32),
            pltpu.VMEM((turns, 1, 2 * SLOTS), F32),
            side, side,
            pltpu.VMEM((16, D), F32),
            pltpu.VMEM((bits + 1, 16, D), F32),
            pltpu.VMEM((bits, 16, D), F32),
            units(plan.tail_a + -(-plan.unit_a // 8) * 8 + 8),
            units(plan.tail_f + -(-plan.unit_f // 8) * 8 + 8),
            units(plan.tail_a), units(plan.tail_f), units(plan.tail_a), units(plan.tail_f),
            low_units(48), low_units(32), low_units(48), low_units(32),
            units(80), units(plan.tail_a), units(plan.tail_f),
            pltpu.SemaphoreType.DMA((sems,)),
            pltpu.SemaphoreType.DMA((sems,)),
            pltpu.SemaphoreType.DMA((n,)),
            pltpu.SemaphoreType.DMA((2,)),
            pltpu.SemaphoreType.DMA((12,)),
        ]
        + Scatter.rooms(nz, D, *plan.part_f)
        + Scatter.rooms(nz, D // 2, *plan.part_a)
        + Scatter.rooms(nz, D // 2, *plan.part_a),
        compiler_params=pltpu.CompilerParams(
            collective_id=0, has_side_effects=True, vmem_limit_bytes=VMEM_LIMIT
        ),
    )(
        layer_in.reshape(t, D),
        pair_ids,
        jnp.swapaxes(pair_lengths, 1, 2),
        attn_shard.reshape(plan.unit_a, LANES),
        ffn_shard.reshape(plan.unit_f, LANES),
        out_grad.reshape(t, D),
    )[:5]
    return (
        layer_out.reshape(layer_in.shape),
        in_grad.reshape(layer_in.shape),
        attn_grad.reshape(-1),
        ffn_grad.reshape(-1),
        bias_grad.reshape(-1),
    )


def unpack_attention(flattened):
    offset = 3 * D * D
    weight_joint = flattened[:offset].reshape(D, 3 * D)
    weight_out = flattened[offset : offset + D * D].reshape(D, D)
    offset = offset + D * D
    vectors = flattened[offset : offset + 5 * D].reshape(5, D)
    return (weight_joint, weight_out, vectors[0], vectors[1], vectors[2], vectors[3], vectors[4])


def unpack_feedforward(flattened):
    offset = D * FF
    weight_in = flattened[:offset].reshape(D, FF)
    bias_in = flattened[offset : offset + FF]
    offset = offset + FF
    weight_back = flattened[offset : offset + FF * D].reshape(FF, D)
    offset = offset + FF * D
    vectors = flattened[offset : offset + 3 * D].reshape(3, D)
    return (weight_in, bias_in, weight_back, vectors[0], vectors[1], vectors[2])


def layer_norm(values, gain_vec, shift_vec):
    row_mean = jnp.mean(values, axis=-1, keepdims=True)
    centred = values - row_mean
    row_var = jnp.mean(centred * centred, axis=-1, keepdims=True)
    return centred * lax.rsqrt(row_var + NORM_EPS) * gain_vec + shift_vec


def exact_gelu(values):
    return jax.nn.gelu(values, approximate=False)


def key_mask(pair_ids, pair_lengths):
    labels = jnp.arange(PAIRS, dtype=jnp.int32)
    member = pair_ids[:, :, None] == labels[None, None, :]
    starts = jnp.sum((pair_ids[:, :, None] < labels[None, None, :]).astype(jnp.int32), axis=1)
    live_len = pair_lengths[:, :, 0] + pair_lengths[:, :, 1]
    slot_start = jnp.sum(jnp.where(member, starts[:, None, :], 0), axis=-1)
    slot_len = jnp.sum(jnp.where(member, live_len[:, None, :], 0), axis=-1)
    places = jnp.arange(pair_ids.shape[1], dtype=jnp.int32)[None, :]
    is_live = places - slot_start < slot_len
    return (pair_ids[:, :, None] == pair_ids[:, None, :]) & is_live[:, None, :]


def contract_rows(one_side, other_side):
    return lax.dot_general(
        one_side, other_side, (((0,), (0,)), ((), ())), preferred_element_type=jnp.float32
    )


def contract_cols(one_side, other_side):
    return lax.dot_general(
        one_side, other_side, (((1,), (1,)), ((), ())), preferred_element_type=jnp.float32
    )


def attend_forward(queries, key_rows, value_rows, key_ok, score_scale):

    def head_block(block_index):
        head_start = block_index * 4
        query_b = lax.dynamic_slice_in_dim(queries, head_start, 4, 2)
        key_b = lax.dynamic_slice_in_dim(key_rows, head_start, 4, 2)
        value_b = lax.dynamic_slice_in_dim(value_rows, head_start, 4, 2)
        scores = (
            jnp.einsum("rqhd,rkhd->rhqk", query_b, key_b, preferred_element_type=jnp.float32)
            * score_scale
        )
        scores = jnp.where(key_ok[:, None], scores, -1e30)
        row_max = jnp.max(scores, axis=-1, keepdims=True)
        raised = jnp.exp(scores - row_max)
        totals = jnp.sum(raised, axis=-1, keepdims=True)
        shares = (raised / totals).astype(jnp.bfloat16)
        context = jnp.einsum("rhqk,rkhd->rqhd", shares, value_b, preferred_element_type=jnp.float32)
        return (context, row_max + jnp.log(totals))

    return lax.map(head_block, jnp.arange(HEADS // 4))


def attend_backward(queries, key_rows, value_rows, grad_context, log_totals, key_ok, score_scale):

    def head_block(operands):
        block_index, log_total = operands
        head_start = block_index * 4
        query_b = lax.dynamic_slice_in_dim(queries, head_start, 4, 2)
        key_b = lax.dynamic_slice_in_dim(key_rows, head_start, 4, 2)
        value_b = lax.dynamic_slice_in_dim(value_rows, head_start, 4, 2)
        grad_block = lax.dynamic_slice_in_dim(grad_context, head_start, 4, 2)
        scores = (
            jnp.einsum("rqhd,rkhd->rhqk", query_b, key_b, preferred_element_type=jnp.float32)
            * score_scale
        )
        shares = jnp.where(key_ok[:, None], jnp.exp(scores - log_total), 0.0)
        grad_shares = jnp.einsum(
            "rqhd,rkhd->rhqk", grad_block, value_b, preferred_element_type=jnp.float32
        )
        inner_sum = jnp.sum(shares * grad_shares, axis=-1, keepdims=True)
        grad_scores = (shares * (grad_shares - inner_sum)).astype(jnp.bfloat16)
        grad_query = (
            jnp.einsum("rhqk,rkhd->rqhd", grad_scores, key_b, preferred_element_type=jnp.float32)
            * score_scale
        )
        grad_key = (
            jnp.einsum("rhqk,rqhd->rkhd", grad_scores, query_b, preferred_element_type=jnp.float32)
            * score_scale
        )
        grad_value = jnp.einsum(
            "rhqk,rqhd->rkhd",
            shares.astype(jnp.bfloat16),
            grad_block,
            preferred_element_type=jnp.float32,
        )
        return (grad_query, grad_key, grad_value)

    gradients = lax.map(head_block, (jnp.arange(HEADS // 4), log_totals))
    return [jnp.moveaxis(piece, 0, 2).reshape(-1, D) for piece in gradients]


def plain_body(layer_in, pair_ids, pair_lengths, attn_shard, ffn_shard, out_grad):
    row_count = layer_in.shape[0]
    tokens = row_count * SLOTS
    score_scale = HEAD_DIM ** (-0.5)
    key_ok = key_mask(pair_ids, pair_lengths)
    att_whole = lax.all_gather(attn_shard, "fsdp", axis=0, tiled=True)
    weight_joint, weight_out, bias_query, bias_value, bias_out, gain_first, shift_first = (
        unpack_attention(att_whole)
    )
    inputs = layer_in.reshape(tokens, D)
    bias_joint = jnp.concatenate([bias_query, jnp.zeros_like(bias_query), bias_value]).astype(
        jnp.float32
    )
    projected = (
        jnp.dot(inputs, weight_joint, preferred_element_type=jnp.float32) + bias_joint
    ).astype(jnp.bfloat16)
    projected = projected.reshape(row_count, SLOTS, 3, HEADS, HEAD_DIM)
    queries = projected[:, :, 0]
    key_rows = projected[:, :, 1]
    value_rows = projected[:, :, 2]
    contexts, log_totals = attend_forward(queries, key_rows, value_rows, key_ok, score_scale)
    context = jnp.moveaxis(contexts, 0, 2).reshape(tokens, D).astype(jnp.bfloat16)
    attn_out = jnp.dot(context, weight_out, preferred_element_type=jnp.float32) + bias_out.astype(
        jnp.float32
    )
    norm_first, first_pull = jax.vjp(
        layer_norm,
        inputs.astype(jnp.float32) + attn_out,
        gain_first.astype(jnp.float32),
        shift_first.astype(jnp.float32),
    )
    norm_first_b = norm_first.astype(jnp.bfloat16)
    feed_whole = lax.all_gather(ffn_shard, "fsdp", axis=0, tiled=True)
    weight_in, bias_in, weight_back, bias_back, gain_second, shift_second = unpack_feedforward(
        feed_whole
    )
    hidden = jnp.dot(norm_first_b, weight_in, preferred_element_type=jnp.float32) + bias_in.astype(
        jnp.float32
    )
    active, gelu_pull = jax.vjp(exact_gelu, hidden)
    active_b = active.astype(jnp.bfloat16)
    ffn_out = jnp.dot(active_b, weight_back, preferred_element_type=jnp.float32) + bias_back.astype(
        jnp.float32
    )
    result, second_pull = jax.vjp(
        layer_norm,
        norm_first + ffn_out,
        gain_second.astype(jnp.float32),
        shift_second.astype(jnp.float32),
    )
    layer_out = result.astype(jnp.bfloat16).reshape(row_count, SLOTS, D)
    feed_back = lax.all_gather(ffn_shard, "fsdp", axis=0, tiled=True)
    weight_in, bias_in, weight_back, bias_back, gain_second, shift_second = unpack_feedforward(
        feed_back
    )
    cotangent = out_grad.reshape(tokens, D).astype(jnp.float32)
    grad_sum_second, grad_gain_second, grad_shift_second = second_pull(cotangent)
    grad_ffn = grad_sum_second.astype(jnp.bfloat16)
    grad_bias_back = jnp.sum(grad_ffn.astype(jnp.float32), axis=0)
    grad_weight_back = contract_rows(active_b, grad_ffn)
    (grad_hidden,) = gelu_pull(contract_cols(grad_ffn, weight_back))
    grad_hidden = grad_hidden.astype(jnp.bfloat16)
    grad_bias_in = jnp.sum(grad_hidden.astype(jnp.float32), axis=0)
    grad_weight_in = contract_rows(norm_first_b, grad_hidden)
    grad_norm_first = grad_sum_second + contract_cols(grad_hidden, weight_in)
    grad_sum_first, grad_gain_first, grad_shift_first = first_pull(grad_norm_first)
    feed_pad = feed_back.shape[0] - (2 * D * FF + FF + 3 * D)
    feed_full = jnp.concatenate(
        [
            grad_weight_in.reshape(-1),
            grad_bias_in,
            grad_weight_back.reshape(-1),
            grad_bias_back,
            grad_gain_second,
            grad_shift_second,
            jnp.zeros((feed_pad,), jnp.float32),
        ]
    )
    ffn_grad = lax.psum_scatter(feed_full, "fsdp", scatter_dimension=0, tiled=True)
    att_back = lax.all_gather(attn_shard, "fsdp", axis=0, tiled=True)
    weight_joint, weight_out, bias_query, bias_value, bias_out, gain_first, shift_first = (
        unpack_attention(att_back)
    )
    grad_attn = grad_sum_first.astype(jnp.bfloat16)
    grad_bias_out = jnp.sum(grad_attn.astype(jnp.float32), axis=0)
    out_bias_grad = lax.psum(grad_bias_out, "fsdp")
    grad_weight_out = contract_rows(context, grad_attn)
    grad_context = (
        contract_cols(grad_attn, weight_out)
        .astype(jnp.bfloat16)
        .reshape(row_count, SLOTS, HEADS, HEAD_DIM)
    )
    grad_query, grad_key, grad_value = attend_backward(
        queries, key_rows, value_rows, grad_context, log_totals, key_ok, score_scale
    )
    grad_projected = jnp.concatenate([grad_query, grad_key, grad_value], axis=-1).astype(
        jnp.bfloat16
    )
    column_sums = jnp.sum(grad_projected.astype(jnp.float32), axis=0)
    grad_weight_joint = contract_rows(inputs, grad_projected)
    in_grad = grad_sum_first + contract_cols(grad_projected, weight_joint)
    att_pad = att_back.shape[0] - (4 * D * D + 5 * D)
    attn_full = jnp.concatenate(
        [
            grad_weight_joint.reshape(-1),
            grad_weight_out.reshape(-1),
            column_sums[:D],
            column_sums[2 * D :],
            grad_bias_out,
            grad_gain_first,
            grad_shift_first,
            jnp.zeros((att_pad,), jnp.float32),
        ]
    )
    attn_grad = lax.psum_scatter(attn_full, "fsdp", scatter_dimension=0, tiled=True)
    return (layer_out, in_grad.reshape(row_count, SLOTS, D), attn_grad, ffn_grad, out_bias_grad)


def body(layer_in, pair_ids, pair_lengths, attn_shard, ffn_shard, out_grad, devices):
    plan = Plan(devices, attn_shard.shape[0], ffn_shard.shape[0], layer_in.shape[0])
    run = functools.partial(fused_body, plan) if plan.fits() else plain_body
    return run(layer_in, pair_ids, pair_lengths, attn_shard, ffn_shard, out_grad)


def solution(mesh):
    placed = (
        P("fsdp", None, None),
        P("fsdp", None),
        P("fsdp", None, None),
        P("fsdp"),
        P("fsdp"),
        P("fsdp", None, None),
    )
    return jax.shard_map(
        functools.partial(body, devices=mesh.shape["fsdp"]),
        mesh=mesh,
        in_specs=placed,
        out_specs=(P("fsdp", None, None), P("fsdp", None, None), P("fsdp"), P("fsdp"), P()),
        check_vma=False,
    )
```

```python
import functools

import jax
import jax.numpy as jnp
from jax import lax
from jax.experimental import pallas as pl
from jax.experimental.pallas import tpu as pltpu
from jax.sharding import PartitionSpec as P

D = 768
HEADS = 12
HEAD_DIM = 64
FF = 3072
SLOTS = 416
PAIRS = 3
LANES = 128
NORM_EPS = 1e-12
F32 = jnp.float32
BF16 = jnp.bfloat16
MESH = pl.DeviceIdType.MESH
VMEM_LIMIT = 62 << 20
FINISH = 11
RELAY, PROJECT, ATTEND, NORM, UP, DOWN, TURN, BACK_WEIGHT, HIDDEN, LEAVE, ATTEND_BACK, JOINT, INPUT_GRAD = range(
    0, 1300, 100
)


def dot_nn(a, b):
    return lax.dot_general(a, b, (((1,), (0,)), ((), ())), preferred_element_type=F32)


def dot_nt(a, b):
    return lax.dot_general(a, b, (((1,), (1,)), ((), ())), preferred_element_type=F32)


def dot_tn(a, b):
    return lax.dot_general(a, b, (((0,), (0,)), ((), ())), preferred_element_type=F32)


def row_mean(v):
    return jnp.sum(v, axis=1, keepdims=True) * (1.0 / D)


def col_sum(v):
    return jnp.sum(v, axis=0, keepdims=True)


class Plan:
    def __init__(self, n, attn_shard_len, ffn_shard_len, row_count):
        self.n = n
        self.nz = n // 8
        self.rows = row_count
        self.tokens = row_count * SLOTS
        self.unit_a = attn_shard_len // LANES
        self.unit_f = ffn_shard_len // LANES
        self.block_a = 4 * D * D // LANES // n
        self.block_f = 2 * D * FF // LANES // n
        self.rows_a = 4 * D // n
        self.rows_f = 2 * FF // n
        self.joint_rows = self.rows_a // 3
        self.joint_src = 3 * n // 4
        self.in_rows = self.rows_f // 4
        self.in_src = n // 2
        self.part_a = (0, self.rows_a, 16, 32)
        self.part_f = (0, self.rows_f, 48, 64)
        self.gap = FF // LANES
        self.at_attn_vec = divmod(4 * D * D // LANES, self.unit_a)
        self.at_bias_in = divmod(D * FF // LANES, self.unit_f)
        self.at_ffn_vec = divmod(2 * D * FF // LANES + self.gap, self.unit_f)

    def shift_a(self, me):
        return me * (self.unit_a - self.block_a)

    def shift_f(self, me):
        return me * (self.unit_f - self.block_f) - jnp.where(me >= self.in_src, self.gap, 0)

    def fits(self):
        n = self.n
        if self.nz != 4 or n % 8 or self.rows_a % 48 or self.rows_f % 64:
            return False
        last_a = (n - 1) * (self.unit_a - self.block_a)
        step_f = self.unit_f - self.block_f
        last_f = max((self.in_src - 1) * step_f, (n - 1) * step_f - self.gap)
        first_f = self.in_src * step_f - self.gap
        self.tail_a = -(-(last_a + 1) // 8) * 8
        self.tail_f = -(-(last_f + 2) // 8) * 8
        vec_a, vec_f = 5 * D // LANES, 3 * D // LANES
        return (
            step_f >= 0
            and self.unit_a >= self.block_a
            and first_f >= 0
            and self.tail_a <= self.block_a
            and self.tail_f <= self.block_f
            and self.at_attn_vec[0] == n - 1
            and self.at_ffn_vec[0] == n - 1
            and self.at_bias_in[0] == self.in_src - 1
            and self.unit_a - self.at_attn_vec[1] <= self.tail_a
            and self.unit_f - self.at_ffn_vec[1] <= self.tail_f
            and self.at_attn_vec[1] + vec_a <= self.unit_a
            and self.at_ffn_vec[1] + vec_f <= self.unit_f
            and self.at_bias_in[1] + self.gap <= self.unit_f
            and self.at_bias_in[1] == self.block_f - (self.in_src - 1) * step_f
        )


class Place:
    def __init__(self, plan):
        self.n, self.nz = plan.n, plan.nz
        me = lax.axis_index("fsdp")
        self.me = me
        self.core = lax.rem(me, 2)
        self.x = lax.rem(me // 2, 2)
        self.y = lax.rem(me // 4, 2)
        self.z = me // 8
        self.sib = me + 1 - 2 * self.core
        self.xn = me + 2 - 4 * self.x
        self.yn = me + 4 - 8 * self.y

    def block(self, column, z, other_core=False):
        x = self.x if column in (0, 2) else 1 - self.x
        y = self.y if column in (0, 1) else 1 - self.y
        core = 1 - self.core if other_core else self.core
        return ((z * 2 + y) * 2 + x) * 2 + core

    def level(self, distance, fn):
        if distance == 0:
            fn(self.z)
            return
        pl.when(self.z >= distance)(lambda: fn(self.z - distance))
        pl.when(self.z + distance < self.nz)(lambda: fn(self.z + distance))

    def onward(self, z, fn):
        pl.when((z <= self.z) & (self.z < self.nz - 1))(lambda: fn(self.me + 8))
        pl.when((z >= self.z) & (self.z > 0))(lambda: fn(self.me - 8))

    def bits(self):
        out = []
        bit = 1
        while bit < self.n:
            out.append(self.me + bit - 2 * bit * lax.rem(self.me // bit, 2))
            bit *= 2
        return out

    def greet(self, hubs):
        sem = pltpu.get_barrier_semaphore()

        def tell(partner):
            pl.semaphore_signal(sem, inc=1, device_id=(partner,), device_id_type=MESH)

        fixed = self.bits()
        for partner in fixed:
            tell(partner)
        z_odd = lax.rem(self.z, 2)
        far_z = (self.z > 0) & (self.z < self.nz - 1)
        far = (self.me > 0) & (self.me < self.n - 1)
        pl.when(far_z)(lambda: tell(self.me - 8 + 16 * z_odd))
        pl.when(far)(lambda: tell(self.me - 1 + 2 * self.core))
        count = len(fixed) + far_z.astype(jnp.int32) + far.astype(jnp.int32)
        for hub in hubs:
            pl.when(self.me != hub)(lambda: tell(hub))
            count = count + jnp.where(self.me == hub, self.n - 1, 0)
        return lambda: pl.semaphore_wait(sem, count)


class Wire:
    def __init__(self, send, recv):
        self.send, self.recv = send, recv
        self.sent = []

    def copy(self, src, dst, number, partner):
        return pltpu.make_async_remote_copy(
            src_ref=src,
            dst_ref=dst,
            send_sem=self.send.at[number],
            recv_sem=self.recv.at[number],
            device_id=(partner,),
            device_id_type=MESH,
        )


def add_over_all(place, wire, base, own, held):
    partners = place.bits()

    def send(s):
        wire.copy(own.at[s], held.at[s], base + s, partners[s]).start()

    def take(s):
        wire.copy(own.at[s], held.at[s], base + s, partners[s]).wait()
        own[s + 1] = own[s] + held[s]

    steps = [lambda: send(0)]
    for s in range(len(partners)):

        def step(s=s):
            take(s)
            if s + 1 < len(partners):
                send(s + 1)

        steps.append(step)
    return steps


def gather_count(nz):
    return 17 * nz + 3


class Gather:
    def __init__(self, place, wire, base, ref, top, rows, late, half):
        self.p, self.w, self.ref = place, wire, ref
        nz = place.nz
        self.early = (top, rows - late)
        self.late = (top + rows - late, late)
        self.first = (top, half)
        self.second = (top + half, rows - late - half)
        at = [base]

        def take(count):
            at[0] += count
            return at[0] - count

        self.line, self.xs, self.ys, self.d1, self.d2 = (take(nz) for _ in range(5))
        self.sib, self.late_line, self.late_sib = (take(4 * nz) for _ in range(3))
        self.px, self.py, self.pd = (take(1) for _ in range(3))

    def move(self, column, z, part, number, partner):
        ref = self.ref.at[self.p.block(column, z), pl.ds(*part)]
        return self.w.copy(ref, ref, number, partner)

    def send(self, *args):
        self.move(*args).start()

    def wait(self, column, z, part, number):
        self.move(column, z, part, number, self.p.sib).wait_recv()

    def to_sib(self, column, z):
        self.send(column, z, self.early, self.sib + column * self.p.nz + z, self.p.sib)

    def spread(self, z):
        p = self.p
        p.onward(z, lambda partner: self.send(0, z, self.early, self.line + z, partner))
        self.send(0, z, self.early, self.xs + z, p.xn)
        self.send(0, z, self.early, self.ys + z, p.yn)
        self.to_sib(0, z)

    def spread_late(self, column, z):
        number = column * self.p.nz + z
        self.p.onward(
            z, lambda partner: self.send(column, z, self.late, self.late_line + number, partner)
        )
        self.send(column, z, self.late, self.late_sib + number, self.p.sib)

    def take_line(self, z):
        self.wait(0, z, self.early, self.line + z)
        self.spread(z)

    def take_x(self, z):
        self.wait(1, z, self.early, self.xs + z)
        self.send(1, z, self.first, self.d1 + z, self.p.yn)
        self.to_sib(1, z)

    def take_y(self, z):
        self.wait(2, z, self.early, self.ys + z)
        self.send(2, z, self.second, self.d2 + z, self.p.xn)
        self.to_sib(2, z)

    def take_corner(self, z):
        self.wait(3, z, self.first, self.d1 + z)
        self.wait(3, z, self.second, self.d2 + z)
        self.to_sib(3, z)

    def take_late(self, z):
        for column in range(4):
            self.wait(column, z, self.late, self.late_line + column * self.p.nz + z)
            self.spread_late(column, z)

    def begin(self):
        self.spread(self.p.z)

    def begin_late(self):
        p = self.p
        self.send(0, p.z, self.late, self.px, p.xn)
        self.send(0, p.z, self.late, self.py, p.yn)

    def late_x(self):
        self.wait(1, self.p.z, self.late, self.px)
        self.send(1, self.p.z, self.late, self.pd, self.p.yn)

    def late_y(self):
        self.wait(2, self.p.z, self.late, self.py)

    def late_corner(self):
        self.wait(3, self.p.z, self.late, self.pd)

    def step(self, kind, number):
        p = self.p
        plane, digit = number // 10, number % 10
        starts = (self.begin, self.begin_late, self.late_x, self.late_y, self.late_corner,
                  lambda: self.spread_late(digit, p.z))
        takes = (self.take_line, self.take_x, self.take_y, self.take_corner, self.take_late)
        if kind == FINISH:
            planes = range(plane, plane + digit)
            return lambda: self.finish(planes)
        if kind < len(starts):
            return lambda: pl.when(p.z == plane)(starts[kind])
        take = takes[kind - len(starts)]
        if digit:
            return lambda: pl.when((p.z == plane - digit) | (p.z == plane + digit))(lambda: take(plane))
        return lambda: take(plane)

    def finish(self, planes):
        p, nz = self.p, self.p.nz

        def one(j, carry):
            for column in range(4):
                ref = self.ref.at[p.block(column, j, True)]
                for part, base in ((self.early, self.sib), (self.late, self.late_sib)):
                    r = ref.at[pl.ds(*part)]
                    self.w.copy(r, r, base + column * nz + j, p.sib).wait_recv()
            return carry

        lax.fori_loop(planes[0], planes[-1] + 1, one, 0)

    def drain(self):
        p, nz = self.p, self.p.nz

        def sent(column, z, part, number):
            self.move(column, z, part, number, p.sib).wait_send()

        sent(0, p.z, self.late, self.px)
        sent(0, p.z, self.late, self.py)
        sent(1, p.z, self.late, self.pd)

        def one(z, carry):
            p.onward(z, lambda partner: sent(0, z, self.early, self.line + z))
            sent(0, z, self.early, self.xs + z)
            sent(0, z, self.early, self.ys + z)
            sent(1, z, self.first, self.d1 + z)
            sent(2, z, self.second, self.d2 + z)
            for column in range(4):
                number = column * nz + z
                sent(column, z, self.early, self.sib + number)
                sent(column, z, self.late, self.late_sib + number)
                p.onward(z, lambda partner: sent(column, z, self.late, self.late_line + number))
            return carry

        lax.fori_loop(0, nz, one, 0)


def gather_count(nz):
    return 17 * nz + 3


ORDER = (
    10030, 10000, 10500, 10010, 10510, 10020, 10120, 0, 10130, 10100, 20030, 20000, 20500, 20020, 20100,
    10110, 10200, 10601, 10501, 20130, 10300, 10621, 10631, 10210, 20010, 10230, 10220, 10611, 10502, 20530,
    10520, 10602, 10622, 10612, 10310, 10632, 10531, 10400, 10512, 10320, 10522, 10430, 10533, 10503, 10521,
    20520, 10603, 10420, 10523, 20200, 20120, 10410, 20501, 10513, 10810, 11002, 10511, 10330, 10633, 10820,
    10720, 11011, 10710, 11001, 10800, 20110, 20230, 10700, 10530, 20400, 20631, 11022, 11021, 10532, 20601,
    10730, 10830, 11012, 11003, 20220, 20521, 20602, 20300, 20621, 20503, 20502, 20310, 11031, 20512, 20330,
    10920, 10910, 20611, 20430, 10900, 20320, 11121, 11111, 20210, 20632, 20533, 11101, 20531, 20522, 100,
    20622, 21001, 102, 20532, 11032, 20510, 20603, 101, 103, 200, 10930, 20420, 20523, 20511, 20612, 20633,
    201, 21002, 11033, 11131, 20410, 20513, 21031, 20700, 21021, 20800, 202, 203, 20710, 20810, 20830,
    21011, 20730, 204, 20900, 20820, 21003, 21032, 205, 300, 20720, 21022, 20910, 301, 21012, 20930, 21102,
    400, 20920, 401, 21033, 21122, 402, 403, 500, 501, 502, 503, 600, 700, 30030, 701, 30020, 30230, 30130,
    30633, 800, 30220, 30120, 30622, 801, 802, 30430, 30330, 30320, 803, 30420, 30632, 804, 805, 806, 30533,
    30621, 807, 30000, 30010, 900, 30100, 901, 30200, 30110, 30603, 902, 30631, 30522, 30210, 30612, 30532,
    30300, 1000, 30400, 30410, 1001, 30602, 30310, 1002, 30630, 30503, 1101, 40001, 40002, 30611, 40003,
    30531, 30730, 1003, 30601, 40101, 30620, 30512, 30720, 40203, 30502, 40201, 40103, 40603, 30830, 1004,
    40403, 30521, 40102, 40401, 30610, 30710, 30820, 40301, 30511, 40303, 40202, 1005, 40302, 40402, 30501,
    1102, 50003, 30600, 40503, 60000, 30920, 50103, 30700, 30810, 30930, 30520, 30530, 50002, 50001, 40602,
    40000, 60001, 50203, 50603, 40502, 50102, 50303, 50403, 1200, 30800, 50101, 40100, 50202, 50602, 30510,
    60002, 50000, 50302, 40601, 30910, 50402, 50503, 50100, 30500, 30900, 50201, 40200, 50401, 50601, 50301,
    50200, 40600, 40700, 60003, 50502, 40501, 50600, 50700, 40300, 40400, 1201, 60004, 50400, 50300, 50501,
    40800, 50800, 1202, 1203, 40500, 40900, 60005, 50900, 50500,
)

class Scatter:
    def __init__(self, place, wire, base, terms, columns, top, rows, late, half, room):
        self.p, self.w, self.terms, self.columns = place, wire, terms, columns
        nz = place.nz
        self.whole = (top, rows)
        self.early = (top, rows - late)
        self.late = (top + rows - late, late)
        self.first = (top, half)
        self.second = (top + half, rows - late - half)
        (self.side, self.in_first, self.in_second, self.in_x, self.in_y, self.in_line, self.in_late,
         self.in_plane) = room
        at = [base]

        def take(count):
            at[0] += count
            return at[0] - count

        self.sib = take(4 * nz)
        self.d1, self.d2, self.xs, self.ys = (take(nz) for _ in range(4))
        self.line = take(nz + 1)
        self.late_line = take(4 * (nz + 1))
        self.plane = take(3)

    @staticmethod
    def rooms(nz, columns, top, rows, late, half):
        def room(count, size):
            return pltpu.VMEM((count, size, columns), BF16)

        early = rows - late
        return [
            room(4 * nz, rows), room(nz, half), room(nz, early - half), room(nz, early), room(nz, early),
            room(nz + 1, early), room(4 * (nz + 1), late), room(3, late),
        ]

    def slot(self, column, z):
        return column * self.p.nz + z

    def term(self, column, z, part, other_core=False):
        return self.terms.at[self.p.block(column, z, other_core), pl.ds(*part), pl.ds(*self.columns)]

    def add(self, target, term):
        count = target.shape[0]
        step = count if count <= 48 else next(s for s in (48, 32, 16) if count % s == 0)

        def some(i, carry):
            rs = pl.ds(pl.multiple_of(i * step, 16), step)
            target[rs, :] = target[rs, :] + term[rs, :]
            return carry

        lax.fori_loop(0, count // step, some, 0)

    def got(self, ref, number):
        self.w.copy(ref, ref, number, self.p.sib).wait_recv()
        return ref

    def send_sib(self, z):
        p = self.p
        for column in (3, 1, 2, 0):
            k = self.slot(column, z)
            self.w.copy(self.term(column, z, self.whole, True), self.side.at[k], self.sib + k, p.sib).start()

    def take_sib(self, column, z):
        k = self.slot(column, z)
        self.add(self.term(column, z, self.whole), self.got(self.side.at[k], self.sib + k))

    def corner(self, z):
        p = self.p
        self.take_sib(3, z)
        self.w.copy(self.term(3, z, self.first), self.in_first.at[z], self.d1 + z, p.yn).start()
        self.w.copy(self.term(3, z, self.second), self.in_second.at[z], self.d2 + z, p.xn).start()

    def take_rest(self, z):
        for column in (1, 2, 0):
            self.take_sib(column, z)

    def side_x(self, z):
        p = self.p
        self.add(self.term(1, z, self.first), self.got(self.in_first.at[z], self.d1 + z))
        self.w.copy(self.term(1, z, self.early), self.in_x.at[z], self.xs + z, p.xn).start()

    def side_y(self, z):
        p = self.p
        self.add(self.term(2, z, self.second), self.got(self.in_second.at[z], self.d2 + z))
        self.w.copy(self.term(2, z, self.early), self.in_y.at[z], self.ys + z, p.yn).start()

    def own(self, z):
        ref = self.term(0, z, self.early)
        self.add(ref, self.got(self.in_x.at[z], self.xs + z))
        self.add(ref, self.got(self.in_y.at[z], self.ys + z))
        self.along(z, ref, self.in_line, self.line, 0)

    def own_late(self, z):
        for column in range(4):
            self.along(z, self.term(column, z, self.late), self.in_late, self.late_line,
                       column * (self.p.nz + 1))

    def along(self, z, ref, room, number, at):
        p, nz = self.p, self.p.nz
        below, above = p.z > 0, p.z < nz - 1

        def take(slot):
            self.add(ref, self.got(room.at[at + slot], number + at + slot))

        def send(slot, partner):
            self.w.copy(ref, room.at[at + slot], number + at + slot, partner).start()

        pl.when((z >= p.z) & below)(lambda: take(z))
        pl.when((z < p.z) & above)(lambda: take(z))
        pl.when((z == p.z) & above)(lambda: take(nz))
        pl.when(z > p.z)(lambda: send(z, p.me + 8))
        pl.when(z < p.z)(lambda: send(jnp.where(z == p.z - 1, nz, z), p.me - 8))

    def plane_corner(self):
        p = self.p
        self.w.copy(self.term(3, p.z, self.late), self.in_plane.at[0], self.plane, p.yn).start()

    def plane_sides(self):
        p = self.p
        self.w.copy(self.term(2, p.z, self.late), self.in_plane.at[2], self.plane + 2, p.yn).start()
        ref = self.term(1, p.z, self.late)
        self.add(ref, self.got(self.in_plane.at[0], self.plane))
        self.w.copy(ref, self.in_plane.at[1], self.plane + 1, p.xn).start()

    def plane_own(self):
        ref = self.term(0, self.p.z, self.late)
        self.add(ref, self.got(self.in_plane.at[1], self.plane + 1))
        self.add(ref, self.got(self.in_plane.at[2], self.plane + 2))

    def step(self, kind, number, by_plane):
        p = self.p
        plane, digit = number // 10, number % 10
        takes = (self.send_sib, self.corner, self.take_rest, self.side_x, self.side_y, self.own, self.own_late)
        ends = (self.plane_corner, self.plane_sides, self.plane_own)
        if kind >= len(takes):
            end = ends[kind - len(takes)]
            return (lambda: pl.when(p.z == plane)(end)) if by_plane else end
        take = takes[kind]
        if not by_plane:
            return lambda: p.level(digit, take)
        if take in (self.own, self.own_late):
            return lambda: pl.when((p.z == plane - digit) | (p.z == plane + digit))(lambda: take(plane))
        return lambda: take(plane)

    def drain(self):
        p, nz = self.p, self.p.nz

        def sent(ref, number):
            self.w.copy(ref, ref, number, p.sib).wait_send()

        for i in range(3):
            sent(self.in_plane.at[i], self.plane + i)

        def one(z, carry):
            for column in range(4):
                k = self.slot(column, z)
                sent(self.side.at[k], self.sib + k)
            sent(self.in_first.at[z], self.d1 + z)
            sent(self.in_second.at[z], self.d2 + z)
            sent(self.in_x.at[z], self.xs + z)
            sent(self.in_y.at[z], self.ys + z)

            def lines(slot):
                sent(self.in_line.at[slot], self.line + slot)
                for column in range(4):
                    at = column * (nz + 1) + slot
                    sent(self.in_late.at[at], self.late_line + at)

            pl.when(z > p.z)(lambda: lines(z))
            pl.when(z < p.z)(lambda: lines(jnp.where(z == p.z - 1, nz, z)))
            return carry

        lax.fori_loop(0, nz, one, 0)


def scatter_count(nz):
    return 4 * nz + 4 * nz + nz + 1 + 4 * (nz + 1) + 3


def build_masks(plan, ids_ref, len_ref, key_add, query_one):
    for r in range(plan.rows):
        ids = jnp.broadcast_to(ids_ref[r : r + 1, :], (LANES, SLOTS))
        label = lax.broadcasted_iota(jnp.int32, (LANES, SLOTS), 0)
        place = lax.broadcasted_iota(jnp.int32, (LANES, SLOTS), 1)
        start = jnp.sum((ids < label).astype(F32), axis=1, keepdims=True)
        lengths = len_ref[r]
        lengths = lengths[0:1, :] + lengths[1:2, :]
        live = jnp.zeros((LANES, SLOTS), jnp.int32)
        for j in range(PAIRS):
            live = jnp.where(label == j, lengths[:, j : j + 1], live)
        same = ids == label
        ok = same & (place.astype(F32) - start < live.astype(F32))
        rs = pl.ds(r * SLOTS, SLOTS)
        key_add[rs, :] = jnp.where(ok | (label >= PAIRS), 0.0, -1e30).T.astype(BF16)
        query_one[rs, :] = same.astype(F32).T.astype(BF16)


def split_heads(v):
    lane = lax.broadcasted_iota(jnp.int32, v.shape, 1)
    zero = jnp.zeros_like(v)
    return jnp.concatenate(
        [jnp.where(lane < HEAD_DIM, v, zero), jnp.where(lane < HEAD_DIM, zero, v)], axis=0
    )


def join_heads(v):
    lane = lax.broadcasted_iota(jnp.int32, (SLOTS, LANES), 1)
    return jnp.where(lane < HEAD_DIM, v[:SLOTS], v[SLOTS:])


def head_pair(i, rows):
    r, p = lax.rem(i, rows), i // rows
    return (
        pl.ds(pl.multiple_of(r * SLOTS, 16), SLOTS),
        pl.ds(pl.multiple_of(p * LANES, LANES), LANES),
    )


def scores_of(rs, cs, qkv, key_add, query_one):
    q, k, one = qkv[0, rs, cs], qkv[1, rs, cs], query_one[rs, :]
    q_side = jnp.concatenate([split_heads(q), jnp.concatenate([one, one], axis=0)], axis=1)
    k_side = jnp.concatenate([k, key_add[rs, :]], axis=1)
    return dot_nt(k_side, q_side), q, k


def attend(i, rows, qkv, key_add, query_one, context, log_totals):
    rs, cs = head_pair(i, rows)
    scores, _, _ = scores_of(rs, cs, qkv, key_add, query_one)
    top = jnp.max(scores, axis=0, keepdims=True)
    raised = jnp.exp(scores - top)
    total = jnp.sum(raised, axis=0, keepdims=True)
    shares = (raised * (1.0 / total)).astype(BF16)
    log_totals[i] = top + jnp.log(total)
    context[rs, cs] = join_heads(dot_tn(shares, qkv[2, rs, cs])).astype(BF16)


def attend_back(i, rows, qkv, key_add, query_one, log_totals, grad_context, grad_qkv):
    rs, cs = head_pair(i, rows)
    scores, q, k = scores_of(rs, cs, qkv, key_add, query_one)
    shares = jnp.exp(scores - log_totals[i])
    grad = split_heads(grad_context[rs, cs])
    grad_shares = dot_nt(qkv[2, rs, cs], grad)
    inner = jnp.sum(shares * grad_shares, axis=0, keepdims=True)
    grad_scores = (shares * (grad_shares - inner)).astype(BF16)
    grad_qkv[2, rs, cs] = dot_nn(shares.astype(BF16), grad).astype(BF16)
    grad_qkv[1, rs, cs] = dot_nn(grad_scores, split_heads(q)).astype(BF16)
    grad_qkv[0, rs, cs] = (join_heads(dot_tn(grad_scores, k)) * 0.125).astype(BF16)


def run_beside(count, body, steps):
    def turn(i, carry):
        body(i)
        for j, some in enumerate(steps):
            if some:

                @pl.when(i == j)
                def _(some=some):
                    for step in some:
                        step()

        return carry

    lax.fori_loop(0, count, turn, 0)


def after(code, steps):
    at = ORDER.index(code) + 1
    out = []
    while at < len(ORDER) and ORDER[at] >= 10000:
        out.append(steps[ORDER[at]])
        at += 1
    return out


def beside(kind, count, steps):
    return [after(kind + i, steps) for i in range(count)]


def run(steps):
    for step in steps:
        step()


def joint_weight(plan, ref, b):
    jr = plan.joint_rows
    return ref[0 : plan.joint_src, b * jr : (b + 1) * jr, :].reshape(D, D)


def out_weight(plan, ref):
    return ref[plan.joint_src : plan.n].reshape(D, D)


def in_weight(plan, ref, c):
    ir = plan.in_rows
    return ref[0 : plan.in_src, pl.ds(pl.multiple_of(c * ir, 16), ir), :].reshape(D, D)


def back_weight(plan, ref, c):
    return ref[back_blocks(plan, c)].reshape(D, D)


def back_blocks(plan, c):
    per = (plan.n - plan.in_src) // 4
    return pl.ds(plan.in_src + c * per, per)


def row_slots(r):
    return pl.ds(pl.multiple_of(r * SLOTS, 16), SLOTS)


def token_tiles(plan, size, fn):
    def one(t, carry):
        fn(pl.ds(pl.multiple_of(t * size, 16), size))
        return carry

    lax.fori_loop(0, plan.tokens // size, one, 0)


def gelu_with_slope(h):
    cdf = 0.5 * (1.0 + lax.erf(h * 0.7071067811865476))
    return h * cdf, cdf + h * jnp.exp(-0.5 * h * h) * 0.3989422804014327


def norm_parts(v):
    centred = v - row_mean(v)
    rstd = lax.rsqrt(row_mean(centred * centred) + NORM_EPS)
    return centred * rstd, rstd


def norm_back(grad, xhat, rstd):
    return rstd * (grad - row_mean(grad) - xhat * row_mean(grad * xhat))


def layer_kernel(plan, *refs):
    (x_in, ids, lens, shard_a, shard_f, out_grad_in) = refs[:6]
    (layer_out, in_grad, attn_grad, ffn_grad, bias_grad, params_far, qkv_far, context_far) = refs[6:14]
    (x, weights, active, slope, terms_f, norm_b, grad_hidden, grad_low, acc, xhat, rstd_first, log_totals, key_add,
     query_one, vec, vec_own, vec_held, joined_a, joined_f, halo_a, halo_f, end_a, end_f, vec_a, vec_b, got_a, got_b,
     got, out_a, out_f, send, recv, vec_send, vec_recv, local) = refs[14:49]
    room_f, room_1, room_2 = refs[49:57], refs[57:65], refs[65:73]
    n, nz, rows = plan.n, plan.nz, plan.rows
    place = Place(plan)
    me = place.me
    wire = Wire(send, recv)
    tail_a, tail_f = plan.tail_a, plan.tail_f
    hub_a, hub_b = plan.at_attn_vec[0], plan.at_bias_in[0]
    va, vf, gap = 5 * D // LANES, 3 * D // LANES, plan.gap
    bits = n.bit_length() - 1
    ra, half = plan.rows_a, D // 2
    jr, ir = plan.joint_rows, plan.in_rows
    per = (n - plan.in_src) // 4
    turns = HEADS // 2 * rows
    cols = [pl.ds(u * LANES, LANES) for u in range(6)]
    params = terms_f.at[:, 0:ra, :]
    qkv, context = slope.at[0:3], slope.at[3]
    out_grad = grad_hidden
    params_back = weights.at[:, 0:ra, :]
    terms_a = weights.at[:, ra : 2 * ra, :]
    qkv_back, context_back = active.at[0:3], active.at[3]
    grad_qkv, grad_context = slope.at[0:3], slope.at[3]

    base = [0]

    def numbers(count):
        base[0] += count
        return base[0] - count

    halo_in, halo_out = numbers(2), numbers(2)
    gather_a = Gather(place, wire, numbers(gather_count(nz)), params, *plan.part_a)
    gather_f = Gather(place, wire, numbers(gather_count(nz)), weights, *plan.part_f)
    scatter_f = Scatter(place, wire, numbers(scatter_count(nz)), terms_f, (0, D), *plan.part_f, room_f)
    scatter_1 = Scatter(place, wire, numbers(scatter_count(nz)), weights, (0, half), ra, *plan.part_a[1:], room_1)
    scatter_2 = Scatter(place, wire, numbers(scatter_count(nz)), weights, (half, half), ra, *plan.part_a[1:], room_2)
    vec_steps = add_over_all(place, wire, numbers(bits), vec_own, vec_held)
    movers = (None, gather_a, gather_f, scatter_f, scatter_1, scatter_2)
    steps = {}
    for code in ORDER:
        family, kind, number = code // 10000, code // 100 % 100, code % 100
        if family == 6:
            steps[code] = vec_steps[number]
        elif family:
            by_plane = () if family < 3 else (family == 3,)
            steps[code] = movers[family].step(kind, number, *by_plane)

    copies = {}

    def copy_here(name, src, dst):
        copies[name] = pltpu.make_async_copy(src, dst, local.at[len(copies)])

    copy_here("x", x_in, x)
    copy_here("out_grad", out_grad_in, out_grad)
    copy_here("params", params, params_far)
    copy_here("qkv", qkv, qkv_far)
    copy_here("context", context, context_far)
    copy_here("result", out_grad, layer_out)
    copy_here("params_back", params_far, params_back)
    copy_here("qkv_back", qkv_far, qkv_back)
    copy_here("context_back", context_far, context_back)
    copy_here("in_grad", acc, in_grad)
    entered = place.greet((hub_a, hub_b))
    copies["x"].start()
    copies["out_grad"].start()

    joined_a[tail_a : tail_a + plan.unit_a, :] = shard_a[...].astype(F32)
    joined_f[tail_f : tail_f + plan.unit_f, :] = shard_f[...].astype(F32)
    end_a[...] = joined_a[plan.unit_a : plan.unit_a + tail_a, :]
    end_f[...] = joined_f[plan.unit_f : plan.unit_f + tail_f, :]
    at = tail_a + plan.at_attn_vec[1]
    vec_a[0:va, :] = joined_a[at : at + va, :].astype(BF16)
    at = tail_f + plan.at_ffn_vec[1]
    vec_a[va : va + vf, :] = joined_f[at : at + vf, :].astype(BF16)
    at = tail_f + plan.at_bias_in[1]
    vec_b[...] = jnp.zeros_like(vec_b)
    vec_b[0:gap, :] = joined_f[at : at + gap, :].astype(BF16)
    entered()

    @pl.when(me < n - 1)
    def _():
        wire.copy(end_a, halo_a, halo_in, me + 1).start()
        wire.copy(end_f, halo_f, halo_in + 1, me + 1).start()

    def vec_copy(src, dst, which, partner):
        return pltpu.make_async_remote_copy(
            src_ref=src, dst_ref=dst, send_sem=vec_send.at[partner], recv_sem=vec_recv.at[which],
            device_id=(partner,), device_id_type=MESH,
        )

    def to_all(src, dst, which, fn):
        @pl.when(me == (hub_a, hub_b)[which])
        def _():
            def one(j, carry):
                pl.when(j != me)(lambda: fn(vec_copy(src, dst, which, j)))
                return carry

            lax.fori_loop(0, n, one, 0)

    to_all(vec_a, got_a, 0, lambda copy: copy.start())
    to_all(vec_b, got_b, 1, lambda copy: copy.start())

    @pl.when(me > 0)
    def _():
        wire.copy(end_a, halo_a, halo_in, me - 1).wait_recv()
        joined_a[0:tail_a, :] = halo_a[...]

    start = tail_a - plan.shift_a(me)
    mine = params.at[me]

    @pl.when(me < plan.joint_src)
    def _():
        for b in range(3):
            for u in range(6):
                mine[b * jr : (b + 1) * jr, cols[u]] = joined_a[
                    pl.ds(start + 6 * b + u, jr, stride=18), :
                ].astype(BF16)

    @pl.when(me >= plan.joint_src)
    def _():
        for u in range(6):
            mine[:, cols[u]] = joined_a[pl.ds(start + u, ra, stride=6), :].astype(BF16)

    run([steps[code] for code in ORDER[: ORDER.index(RELAY)]])

    @pl.when(me > 0)
    def _():
        wire.copy(end_f, halo_f, halo_in + 1, me - 1).wait_recv()
        joined_f[0:tail_f, :] = halo_f[...]

    start_f = tail_f - plan.shift_f(me)
    mine_f = weights.at[me]

    @pl.when(me < plan.in_src)
    def _():
        for c in range(4):
            for u in range(6):
                mine_f[c * ir : (c + 1) * ir, cols[u]] = joined_f[
                    pl.ds(start_f + 6 * c + u, ir, stride=24), :
                ].astype(BF16)

    @pl.when(me >= plan.in_src)
    def _():
        for u in range(6):
            mine_f[:, cols[u]] = joined_f[pl.ds(start_f + u, plan.rows_f, stride=6), :].astype(BF16)

    run(after(RELAY, steps))
    build_masks(plan, ids, lens, key_add, query_one)

    @pl.when(me == hub_a)
    def _():
        got_a[...] = vec_a[...]

    @pl.when(me == hub_b)
    def _():
        got_b[...] = vec_b[...]

    @pl.when(me != hub_a)
    def _():
        vec_copy(vec_a, got_a, 0, hub_a).wait_recv()

    @pl.when(me != hub_b)
    def _():
        vec_copy(vec_b, got_b, 1, hub_b).wait_recv()

    got[0 : va + vf, :] = got_a[0 : va + vf, :].astype(F32)
    got[va + vf : va + vf + gap, :] = got_b[0:gap, :].astype(F32)
    vec[...] = jnp.zeros_like(vec)
    for u in range(6):
        vec[0:5, cols[u]] = got[pl.ds(u, 5, stride=6), :]
        vec[9:12, cols[u]] = got[pl.ds(va + u, 3, stride=6), :]
        vec[5:9, cols[u]] = got[pl.ds(va + vf + u, 4, stride=6), :]

    copies["x"].wait()
    scale = jnp.asarray(HEAD_DIM ** (-0.5), BF16)
    held = D // (nz - 1)
    partial = (acc, xhat)
    project = [code for code in ORDER if PROJECT <= code < PROJECT + nz]
    for j, code in enumerate(project):
        z = code - PROJECT
        if z < nz - 1:
            blocks, columns = pl.ds(8 * z, 8), pl.ds(held * z, held)
            for b in range(2):
                now = dot_nn(x[:, columns], params[blocks, b * jr : (b + 1) * jr, :].reshape(held, D))
                if j > 0:
                    now = now + partial[b][...]
                if j < nz - 2:
                    partial[b][...] = now
                elif b == 0:
                    qkv[0] = (now + vec[0:1, :]).astype(BF16) * scale
                else:
                    qkv[1] = now.astype(BF16)
        else:
            qkv[2] = (dot_nn(x[...], joint_weight(plan, params, 2)) + vec[1:2, :]).astype(BF16)
        run(after(code, steps))
    copies["qkv"].start()
    pairs = turns // rows

    def attend_pair(i):
        for r in range(rows):
            attend(i * rows + r, rows, qkv, key_add, query_one, context, log_totals)

    run_beside(pairs, attend_pair, beside(ATTEND, pairs, steps))
    copies["params"].start()
    copies["context"].start()
    gain_first, shift_first, bias_back = vec[3:4, :], vec[4:5, :], vec[9:10, :]
    gain_second, shift_second = vec[10:11, :], vec[11:12, :]

    def norm(t):
        rs = row_slots(t)
        v = x[rs, :].astype(F32) + (dot_nn(context[rs, :], out_weight(plan, params)) + vec[2:3, :])
        now, rstd = norm_parts(v)
        xhat[rs, :] = now
        rstd_first[rs, :] = jnp.broadcast_to(rstd, (rstd.shape[0], LANES))
        v = now * gain_first + shift_first
        norm_b[rs, :] = v.astype(BF16)
        acc[rs, :] = v + bias_back

    run_beside(rows, norm, beside(NORM, rows, steps))

    copies["qkv"].wait()
    copies["context"].wait()

    def up(c):
        hidden = dot_nn(norm_b[...], in_weight(plan, weights, c)) + vec[pl.ds(5 + c, 1), :]
        value, incline = gelu_with_slope(hidden)
        active[c] = value.astype(BF16)
        slope[c] = incline.astype(BF16)

    run_beside(4, up, beside(UP, 4, steps))

    def down(c):
        acc[...] += dot_nn(active[c], back_weight(plan, weights, c))

    run_beside(4, down, beside(DOWN, 4, steps))
    copies["out_grad"].wait()
    grads = vec_own.at[0]
    grads[...] = jnp.zeros(grads.shape, F32)

    def turn(rs):
        now, rstd = norm_parts(acc[rs, :])
        cot = out_grad[rs, :].astype(F32)
        out_grad[rs, :] = (now * gain_second + shift_second).astype(BF16)
        grads[10:11, :] += col_sum(cot * now)
        grads[11:12, :] += col_sum(cot)
        grad = norm_back(cot * gain_second, now, rstd)
        acc[rs, :] = grad
        low = grad.astype(BF16)
        grad_low[rs, :] = low
        grads[9:10, :] += col_sum(low.astype(F32))

    token_tiles(plan, SLOTS, turn)
    copies["result"].start()
    copies["params"].wait()
    gather_a.drain()

    back_order = (2, 3, 0, 1)
    for c in back_order:
        terms_f[back_blocks(plan, c)] = (
            dot_tn(active[c], grad_low[...]).astype(BF16).reshape(per, plan.rows_f, D)
        )
        if c == back_order[1]:
            run(after(BACK_WEIGHT, steps))
    run(after(BACK_WEIGHT + 1, steps))
    copies["context_back"].start()
    copies["qkv_back"].start()
    copies["result"].wait()

    def hidden_back(i):
        c = i // 2

        @pl.when(i == 2 * c)
        def _():
            into_hidden = dot_nt(grad_low[...], back_weight(plan, weights, c))
            grad = (slope[c].astype(F32) * into_hidden).astype(BF16)
            grad_hidden[...] = grad
            grads[pl.ds(5 + c, 1), :] += col_sum(grad.astype(F32))
            acc[...] += dot_nt(grad, in_weight(plan, weights, c))

        @pl.when(i != 2 * c)
        def _():
            in_rows = pl.ds(pl.multiple_of(c * ir, 16), ir)
            terms_f[0 : plan.in_src, in_rows, :] = (
                dot_tn(norm_b[...], grad_hidden[...]).astype(BF16).reshape(plan.in_src, ir, D)
            )

    run_beside(8, hidden_back, beside(HIDDEN, 8, steps))
    gather_f.drain()
    copies["params_back"].start()

    def leave(rs):
        grad, now = acc[rs, :], xhat[rs, :]
        grads[3:4, :] += col_sum(grad * now)
        grads[4:5, :] += col_sum(grad)
        grad = norm_back(grad * gain_first, now, rstd_first[rs, 0:1])
        acc[rs, :] = grad
        grad = grad.astype(BF16)
        grad_low[rs, :] = grad
        grads[2:3, :] += col_sum(grad.astype(F32))

    token_tiles(plan, SLOTS, leave)
    run(after(LEAVE, steps))
    copies["params_back"].wait()

    def into_context(rs):
        grad_context[rs, :] = dot_nt(grad_low[rs, :], out_weight(plan, params_back)).astype(BF16)

    token_tiles(plan, SLOTS, into_context)
    run(after(LEAVE + 1, steps))
    copies["context_back"].wait()
    terms_a[plan.joint_src : n] = (
        dot_tn(context_back[...], grad_low[...]).astype(BF16).reshape(n - plan.joint_src, ra, D)
    )
    copies["qkv_back"].wait()
    run(after(LEAVE + 2, steps))

    def joint_terms(first):
        for b in range(3):
            terms_a[0 : plan.joint_src, b * jr : (b + 1) * jr, first : first + half] = (
                dot_tn(x[...], grad_qkv[b, :, first : first + half]).astype(BF16).reshape(plan.joint_src, jr, half)
            )

    def back_pair(i):
        for r in range(rows):
            attend_back(i * rows + r, rows, qkv_back, key_add, query_one, log_totals, grad_context, grad_qkv)

    beside_back = beside(ATTEND_BACK, pairs, steps)
    beside_back[pairs // 2 - 1] += [lambda: joint_terms(0)] + after(JOINT + 1, steps)
    run_beside(pairs, back_pair, beside_back)
    joint_terms(half)
    grads[0:1, :] = col_sum(grad_qkv[0].astype(F32))
    grads[1:2, :] = col_sum(grad_qkv[2].astype(F32))
    run(after(JOINT + 2, steps))

    def input_grad(rs):
        now = acc[rs, :]
        for b in range(3):
            now = now + dot_nt(grad_qkv[b, rs, :], joint_weight(plan, params_back, b))
        acc[rs, :] = now

    size = plan.tokens // 4
    for j in range(4):
        input_grad(pl.ds(j * size, size))
        if j == 3:
            copies["in_grad"].start()
        run(after(INPUT_GRAD + j, steps))

    summed = vec_own.at[bits]
    total_f, total_a = terms_f.at[me], terms_a.at[me]

    @pl.when(me < plan.in_src)
    def _():
        for c in range(4):
            for u in range(6):
                joined_f[pl.ds(6 * c + u, ir, stride=24), :] = total_f[c * ir : (c + 1) * ir, cols[u]].astype(F32)

    @pl.when(me >= plan.in_src)
    def _():
        for u in range(6):
            joined_f[pl.ds(u, plan.rows_f, stride=6), :] = total_f[:, cols[u]].astype(F32)

    @pl.when(me < plan.joint_src)
    def _():
        for b in range(3):
            for u in range(6):
                joined_a[pl.ds(6 * b + u, jr, stride=18), :] = total_a[b * jr : (b + 1) * jr, cols[u]].astype(F32)

    @pl.when(me >= plan.joint_src)
    def _():
        for u in range(6):
            joined_a[pl.ds(u, ra, stride=6), :] = total_a[:, cols[u]].astype(F32)

    head_a, head_f = joined_a.at[0:tail_a], joined_f.at[0:tail_f]

    @pl.when(me > 0)
    def _():
        wire.copy(head_f, out_f, halo_out + 1, me - 1).start()
        wire.copy(head_a, out_a, halo_out, me - 1).start()

    rest_a = pl.ds(plan.block_a, tail_a)
    rest_f = pl.ds(plan.block_f, tail_f)

    @pl.when(me < n - 1)
    def _():
        wire.copy(head_f, out_f, halo_out + 1, me + 1).wait_recv()
        wire.copy(head_a, out_a, halo_out, me + 1).wait_recv()
        joined_f[rest_f, :] = out_f[...]
        joined_a[rest_a, :] = out_a[...]

    @pl.when(me == hub_b)
    def _():
        for u in range(6):
            joined_f[pl.ds(plan.block_f + u, 4, stride=6), :] = summed[5:9, cols[u]]
        joined_f[plan.block_f + gap : plan.block_f + tail_f, :] = out_f[0 : tail_f - gap, :]

    @pl.when(me == n - 1)
    def _():
        joined_f[rest_f, :] = jnp.zeros((tail_f, LANES), F32)
        joined_a[rest_a, :] = jnp.zeros((tail_a, LANES), F32)
        for u in range(6):
            joined_f[pl.ds(plan.block_f + u, 3, stride=6), :] = summed[9:12, cols[u]]
            joined_a[pl.ds(plan.block_a + u, 5, stride=6), :] = summed[0:5, cols[u]]

    ffn_grad[...] = joined_f[pl.ds(plan.shift_f(me), plan.unit_f), :]
    attn_grad[...] = joined_a[pl.ds(plan.shift_a(me), plan.unit_a), :]
    for u in range(6):
        bias_grad[u : u + 1, :] = summed[2:3, cols[u]]
    copies["in_grad"].wait()
    for mover in (scatter_f, scatter_1, scatter_2):
        mover.drain()
    to_all(vec_a, got_a, 0, lambda copy: copy.wait_send())
    to_all(vec_b, got_b, 1, lambda copy: copy.wait_send())

    @pl.when(me < n - 1)
    def _():
        wire.copy(end_a, halo_a, halo_in, me + 1).wait_send()
        wire.copy(end_f, halo_f, halo_in + 1, me + 1).wait_send()

    @pl.when(me > 0)
    def _():
        wire.copy(head_f, out_f, halo_out + 1, me - 1).wait_send()
        wire.copy(head_a, out_a, halo_out, me - 1).wait_send()


def hand_over(*arrays):
    def kernel(*refs):
        for j in range(len(arrays)):
            refs[len(arrays) + j][...] = refs[j][...]

    parts = 4
    specs = []
    for array in arrays:
        count, width = array.shape
        if count % (16 * parts) == 0:
            specs.append(pl.BlockSpec((count // parts, width), lambda i: (i, 0)))
        else:
            specs.append(pl.BlockSpec((count, width), lambda i: (0, 0)))
    return pl.pallas_call(
        kernel,
        name="hand_over",
        grid=(parts,),
        out_shape=[jax.ShapeDtypeStruct(array.shape, array.dtype) for array in arrays],
        in_specs=specs,
        out_specs=specs,
    )(*arrays)


def fused_body(plan, layer_in, pair_ids, pair_lengths, attn_shard, ffn_shard, out_grad):
    n, t, nz = plan.n, plan.tokens, plan.nz
    shape = jax.ShapeDtypeStruct
    bits = n.bit_length() - 1
    turns = HEADS // 2 * plan.rows
    sems = 4 + bits + 2 * gather_count(nz) + 3 * scatter_count(nz)
    low, full = pltpu.VMEM((t, D), BF16), pltpu.VMEM((t, D), F32)
    blocks = pltpu.VMEM((n, plan.rows_f, D), BF16)
    wide = pltpu.VMEM((4, t, D), BF16)
    side = pltpu.VMEM((t, LANES), BF16)
    vmem, far = pl.BlockSpec(memory_space=pltpu.VMEM), pl.BlockSpec(memory_space=pl.ANY)

    def units(count):
        return pltpu.VMEM((count, LANES), F32)

    def low_units(count):
        return pltpu.VMEM((count, LANES), BF16)

    layer_out, in_grad, attn_grad, ffn_grad, bias_grad = pl.pallas_call(
        functools.partial(layer_kernel, plan),
        name="layer",
        out_shape=[
            shape((t, D), BF16),
            shape((t, D), F32),
            shape((plan.unit_a, LANES), F32),
            shape((plan.unit_f, LANES), F32),
            shape((D // LANES, LANES), F32),
            shape((n, plan.rows_a, D), BF16),
            shape((3, t, D), BF16),
            shape((t, D), BF16),
        ],
        in_specs=[far] + [vmem] * 4 + [far],
        out_specs=[far] * 2 + [vmem] * 3 + [far] * 3,
        scratch_shapes=[
            low, blocks, wide, wide, blocks, low, low, low, full, full,
            pltpu.VMEM((t, LANES), F32),
            pltpu.VMEM((turns, 1, 2 * SLOTS), F32),
            side, side,
            pltpu.VMEM((16, D), F32),
            pltpu.VMEM((bits + 1, 16, D), F32),
            pltpu.VMEM((bits, 16, D), F32),
            units(plan.tail_a + -(-plan.unit_a // 8) * 8 + 8),
            units(plan.tail_f + -(-plan.unit_f // 8) * 8 + 8),
            units(plan.tail_a), units(plan.tail_f), units(plan.tail_a), units(plan.tail_f),
            low_units(48), low_units(32), low_units(48), low_units(32),
            units(80), units(plan.tail_a), units(plan.tail_f),
            pltpu.SemaphoreType.DMA((sems,)),
            pltpu.SemaphoreType.DMA((sems,)),
            pltpu.SemaphoreType.DMA((n,)),
            pltpu.SemaphoreType.DMA((2,)),
            pltpu.SemaphoreType.DMA((12,)),
        ]
        + Scatter.rooms(nz, D, *plan.part_f)
        + Scatter.rooms(nz, D // 2, *plan.part_a)
        + Scatter.rooms(nz, D // 2, *plan.part_a),
        compiler_params=pltpu.CompilerParams(
            collective_id=0, has_side_effects=True, vmem_limit_bytes=VMEM_LIMIT
        ),
    )(
        layer_in.reshape(t, D),
        pair_ids,
        jnp.swapaxes(pair_lengths, 1, 2),
        attn_shard.reshape(plan.unit_a, LANES),
        ffn_shard.reshape(plan.unit_f, LANES),
        out_grad.reshape(t, D),
    )[:5]
    layer_out, in_grad, attn_grad, ffn_grad, bias_grad = hand_over(layer_out, in_grad, attn_grad, ffn_grad, bias_grad)
    return (
        layer_out.reshape(layer_in.shape),
        in_grad.reshape(layer_in.shape),
        attn_grad.reshape(-1),
        ffn_grad.reshape(-1),
        bias_grad.reshape(-1),
    )


def unpack_attention(flattened):
    offset = 3 * D * D
    weight_joint = flattened[:offset].reshape(D, 3 * D)
    weight_out = flattened[offset : offset + D * D].reshape(D, D)
    offset = offset + D * D
    vectors = flattened[offset : offset + 5 * D].reshape(5, D)
    return (weight_joint, weight_out, vectors[0], vectors[1], vectors[2], vectors[3], vectors[4])


def unpack_feedforward(flattened):
    offset = D * FF
    weight_in = flattened[:offset].reshape(D, FF)
    bias_in = flattened[offset : offset + FF]
    offset = offset + FF
    weight_back = flattened[offset : offset + FF * D].reshape(FF, D)
    offset = offset + FF * D
    vectors = flattened[offset : offset + 3 * D].reshape(3, D)
    return (weight_in, bias_in, weight_back, vectors[0], vectors[1], vectors[2])


def layer_norm(values, gain_vec, shift_vec):
    row_mean = jnp.mean(values, axis=-1, keepdims=True)
    centred = values - row_mean
    row_var = jnp.mean(centred * centred, axis=-1, keepdims=True)
    return centred * lax.rsqrt(row_var + NORM_EPS) * gain_vec + shift_vec


def exact_gelu(values):
    return jax.nn.gelu(values, approximate=False)


def key_mask(pair_ids, pair_lengths):
    labels = jnp.arange(PAIRS, dtype=jnp.int32)
    member = pair_ids[:, :, None] == labels[None, None, :]
    starts = jnp.sum((pair_ids[:, :, None] < labels[None, None, :]).astype(jnp.int32), axis=1)
    live_len = pair_lengths[:, :, 0] + pair_lengths[:, :, 1]
    slot_start = jnp.sum(jnp.where(member, starts[:, None, :], 0), axis=-1)
    slot_len = jnp.sum(jnp.where(member, live_len[:, None, :], 0), axis=-1)
    places = jnp.arange(pair_ids.shape[1], dtype=jnp.int32)[None, :]
    is_live = places - slot_start < slot_len
    return (pair_ids[:, :, None] == pair_ids[:, None, :]) & is_live[:, None, :]


def contract_rows(one_side, other_side):
    return lax.dot_general(
        one_side, other_side, (((0,), (0,)), ((), ())), preferred_element_type=jnp.float32
    )


def contract_cols(one_side, other_side):
    return lax.dot_general(
        one_side, other_side, (((1,), (1,)), ((), ())), preferred_element_type=jnp.float32
    )


def attend_forward(queries, key_rows, value_rows, key_ok, score_scale):

    def head_block(block_index):
        head_start = block_index * 4
        query_b = lax.dynamic_slice_in_dim(queries, head_start, 4, 2)
        key_b = lax.dynamic_slice_in_dim(key_rows, head_start, 4, 2)
        value_b = lax.dynamic_slice_in_dim(value_rows, head_start, 4, 2)
        scores = (
            jnp.einsum("rqhd,rkhd->rhqk", query_b, key_b, preferred_element_type=jnp.float32)
            * score_scale
        )
        scores = jnp.where(key_ok[:, None], scores, -1e30)
        row_max = jnp.max(scores, axis=-1, keepdims=True)
        raised = jnp.exp(scores - row_max)
        totals = jnp.sum(raised, axis=-1, keepdims=True)
        shares = (raised / totals).astype(jnp.bfloat16)
        context = jnp.einsum("rhqk,rkhd->rqhd", shares, value_b, preferred_element_type=jnp.float32)
        return (context, row_max + jnp.log(totals))

    return lax.map(head_block, jnp.arange(HEADS // 4))


def attend_backward(queries, key_rows, value_rows, grad_context, log_totals, key_ok, score_scale):

    def head_block(operands):
        block_index, log_total = operands
        head_start = block_index * 4
        query_b = lax.dynamic_slice_in_dim(queries, head_start, 4, 2)
        key_b = lax.dynamic_slice_in_dim(key_rows, head_start, 4, 2)
        value_b = lax.dynamic_slice_in_dim(value_rows, head_start, 4, 2)
        grad_block = lax.dynamic_slice_in_dim(grad_context, head_start, 4, 2)
        scores = (
            jnp.einsum("rqhd,rkhd->rhqk", query_b, key_b, preferred_element_type=jnp.float32)
            * score_scale
        )
        shares = jnp.where(key_ok[:, None], jnp.exp(scores - log_total), 0.0)
        grad_shares = jnp.einsum(
            "rqhd,rkhd->rhqk", grad_block, value_b, preferred_element_type=jnp.float32
        )
        inner_sum = jnp.sum(shares * grad_shares, axis=-1, keepdims=True)
        grad_scores = (shares * (grad_shares - inner_sum)).astype(jnp.bfloat16)
        grad_query = (
            jnp.einsum("rhqk,rkhd->rqhd", grad_scores, key_b, preferred_element_type=jnp.float32)
            * score_scale
        )
        grad_key = (
            jnp.einsum("rhqk,rqhd->rkhd", grad_scores, query_b, preferred_element_type=jnp.float32)
            * score_scale
        )
        grad_value = jnp.einsum(
            "rhqk,rqhd->rkhd",
            shares.astype(jnp.bfloat16),
            grad_block,
            preferred_element_type=jnp.float32,
        )
        return (grad_query, grad_key, grad_value)

    gradients = lax.map(head_block, (jnp.arange(HEADS // 4), log_totals))
    return [jnp.moveaxis(piece, 0, 2).reshape(-1, D) for piece in gradients]


def plain_body(layer_in, pair_ids, pair_lengths, attn_shard, ffn_shard, out_grad):
    row_count = layer_in.shape[0]
    tokens = row_count * SLOTS
    score_scale = HEAD_DIM ** (-0.5)
    key_ok = key_mask(pair_ids, pair_lengths)
    att_whole = lax.all_gather(attn_shard, "fsdp", axis=0, tiled=True)
    weight_joint, weight_out, bias_query, bias_value, bias_out, gain_first, shift_first = (
        unpack_attention(att_whole)
    )
    inputs = layer_in.reshape(tokens, D)
    bias_joint = jnp.concatenate([bias_query, jnp.zeros_like(bias_query), bias_value]).astype(
        jnp.float32
    )
    projected = (
        jnp.dot(inputs, weight_joint, preferred_element_type=jnp.float32) + bias_joint
    ).astype(jnp.bfloat16)
    projected = projected.reshape(row_count, SLOTS, 3, HEADS, HEAD_DIM)
    queries = projected[:, :, 0]
    key_rows = projected[:, :, 1]
    value_rows = projected[:, :, 2]
    contexts, log_totals = attend_forward(queries, key_rows, value_rows, key_ok, score_scale)
    context = jnp.moveaxis(contexts, 0, 2).reshape(tokens, D).astype(jnp.bfloat16)
    attn_out = jnp.dot(context, weight_out, preferred_element_type=jnp.float32) + bias_out.astype(
        jnp.float32
    )
    norm_first, first_pull = jax.vjp(
        layer_norm,
        inputs.astype(jnp.float32) + attn_out,
        gain_first.astype(jnp.float32),
        shift_first.astype(jnp.float32),
    )
    norm_first_b = norm_first.astype(jnp.bfloat16)
    feed_whole = lax.all_gather(ffn_shard, "fsdp", axis=0, tiled=True)
    weight_in, bias_in, weight_back, bias_back, gain_second, shift_second = unpack_feedforward(
        feed_whole
    )
    hidden = jnp.dot(norm_first_b, weight_in, preferred_element_type=jnp.float32) + bias_in.astype(
        jnp.float32
    )
    active, gelu_pull = jax.vjp(exact_gelu, hidden)
    active_b = active.astype(jnp.bfloat16)
    ffn_out = jnp.dot(active_b, weight_back, preferred_element_type=jnp.float32) + bias_back.astype(
        jnp.float32
    )
    result, second_pull = jax.vjp(
        layer_norm,
        norm_first + ffn_out,
        gain_second.astype(jnp.float32),
        shift_second.astype(jnp.float32),
    )
    layer_out = result.astype(jnp.bfloat16).reshape(row_count, SLOTS, D)
    feed_back = lax.all_gather(ffn_shard, "fsdp", axis=0, tiled=True)
    weight_in, bias_in, weight_back, bias_back, gain_second, shift_second = unpack_feedforward(
        feed_back
    )
    cotangent = out_grad.reshape(tokens, D).astype(jnp.float32)
    grad_sum_second, grad_gain_second, grad_shift_second = second_pull(cotangent)
    grad_ffn = grad_sum_second.astype(jnp.bfloat16)
    grad_bias_back = jnp.sum(grad_ffn.astype(jnp.float32), axis=0)
    grad_weight_back = contract_rows(active_b, grad_ffn)
    (grad_hidden,) = gelu_pull(contract_cols(grad_ffn, weight_back))
    grad_hidden = grad_hidden.astype(jnp.bfloat16)
    grad_bias_in = jnp.sum(grad_hidden.astype(jnp.float32), axis=0)
    grad_weight_in = contract_rows(norm_first_b, grad_hidden)
    grad_norm_first = grad_sum_second + contract_cols(grad_hidden, weight_in)
    grad_sum_first, grad_gain_first, grad_shift_first = first_pull(grad_norm_first)
    feed_pad = feed_back.shape[0] - (2 * D * FF + FF + 3 * D)
    feed_full = jnp.concatenate(
        [
            grad_weight_in.reshape(-1),
            grad_bias_in,
            grad_weight_back.reshape(-1),
            grad_bias_back,
            grad_gain_second,
            grad_shift_second,
            jnp.zeros((feed_pad,), jnp.float32),
        ]
    )
    ffn_grad = lax.psum_scatter(feed_full, "fsdp", scatter_dimension=0, tiled=True)
    att_back = lax.all_gather(attn_shard, "fsdp", axis=0, tiled=True)
    weight_joint, weight_out, bias_query, bias_value, bias_out, gain_first, shift_first = (
        unpack_attention(att_back)
    )
    grad_attn = grad_sum_first.astype(jnp.bfloat16)
    grad_bias_out = jnp.sum(grad_attn.astype(jnp.float32), axis=0)
    out_bias_grad = lax.psum(grad_bias_out, "fsdp")
    grad_weight_out = contract_rows(context, grad_attn)
    grad_context = (
        contract_cols(grad_attn, weight_out)
        .astype(jnp.bfloat16)
        .reshape(row_count, SLOTS, HEADS, HEAD_DIM)
    )
    grad_query, grad_key, grad_value = attend_backward(
        queries, key_rows, value_rows, grad_context, log_totals, key_ok, score_scale
    )
    grad_projected = jnp.concatenate([grad_query, grad_key, grad_value], axis=-1).astype(
        jnp.bfloat16
    )
    column_sums = jnp.sum(grad_projected.astype(jnp.float32), axis=0)
    grad_weight_joint = contract_rows(inputs, grad_projected)
    in_grad = grad_sum_first + contract_cols(grad_projected, weight_joint)
    att_pad = att_back.shape[0] - (4 * D * D + 5 * D)
    attn_full = jnp.concatenate(
        [
            grad_weight_joint.reshape(-1),
            grad_weight_out.reshape(-1),
            column_sums[:D],
            column_sums[2 * D :],
            grad_bias_out,
            grad_gain_first,
            grad_shift_first,
            jnp.zeros((att_pad,), jnp.float32),
        ]
    )
    attn_grad = lax.psum_scatter(attn_full, "fsdp", scatter_dimension=0, tiled=True)
    return (layer_out, in_grad.reshape(row_count, SLOTS, D), attn_grad, ffn_grad, out_bias_grad)


def body(layer_in, pair_ids, pair_lengths, attn_shard, ffn_shard, out_grad, devices):
    plan = Plan(devices, attn_shard.shape[0], ffn_shard.shape[0], layer_in.shape[0])
    run = functools.partial(fused_body, plan) if plan.fits() else plain_body
    return run(layer_in, pair_ids, pair_lengths, attn_shard, ffn_shard, out_grad)


def solution(mesh):
    placed = (
        P("fsdp", None, None),
        P("fsdp", None),
        P("fsdp", None, None),
        P("fsdp"),
        P("fsdp"),
        P("fsdp", None, None),
    )
    return jax.shard_map(
        functools.partial(body, devices=mesh.shape["fsdp"]),
        mesh=mesh,
        in_specs=placed,
        out_specs=(P("fsdp", None, None), P("fsdp", None, None), P("fsdp"), P("fsdp"), P()),
        check_vma=False,
    )
```

```python
import functools

import jax
import jax.numpy as jnp
from jax import lax
from jax.experimental import pallas as pl
from jax.experimental.pallas import tpu as pltpu
from jax.sharding import PartitionSpec as P

D = 768
HEADS = 12
HEAD_DIM = 64
FF = 3072
SLOTS = 416
PAIRS = 3
LANES = 128
NORM_EPS = 1e-12
F32 = jnp.float32
BF16 = jnp.bfloat16
MESH = pl.DeviceIdType.MESH
VMEM_LIMIT = 62 << 20
FINISH = 11
RELAY, PROJECT, ATTEND, NORM, UP, DOWN, TURN, BACK_WEIGHT, HIDDEN, LEAVE, ATTEND_BACK, JOINT, INPUT_GRAD = range(
    0, 1300, 100
)


def dot_nn(a, b):
    return lax.dot_general(a, b, (((1,), (0,)), ((), ())), preferred_element_type=F32)


def dot_nt(a, b):
    return lax.dot_general(a, b, (((1,), (1,)), ((), ())), preferred_element_type=F32)


def dot_tn(a, b):
    return lax.dot_general(a, b, (((0,), (0,)), ((), ())), preferred_element_type=F32)


def row_mean(v):
    return jnp.sum(v, axis=1, keepdims=True) * (1.0 / D)


def col_sum(v):
    return jnp.sum(v, axis=0, keepdims=True)


class Plan:
    def __init__(self, n, attn_shard_len, ffn_shard_len, row_count):
        self.n = n
        self.nz = n // 8
        self.rows = row_count
        self.tokens = row_count * SLOTS
        self.unit_a = attn_shard_len // LANES
        self.unit_f = ffn_shard_len // LANES
        self.block_a = 4 * D * D // LANES // n
        self.block_f = 2 * D * FF // LANES // n
        self.rows_a = 4 * D // n
        self.rows_f = 2 * FF // n
        self.joint_rows = self.rows_a // 3
        self.joint_src = 3 * n // 4
        self.in_rows = self.rows_f // 4
        self.in_src = n // 2
        self.part_a = (0, self.rows_a, 16, 32)
        self.part_f = (0, self.rows_f, 48, 64)
        self.gap = FF // LANES
        self.at_attn_vec = divmod(4 * D * D // LANES, self.unit_a)
        self.at_bias_in = divmod(D * FF // LANES, self.unit_f)
        self.at_ffn_vec = divmod(2 * D * FF // LANES + self.gap, self.unit_f)

    def shift_a(self, me):
        return me * (self.unit_a - self.block_a)

    def shift_f(self, me):
        return me * (self.unit_f - self.block_f) - jnp.where(me >= self.in_src, self.gap, 0)

    def fits(self):
        n = self.n
        if self.nz != 4 or n % 8 or self.rows_a % 48 or self.rows_f % 64:
            return False
        last_a = (n - 1) * (self.unit_a - self.block_a)
        step_f = self.unit_f - self.block_f
        last_f = max((self.in_src - 1) * step_f, (n - 1) * step_f - self.gap)
        first_f = self.in_src * step_f - self.gap
        self.tail_a = -(-(last_a + 1) // 8) * 8
        self.tail_f = -(-(last_f + 2) // 8) * 8
        vec_a, vec_f = 5 * D // LANES, 3 * D // LANES
        return (
            step_f >= 0
            and self.unit_a >= self.block_a
            and first_f >= 0
            and self.tail_a <= self.block_a
            and self.tail_f <= self.block_f
            and self.at_attn_vec[0] == n - 1
            and self.at_ffn_vec[0] == n - 1
            and self.at_bias_in[0] == self.in_src - 1
            and self.unit_a - self.at_attn_vec[1] <= self.tail_a
            and self.unit_f - self.at_ffn_vec[1] <= self.tail_f
            and self.at_attn_vec[1] + vec_a <= self.unit_a
            and self.at_ffn_vec[1] + vec_f <= self.unit_f
            and self.at_bias_in[1] + self.gap <= self.unit_f
            and self.at_bias_in[1] == self.block_f - (self.in_src - 1) * step_f
        )


class Place:
    def __init__(self, plan):
        self.n, self.nz = plan.n, plan.nz
        me = lax.axis_index("fsdp")
        self.me = me
        self.core = lax.rem(me, 2)
        self.x = lax.rem(me // 2, 2)
        self.y = lax.rem(me // 4, 2)
        self.z = me // 8
        self.sib = me + 1 - 2 * self.core
        self.xn = me + 2 - 4 * self.x
        self.yn = me + 4 - 8 * self.y

    def block(self, column, z, other_core=False):
        x = self.x if column in (0, 2) else 1 - self.x
        y = self.y if column in (0, 1) else 1 - self.y
        core = 1 - self.core if other_core else self.core
        return ((z * 2 + y) * 2 + x) * 2 + core

    def level(self, distance, fn):
        if distance == 0:
            fn(self.z)
            return
        pl.when(self.z >= distance)(lambda: fn(self.z - distance))
        pl.when(self.z + distance < self.nz)(lambda: fn(self.z + distance))

    def onward(self, z, fn):
        pl.when((z <= self.z) & (self.z < self.nz - 1))(lambda: fn(self.me + 8))
        pl.when((z >= self.z) & (self.z > 0))(lambda: fn(self.me - 8))

    def bits(self):
        out = []
        bit = 1
        while bit < self.n:
            out.append(self.me + bit - 2 * bit * lax.rem(self.me // bit, 2))
            bit *= 2
        return out

    def greet(self, hubs):
        sem = pltpu.get_barrier_semaphore()

        def tell(partner):
            pl.semaphore_signal(sem, inc=1, device_id=(partner,), device_id_type=MESH)

        fixed = self.bits()
        for partner in fixed:
            tell(partner)
        z_odd = lax.rem(self.z, 2)
        far_z = (self.z > 0) & (self.z < self.nz - 1)
        far = (self.me > 0) & (self.me < self.n - 1)
        pl.when(far_z)(lambda: tell(self.me - 8 + 16 * z_odd))
        pl.when(far)(lambda: tell(self.me - 1 + 2 * self.core))
        count = len(fixed) + far_z.astype(jnp.int32) + far.astype(jnp.int32)
        for hub in hubs:
            pl.when(self.me != hub)(lambda: tell(hub))
            count = count + jnp.where(self.me == hub, self.n - 1, 0)
        return lambda: pl.semaphore_wait(sem, count)


class Wire:
    def __init__(self, send, recv):
        self.send, self.recv = send, recv
        self.sent = []

    def copy(self, src, dst, number, partner):
        return pltpu.make_async_remote_copy(
            src_ref=src,
            dst_ref=dst,
            send_sem=self.send.at[number],
            recv_sem=self.recv.at[number],
            device_id=(partner,),
            device_id_type=MESH,
        )


def add_over_all(place, wire, base, own, held):
    partners = place.bits()

    def send(s):
        wire.copy(own.at[s], held.at[s], base + s, partners[s]).start()

    def take(s):
        wire.copy(own.at[s], held.at[s], base + s, partners[s]).wait()
        own[s + 1] = own[s] + held[s]

    steps = [lambda: send(0)]
    for s in range(len(partners)):

        def step(s=s):
            take(s)
            if s + 1 < len(partners):
                send(s + 1)

        steps.append(step)
    return steps


def gather_count(nz):
    return 17 * nz + 3


class Gather:
    def __init__(self, place, wire, base, ref, top, rows, late, half):
        self.p, self.w, self.ref = place, wire, ref
        nz = place.nz
        self.early = (top, rows - late)
        self.late = (top + rows - late, late)
        self.first = (top, half)
        self.second = (top + half, rows - late - half)
        at = [base]

        def take(count):
            at[0] += count
            return at[0] - count

        self.line, self.xs, self.ys, self.d1, self.d2 = (take(nz) for _ in range(5))
        self.sib, self.late_line, self.late_sib = (take(4 * nz) for _ in range(3))
        self.px, self.py, self.pd = (take(1) for _ in range(3))

    def move(self, column, z, part, number, partner):
        ref = self.ref.at[self.p.block(column, z), pl.ds(*part)]
        return self.w.copy(ref, ref, number, partner)

    def send(self, *args):
        self.move(*args).start()

    def wait(self, column, z, part, number):
        self.move(column, z, part, number, self.p.sib).wait_recv()

    def to_sib(self, column, z):
        self.send(column, z, self.early, self.sib + column * self.p.nz + z, self.p.sib)

    def spread(self, z):
        p = self.p
        p.onward(z, lambda partner: self.send(0, z, self.early, self.line + z, partner))
        self.send(0, z, self.early, self.xs + z, p.xn)
        self.send(0, z, self.early, self.ys + z, p.yn)
        self.to_sib(0, z)

    def spread_late(self, column, z):
        number = column * self.p.nz + z
        self.p.onward(
            z, lambda partner: self.send(column, z, self.late, self.late_line + number, partner)
        )
        self.send(column, z, self.late, self.late_sib + number, self.p.sib)

    def take_line(self, z):
        self.wait(0, z, self.early, self.line + z)
        self.spread(z)

    def take_x(self, z):
        self.wait(1, z, self.early, self.xs + z)
        self.send(1, z, self.first, self.d1 + z, self.p.yn)
        self.to_sib(1, z)

    def take_y(self, z):
        self.wait(2, z, self.early, self.ys + z)
        self.send(2, z, self.second, self.d2 + z, self.p.xn)
        self.to_sib(2, z)

    def take_corner(self, z):
        self.wait(3, z, self.first, self.d1 + z)
        self.wait(3, z, self.second, self.d2 + z)
        self.to_sib(3, z)

    def take_late(self, z):
        for column in range(4):
            self.wait(column, z, self.late, self.late_line + column * self.p.nz + z)
            self.spread_late(column, z)

    def begin(self):
        self.spread(self.p.z)

    def begin_late(self):
        p = self.p
        self.send(0, p.z, self.late, self.px, p.xn)
        self.send(0, p.z, self.late, self.py, p.yn)

    def late_x(self):
        self.wait(1, self.p.z, self.late, self.px)
        self.send(1, self.p.z, self.late, self.pd, self.p.yn)

    def late_y(self):
        self.wait(2, self.p.z, self.late, self.py)

    def late_corner(self):
        self.wait(3, self.p.z, self.late, self.pd)

    def step(self, kind, number):
        p = self.p
        plane, digit = number // 10, number % 10
        starts = (self.begin, self.begin_late, self.late_x, self.late_y, self.late_corner,
                  lambda: self.spread_late(digit, p.z))
        takes = (self.take_line, self.take_x, self.take_y, self.take_corner, self.take_late)
        if kind == FINISH:
            planes = range(plane, plane + digit)
            return lambda: self.finish(planes)
        if kind < len(starts):
            return lambda: pl.when(p.z == plane)(starts[kind])
        take = takes[kind - len(starts)]
        if digit:
            return lambda: pl.when((p.z == plane - digit) | (p.z == plane + digit))(lambda: take(plane))
        return lambda: take(plane)

    def finish(self, planes):
        p, nz = self.p, self.p.nz

        def one(j, carry):
            for column in range(4):
                ref = self.ref.at[p.block(column, j, True)]
                for part, base in ((self.early, self.sib), (self.late, self.late_sib)):
                    r = ref.at[pl.ds(*part)]
                    self.w.copy(r, r, base + column * nz + j, p.sib).wait_recv()
            return carry

        lax.fori_loop(planes[0], planes[-1] + 1, one, 0)

    def drain(self):
        p, nz = self.p, self.p.nz

        def sent(column, z, part, number):
            self.move(column, z, part, number, p.sib).wait_send()

        sent(0, p.z, self.late, self.px)
        sent(0, p.z, self.late, self.py)
        sent(1, p.z, self.late, self.pd)

        def one(z, carry):
            p.onward(z, lambda partner: sent(0, z, self.early, self.line + z))
            sent(0, z, self.early, self.xs + z)
            sent(0, z, self.early, self.ys + z)
            sent(1, z, self.first, self.d1 + z)
            sent(2, z, self.second, self.d2 + z)
            for column in range(4):
                number = column * nz + z
                sent(column, z, self.early, self.sib + number)
                sent(column, z, self.late, self.late_sib + number)
                p.onward(z, lambda partner: sent(column, z, self.late, self.late_line + number))
            return carry

        lax.fori_loop(0, nz, one, 0)


def gather_count(nz):
    return 17 * nz + 3


ORDER = (
    10030, 10000, 10500, 10010, 10510, 10020, 10120, 0, 10130, 10100, 20030, 20000, 20500, 20020, 20100,
    10110, 10200, 10601, 10501, 20130, 10300, 10621, 10631, 10210, 20010, 10230, 10220, 10611, 10502, 20530,
    10520, 10602, 10622, 10612, 10310, 10632, 10531, 10400, 10512, 10320, 10522, 10430, 10533, 10503, 10521,
    20520, 10603, 10420, 10523, 20200, 20120, 10410, 20501, 10513, 10810, 11002, 10511, 10330, 10633, 10820,
    10720, 11011, 10710, 11001, 10800, 20110, 20230, 10700, 10530, 20400, 20631, 11022, 11021, 10532, 20601,
    10730, 10830, 11012, 11003, 20220, 20521, 20602, 20300, 20621, 20503, 20502, 20310, 11031, 20512, 20330,
    10920, 10910, 20611, 20430, 10900, 20320, 11121, 11111, 20210, 20632, 20533, 11101, 20531, 20522, 100,
    20622, 21001, 102, 20532, 11032, 20510, 20603, 101, 103, 200, 10930, 20420, 20523, 20511, 20612, 20633,
    201, 21002, 11033, 11131, 20410, 20513, 21031, 20700, 21021, 20800, 202, 203, 20710, 20810, 20830,
    21011, 20730, 204, 20900, 20820, 21003, 21032, 205, 300, 20720, 21022, 20910, 301, 21012, 20930, 21102,
    400, 20920, 401, 21033, 21122, 402, 403, 500, 501, 502, 503, 600, 700, 30030, 701, 30020, 30230, 30130,
    30633, 800, 30220, 30120, 30622, 801, 802, 30430, 30330, 30320, 803, 30420, 30632, 804, 805, 806, 30533,
    30621, 807, 30000, 30010, 900, 30100, 901, 30200, 30110, 30603, 902, 30631, 30522, 30210, 30612, 30532,
    30300, 1000, 30400, 30410, 1001, 30602, 30310, 1002, 30630, 30503, 1101, 40001, 40002, 30611, 40003,
    30531, 30730, 1003, 30601, 40101, 30620, 30512, 30720, 40203, 30502, 40201, 40103, 40603, 30830, 1004,
    40403, 30521, 40102, 40401, 30610, 30710, 30820, 40301, 30511, 40303, 40202, 1005, 40302, 40402, 30501,
    1102, 50003, 30600, 40503, 60000, 30920, 50103, 30700, 30810, 30930, 30520, 30530, 50002, 50001, 40602,
    40000, 60001, 50203, 50603, 40502, 50102, 50303, 50403, 1200, 30800, 50101, 40100, 50202, 50602, 30510,
    60002, 50000, 50302, 40601, 30910, 50402, 50503, 50100, 30500, 30900, 50201, 40200, 50401, 50601, 50301,
    50200, 40600, 40700, 60003, 50502, 40501, 50600, 50700, 40300, 40400, 1201, 60004, 50400, 50300, 50501,
    40800, 50800, 1202, 1203, 40500, 40900, 60005, 50900, 50500,
)

class Scatter:
    def __init__(self, place, wire, base, terms, columns, top, rows, late, half, room):
        self.p, self.w, self.terms, self.columns = place, wire, terms, columns
        nz = place.nz
        self.whole = (top, rows)
        self.early = (top, rows - late)
        self.late = (top + rows - late, late)
        self.first = (top, half)
        self.second = (top + half, rows - late - half)
        (self.side, self.in_first, self.in_second, self.in_x, self.in_y, self.in_line, self.in_late,
         self.in_plane) = room
        at = [base]

        def take(count):
            at[0] += count
            return at[0] - count

        self.sib = take(4 * nz)
        self.d1, self.d2, self.xs, self.ys = (take(nz) for _ in range(4))
        self.line = take(nz + 1)
        self.late_line = take(4 * (nz + 1))
        self.plane = take(3)

    @staticmethod
    def rooms(nz, columns, top, rows, late, half):
        def room(count, size):
            return pltpu.VMEM((count, size, columns), BF16)

        early = rows - late
        return [
            room(4 * nz, rows), room(nz, half), room(nz, early - half), room(nz, early), room(nz, early),
            room(nz + 1, early), room(4 * (nz + 1), late), room(3, late),
        ]

    def slot(self, column, z):
        return column * self.p.nz + z

    def term(self, column, z, part, other_core=False):
        return self.terms.at[self.p.block(column, z, other_core), pl.ds(*part), pl.ds(*self.columns)]

    def add(self, target, term):
        count = target.shape[0]
        step = count if count <= 48 else next(s for s in (48, 32, 16) if count % s == 0)

        def some(i, carry):
            rs = pl.ds(pl.multiple_of(i * step, 16), step)
            target[rs, :] = target[rs, :] + term[rs, :]
            return carry

        lax.fori_loop(0, count // step, some, 0)

    def got(self, ref, number):
        self.w.copy(ref, ref, number, self.p.sib).wait_recv()
        return ref

    def send_sib(self, z):
        p = self.p
        for column in (3, 1, 2, 0):
            k = self.slot(column, z)
            self.w.copy(self.term(column, z, self.whole, True), self.side.at[k], self.sib + k, p.sib).start()

    def take_sib(self, column, z):
        k = self.slot(column, z)
        self.add(self.term(column, z, self.whole), self.got(self.side.at[k], self.sib + k))

    def corner(self, z):
        p = self.p
        self.take_sib(3, z)
        self.w.copy(self.term(3, z, self.first), self.in_first.at[z], self.d1 + z, p.yn).start()
        self.w.copy(self.term(3, z, self.second), self.in_second.at[z], self.d2 + z, p.xn).start()

    def take_rest(self, z):
        for column in (1, 2, 0):
            self.take_sib(column, z)

    def side_x(self, z):
        p = self.p
        self.add(self.term(1, z, self.first), self.got(self.in_first.at[z], self.d1 + z))
        self.w.copy(self.term(1, z, self.early), self.in_x.at[z], self.xs + z, p.xn).start()

    def side_y(self, z):
        p = self.p
        self.add(self.term(2, z, self.second), self.got(self.in_second.at[z], self.d2 + z))
        self.w.copy(self.term(2, z, self.early), self.in_y.at[z], self.ys + z, p.yn).start()

    def own(self, z):
        ref = self.term(0, z, self.early)
        self.add(ref, self.got(self.in_x.at[z], self.xs + z))
        self.add(ref, self.got(self.in_y.at[z], self.ys + z))
        self.along(z, ref, self.in_line, self.line, 0)

    def own_late(self, z):
        for column in range(4):
            self.along(z, self.term(column, z, self.late), self.in_late, self.late_line,
                       column * (self.p.nz + 1))

    def along(self, z, ref, room, number, at):
        p, nz = self.p, self.p.nz
        below, above = p.z > 0, p.z < nz - 1

        def take(slot):
            self.add(ref, self.got(room.at[at + slot], number + at + slot))

        def send(slot, partner):
            self.w.copy(ref, room.at[at + slot], number + at + slot, partner).start()

        pl.when((z >= p.z) & below)(lambda: take(z))
        pl.when((z < p.z) & above)(lambda: take(z))
        pl.when((z == p.z) & above)(lambda: take(nz))
        pl.when(z > p.z)(lambda: send(z, p.me + 8))
        pl.when(z < p.z)(lambda: send(jnp.where(z == p.z - 1, nz, z), p.me - 8))

    def plane_corner(self):
        p = self.p
        self.w.copy(self.term(3, p.z, self.late), self.in_plane.at[0], self.plane, p.yn).start()

    def plane_sides(self):
        p = self.p
        self.w.copy(self.term(2, p.z, self.late), self.in_plane.at[2], self.plane + 2, p.yn).start()
        ref = self.term(1, p.z, self.late)
        self.add(ref, self.got(self.in_plane.at[0], self.plane))
        self.w.copy(ref, self.in_plane.at[1], self.plane + 1, p.xn).start()

    def plane_own(self):
        ref = self.term(0, self.p.z, self.late)
        self.add(ref, self.got(self.in_plane.at[1], self.plane + 1))
        self.add(ref, self.got(self.in_plane.at[2], self.plane + 2))

    def step(self, kind, number, by_plane):
        p = self.p
        plane, digit = number // 10, number % 10
        takes = (self.send_sib, self.corner, self.take_rest, self.side_x, self.side_y, self.own, self.own_late)
        ends = (self.plane_corner, self.plane_sides, self.plane_own)
        if kind >= len(takes):
            end = ends[kind - len(takes)]
            return (lambda: pl.when(p.z == plane)(end)) if by_plane else end
        take = takes[kind]
        if not by_plane:
            return lambda: p.level(digit, take)
        if take in (self.own, self.own_late):
            return lambda: pl.when((p.z == plane - digit) | (p.z == plane + digit))(lambda: take(plane))
        return lambda: take(plane)

    def drain(self):
        p, nz = self.p, self.p.nz

        def sent(ref, number):
            self.w.copy(ref, ref, number, p.sib).wait_send()

        for i in range(3):
            sent(self.in_plane.at[i], self.plane + i)

        def one(z, carry):
            for column in range(4):
                k = self.slot(column, z)
                sent(self.side.at[k], self.sib + k)
            sent(self.in_first.at[z], self.d1 + z)
            sent(self.in_second.at[z], self.d2 + z)
            sent(self.in_x.at[z], self.xs + z)
            sent(self.in_y.at[z], self.ys + z)

            def lines(slot):
                sent(self.in_line.at[slot], self.line + slot)
                for column in range(4):
                    at = column * (nz + 1) + slot
                    sent(self.in_late.at[at], self.late_line + at)

            pl.when(z > p.z)(lambda: lines(z))
            pl.when(z < p.z)(lambda: lines(jnp.where(z == p.z - 1, nz, z)))
            return carry

        lax.fori_loop(0, nz, one, 0)


def scatter_count(nz):
    return 4 * nz + 4 * nz + nz + 1 + 4 * (nz + 1) + 3


def build_masks(plan, ids_ref, len_ref, key_add, query_one):
    for r in range(plan.rows):
        ids = jnp.broadcast_to(ids_ref[r : r + 1, :], (LANES, SLOTS))
        label = lax.broadcasted_iota(jnp.int32, (LANES, SLOTS), 0)
        place = lax.broadcasted_iota(jnp.int32, (LANES, SLOTS), 1)
        start = jnp.sum((ids < label).astype(F32), axis=1, keepdims=True)
        lengths = len_ref[r]
        lengths = lengths[0:1, :] + lengths[1:2, :]
        live = jnp.zeros((LANES, SLOTS), jnp.int32)
        for j in range(PAIRS):
            live = jnp.where(label == j, lengths[:, j : j + 1], live)
        same = ids == label
        ok = same & (place.astype(F32) - start < live.astype(F32))
        rs = pl.ds(r * SLOTS, SLOTS)
        key_add[rs, :] = jnp.where(ok | (label >= PAIRS), 0.0, -1e30).T.astype(BF16)
        query_one[rs, :] = same.astype(F32).T.astype(BF16)


def split_heads(v):
    lane = lax.broadcasted_iota(jnp.int32, v.shape, 1)
    zero = jnp.zeros_like(v)
    return jnp.concatenate(
        [jnp.where(lane < HEAD_DIM, v, zero), jnp.where(lane < HEAD_DIM, zero, v)], axis=0
    )


def join_heads(v):
    lane = lax.broadcasted_iota(jnp.int32, (SLOTS, LANES), 1)
    return jnp.where(lane < HEAD_DIM, v[:SLOTS], v[SLOTS:])


def head_pair(i, rows):
    r, p = lax.rem(i, rows), i // rows
    return (
        pl.ds(pl.multiple_of(r * SLOTS, 16), SLOTS),
        pl.ds(pl.multiple_of(p * LANES, LANES), LANES),
    )


def scores_of(rs, cs, qkv, key_add, query_one):
    q, k, one = qkv[0, rs, cs], qkv[1, rs, cs], query_one[rs, :]
    q_side = jnp.concatenate([split_heads(q), jnp.concatenate([one, one], axis=0)], axis=1)
    k_side = jnp.concatenate([k, key_add[rs, :]], axis=1)
    return dot_nt(k_side, q_side), q, k


def attend(i, rows, qkv, key_add, query_one, context, log_totals):
    rs, cs = head_pair(i, rows)
    scores, _, _ = scores_of(rs, cs, qkv, key_add, query_one)
    top = jnp.max(scores, axis=0, keepdims=True)
    raised = jnp.exp(scores - top)
    total = jnp.sum(raised, axis=0, keepdims=True)
    shares = (raised * (1.0 / total)).astype(BF16)
    log_totals[i] = top + jnp.log(total)
    turned = dot_tn(qkv[2, rs, cs], shares)
    row = lax.broadcasted_iota(jnp.int32, (LANES, SLOTS), 0)
    context[rs, cs] = jnp.where(row < HEAD_DIM, turned[:, :SLOTS], turned[:, SLOTS:]).T.astype(BF16)


def attend_back(i, rows, qkv, key_add, query_one, log_totals, grad_context, grad_qkv):
    rs, cs = head_pair(i, rows)
    scores, q, k = scores_of(rs, cs, qkv, key_add, query_one)
    shares = jnp.exp(scores - log_totals[i])
    grad = split_heads(grad_context[rs, cs])
    grad_shares = dot_nt(qkv[2, rs, cs], grad)
    inner = jnp.sum(shares * grad_shares, axis=0, keepdims=True)
    grad_scores = (shares * (grad_shares - inner)).astype(BF16)
    grad_qkv[2, rs, cs] = dot_nn(shares.astype(BF16), grad).astype(BF16)
    grad_qkv[1, rs, cs] = dot_nn(grad_scores, split_heads(q)).astype(BF16)
    grad_qkv[0, rs, cs] = (join_heads(dot_tn(grad_scores, k)) * 0.125).astype(BF16)


def run_beside(count, body, steps):
    def turn(i, carry):
        body(i)
        for j, some in enumerate(steps):
            if some:

                @pl.when(i == j)
                def _(some=some):
                    for step in some:
                        step()

        return carry

    lax.fori_loop(0, count, turn, 0)


def after(code, steps):
    at = ORDER.index(code) + 1
    out = []
    while at < len(ORDER) and ORDER[at] >= 10000:
        out.append(steps[ORDER[at]])
        at += 1
    return out


def beside(kind, count, steps):
    return [after(kind + i, steps) for i in range(count)]


def run(steps):
    for step in steps:
        step()


def joint_weight(plan, ref, b):
    jr = plan.joint_rows
    return ref[0 : plan.joint_src, b * jr : (b + 1) * jr, :].reshape(D, D)


def out_weight(plan, ref):
    return ref[plan.joint_src : plan.n].reshape(D, D)


def in_weight(plan, ref, c):
    ir = plan.in_rows
    return ref[0 : plan.in_src, pl.ds(pl.multiple_of(c * ir, 16), ir), :].reshape(D, D)


def back_weight(plan, ref, c):
    return ref[back_blocks(plan, c)].reshape(D, D)


def back_blocks(plan, c):
    per = (plan.n - plan.in_src) // 4
    return pl.ds(plan.in_src + c * per, per)


def row_slots(r):
    return pl.ds(pl.multiple_of(r * SLOTS, 16), SLOTS)


def token_tiles(plan, size, fn):
    def one(t, carry):
        fn(pl.ds(pl.multiple_of(t * size, 16), size))
        return carry

    lax.fori_loop(0, plan.tokens // size, one, 0)


def gelu_with_slope(h):
    cdf = 0.5 * (1.0 + lax.erf(h * 0.7071067811865476))
    return h * cdf, cdf + h * jnp.exp(-0.5 * h * h) * 0.3989422804014327


def norm_parts(v):
    centred = v - row_mean(v)
    rstd = lax.rsqrt(row_mean(centred * centred) + NORM_EPS)
    return centred * rstd, rstd


def norm_back(grad, xhat, rstd):
    return rstd * (grad - row_mean(grad) - xhat * row_mean(grad * xhat))


def layer_kernel(plan, *refs):
    (x_in, ids, lens, shard_a, shard_f, out_grad_in) = refs[:6]
    (layer_out, in_grad, attn_grad, ffn_grad, bias_grad, params_far, qkv_far, context_far) = refs[6:14]
    (x, weights, active, slope, terms_f, norm_b, grad_hidden, grad_low, acc, xhat, rstd_first, log_totals, key_add,
     query_one, vec, vec_own, vec_held, joined_a, joined_f, halo_a, halo_f, end_a, end_f, vec_a, vec_b, got_a, got_b,
     got, out_a, out_f, send, recv, vec_send, vec_recv, local) = refs[14:49]
    room_f, room_1, room_2 = refs[49:57], refs[57:65], refs[65:73]
    n, nz, rows = plan.n, plan.nz, plan.rows
    place = Place(plan)
    me = place.me
    wire = Wire(send, recv)
    tail_a, tail_f = plan.tail_a, plan.tail_f
    hub_a, hub_b = plan.at_attn_vec[0], plan.at_bias_in[0]
    va, vf, gap = 5 * D // LANES, 3 * D // LANES, plan.gap
    bits = n.bit_length() - 1
    ra, half = plan.rows_a, D // 2
    jr, ir = plan.joint_rows, plan.in_rows
    per = (n - plan.in_src) // 4
    turns = HEADS // 2 * rows
    cols = [pl.ds(u * LANES, LANES) for u in range(6)]
    params = terms_f.at[:, 0:ra, :]
    qkv, context = slope.at[0:3], slope.at[3]
    out_grad = grad_hidden
    params_back = weights.at[:, 0:ra, :]
    terms_a = weights.at[:, ra : 2 * ra, :]
    qkv_back, context_back = active.at[0:3], active.at[3]
    grad_qkv, grad_context = slope.at[0:3], slope.at[3]

    base = [0]

    def numbers(count):
        base[0] += count
        return base[0] - count

    halo_in, halo_out = numbers(2), numbers(2)
    gather_a = Gather(place, wire, numbers(gather_count(nz)), params, *plan.part_a)
    gather_f = Gather(place, wire, numbers(gather_count(nz)), weights, *plan.part_f)
    scatter_f = Scatter(place, wire, numbers(scatter_count(nz)), terms_f, (0, D), *plan.part_f, room_f)
    scatter_1 = Scatter(place, wire, numbers(scatter_count(nz)), weights, (0, half), ra, *plan.part_a[1:], room_1)
    scatter_2 = Scatter(place, wire, numbers(scatter_count(nz)), weights, (half, half), ra, *plan.part_a[1:], room_2)
    vec_steps = add_over_all(place, wire, numbers(bits), vec_own, vec_held)
    movers = (None, gather_a, gather_f, scatter_f, scatter_1, scatter_2)
    steps = {}
    for code in ORDER:
        family, kind, number = code // 10000, code // 100 % 100, code % 100
        if family == 6:
            steps[code] = vec_steps[number]
        elif family:
            by_plane = () if family < 3 else (family == 3,)
            steps[code] = movers[family].step(kind, number, *by_plane)

    copies = {}

    def copy_here(name, src, dst):
        copies[name] = pltpu.make_async_copy(src, dst, local.at[len(copies)])

    copy_here("x", x_in, x)
    copy_here("out_grad", out_grad_in, out_grad)
    copy_here("params", params, params_far)
    copy_here("qkv", qkv, qkv_far)
    copy_here("context", context, context_far)
    copy_here("result", out_grad, layer_out)
    copy_here("params_back", params_far, params_back)
    copy_here("qkv_back", qkv_far, qkv_back)
    copy_here("context_back", context_far, context_back)
    copy_here("in_grad", acc, in_grad)
    entered = place.greet((hub_a, hub_b))
    copies["x"].start()
    copies["out_grad"].start()

    joined_a[tail_a : tail_a + plan.unit_a, :] = shard_a[...].astype(F32)
    joined_f[tail_f : tail_f + plan.unit_f, :] = shard_f[...].astype(F32)
    end_a[...] = joined_a[plan.unit_a : plan.unit_a + tail_a, :]
    end_f[...] = joined_f[plan.unit_f : plan.unit_f + tail_f, :]
    at = tail_a + plan.at_attn_vec[1]
    vec_a[0:va, :] = joined_a[at : at + va, :].astype(BF16)
    at = tail_f + plan.at_ffn_vec[1]
    vec_a[va : va + vf, :] = joined_f[at : at + vf, :].astype(BF16)
    at = tail_f + plan.at_bias_in[1]
    vec_b[...] = jnp.zeros_like(vec_b)
    vec_b[0:gap, :] = joined_f[at : at + gap, :].astype(BF16)
    entered()

    @pl.when(me < n - 1)
    def _():
        wire.copy(end_a, halo_a, halo_in, me + 1).start()
        wire.copy(end_f, halo_f, halo_in + 1, me + 1).start()

    def vec_copy(src, dst, which, partner):
        return pltpu.make_async_remote_copy(
            src_ref=src, dst_ref=dst, send_sem=vec_send.at[partner], recv_sem=vec_recv.at[which],
            device_id=(partner,), device_id_type=MESH,
        )

    def to_all(src, dst, which, fn):
        @pl.when(me == (hub_a, hub_b)[which])
        def _():
            def one(j, carry):
                pl.when(j != me)(lambda: fn(vec_copy(src, dst, which, j)))
                return carry

            lax.fori_loop(0, n, one, 0)

    to_all(vec_a, got_a, 0, lambda copy: copy.start())
    to_all(vec_b, got_b, 1, lambda copy: copy.start())

    @pl.when(me > 0)
    def _():
        wire.copy(end_a, halo_a, halo_in, me - 1).wait_recv()
        joined_a[0:tail_a, :] = halo_a[...]

    start = tail_a - plan.shift_a(me)
    mine = params.at[me]

    @pl.when(me < plan.joint_src)
    def _():
        for b in range(3):
            for u in range(6):
                mine[b * jr : (b + 1) * jr, cols[u]] = joined_a[
                    pl.ds(start + 6 * b + u, jr, stride=18), :
                ].astype(BF16)

    @pl.when(me >= plan.joint_src)
    def _():
        for u in range(6):
            mine[:, cols[u]] = joined_a[pl.ds(start + u, ra, stride=6), :].astype(BF16)

    run([steps[code] for code in ORDER[: ORDER.index(RELAY)]])

    @pl.when(me > 0)
    def _():
        wire.copy(end_f, halo_f, halo_in + 1, me - 1).wait_recv()
        joined_f[0:tail_f, :] = halo_f[...]

    start_f = tail_f - plan.shift_f(me)
    mine_f = weights.at[me]

    @pl.when(me < plan.in_src)
    def _():
        for c in range(4):
            for u in range(6):
                mine_f[c * ir : (c + 1) * ir, cols[u]] = joined_f[
                    pl.ds(start_f + 6 * c + u, ir, stride=24), :
                ].astype(BF16)

    @pl.when(me >= plan.in_src)
    def _():
        for u in range(6):
            mine_f[:, cols[u]] = joined_f[pl.ds(start_f + u, plan.rows_f, stride=6), :].astype(BF16)

    run(after(RELAY, steps))
    build_masks(plan, ids, lens, key_add, query_one)

    @pl.when(me == hub_a)
    def _():
        got_a[...] = vec_a[...]

    @pl.when(me == hub_b)
    def _():
        got_b[...] = vec_b[...]

    @pl.when(me != hub_a)
    def _():
        vec_copy(vec_a, got_a, 0, hub_a).wait_recv()

    @pl.when(me != hub_b)
    def _():
        vec_copy(vec_b, got_b, 1, hub_b).wait_recv()

    got[0 : va + vf, :] = got_a[0 : va + vf, :].astype(F32)
    got[va + vf : va + vf + gap, :] = got_b[0:gap, :].astype(F32)
    vec[...] = jnp.zeros_like(vec)
    for u in range(6):
        vec[0:5, cols[u]] = got[pl.ds(u, 5, stride=6), :]
        vec[9:12, cols[u]] = got[pl.ds(va + u, 3, stride=6), :]
        vec[5:9, cols[u]] = got[pl.ds(va + vf + u, 4, stride=6), :]

    copies["x"].wait()
    scale = jnp.asarray(HEAD_DIM ** (-0.5), BF16)
    held = D // (nz - 1)
    partial = (acc, xhat)
    project = [code for code in ORDER if PROJECT <= code < PROJECT + nz]
    for j, code in enumerate(project):
        z = code - PROJECT
        if z < nz - 1:
            blocks, columns = pl.ds(8 * z, 8), pl.ds(held * z, held)
            for b in range(2):
                now = dot_nn(x[:, columns], params[blocks, b * jr : (b + 1) * jr, :].reshape(held, D))
                if j > 0:
                    now = now + partial[b][...]
                if j < nz - 2:
                    partial[b][...] = now
                elif b == 0:
                    qkv[0] = (now + vec[0:1, :]).astype(BF16) * scale
                else:
                    qkv[1] = now.astype(BF16)
        else:
            qkv[2] = (dot_nn(x[...], joint_weight(plan, params, 2)) + vec[1:2, :]).astype(BF16)
        run(after(code, steps))
    copies["qkv"].start()
    pairs = turns // rows

    def attend_pair(i):
        for r in range(rows):
            attend(i * rows + r, rows, qkv, key_add, query_one, context, log_totals)

    run_beside(pairs, attend_pair, beside(ATTEND, pairs, steps))
    copies["params"].start()
    copies["context"].start()
    gain_first, shift_first, bias_back = vec[3:4, :], vec[4:5, :], vec[9:10, :]
    gain_second, shift_second = vec[10:11, :], vec[11:12, :]

    def norm(t):
        rs = row_slots(t)
        v = x[rs, :].astype(F32) + (dot_nn(context[rs, :], out_weight(plan, params)) + vec[2:3, :])
        now, rstd = norm_parts(v)
        xhat[rs, :] = now
        rstd_first[rs, :] = jnp.broadcast_to(rstd, (rstd.shape[0], LANES))
        v = now * gain_first + shift_first
        norm_b[rs, :] = v.astype(BF16)
        acc[rs, :] = v + bias_back

    run_beside(rows, norm, beside(NORM, rows, steps))

    copies["qkv"].wait()
    copies["context"].wait()

    def up(c):
        hidden = dot_nn(norm_b[...], in_weight(plan, weights, c)) + vec[pl.ds(5 + c, 1), :]
        value, incline = gelu_with_slope(hidden)
        active[c] = value.astype(BF16)
        slope[c] = incline.astype(BF16)

    run_beside(4, up, beside(UP, 4, steps))

    def down(c):
        acc[...] += dot_nn(active[c], back_weight(plan, weights, c))

    run_beside(4, down, beside(DOWN, 4, steps))
    copies["out_grad"].wait()
    grads = vec_own.at[0]
    grads[...] = jnp.zeros(grads.shape, F32)

    def turn(rs):
        now, rstd = norm_parts(acc[rs, :])
        cot = out_grad[rs, :].astype(F32)
        out_grad[rs, :] = (now * gain_second + shift_second).astype(BF16)
        grads[10:11, :] += col_sum(cot * now)
        grads[11:12, :] += col_sum(cot)
        grad = norm_back(cot * gain_second, now, rstd)
        acc[rs, :] = grad
        low = grad.astype(BF16)
        grad_low[rs, :] = low
        grads[9:10, :] += col_sum(low.astype(F32))

    token_tiles(plan, SLOTS, turn)
    copies["result"].start()
    copies["params"].wait()
    gather_a.drain()

    back_order = (2, 3, 0, 1)
    for c in back_order:
        terms_f[back_blocks(plan, c)] = (
            dot_tn(active[c], grad_low[...]).astype(BF16).reshape(per, plan.rows_f, D)
        )
        if c == back_order[1]:
            run(after(BACK_WEIGHT, steps))
    run(after(BACK_WEIGHT + 1, steps))
    copies["context_back"].start()
    copies["qkv_back"].start()
    copies["result"].wait()

    def hidden_back(i):
        c = i // 2

        @pl.when(i == 2 * c)
        def _():
            into_hidden = dot_nt(grad_low[...], back_weight(plan, weights, c))
            grad = (slope[c].astype(F32) * into_hidden).astype(BF16)
            grad_hidden[...] = grad
            grads[pl.ds(5 + c, 1), :] += col_sum(grad.astype(F32))
            acc[...] += dot_nt(grad, in_weight(plan, weights, c))

        @pl.when(i != 2 * c)
        def _():
            in_rows = pl.ds(pl.multiple_of(c * ir, 16), ir)
            terms_f[0 : plan.in_src, in_rows, :] = (
                dot_tn(norm_b[...], grad_hidden[...]).astype(BF16).reshape(plan.in_src, ir, D)
            )

    run_beside(8, hidden_back, beside(HIDDEN, 8, steps))
    gather_f.drain()
    copies["params_back"].start()

    def leave(rs):
        grad, now = acc[rs, :], xhat[rs, :]
        grads[3:4, :] += col_sum(grad * now)
        grads[4:5, :] += col_sum(grad)
        grad = norm_back(grad * gain_first, now, rstd_first[rs, 0:1])
        acc[rs, :] = grad
        grad = grad.astype(BF16)
        grad_low[rs, :] = grad
        grads[2:3, :] += col_sum(grad.astype(F32))

    token_tiles(plan, SLOTS, leave)
    run(after(LEAVE, steps))
    copies["params_back"].wait()

    def into_context(rs):
        grad_context[rs, :] = dot_nt(grad_low[rs, :], out_weight(plan, params_back)).astype(BF16)

    token_tiles(plan, SLOTS, into_context)
    run(after(LEAVE + 1, steps))
    copies["context_back"].wait()
    terms_a[plan.joint_src : n] = (
        dot_tn(context_back[...], grad_low[...]).astype(BF16).reshape(n - plan.joint_src, ra, D)
    )
    copies["qkv_back"].wait()
    run(after(LEAVE + 2, steps))

    def joint_terms(first):
        for b in range(3):
            terms_a[0 : plan.joint_src, b * jr : (b + 1) * jr, first : first + half] = (
                dot_tn(x[...], grad_qkv[b, :, first : first + half]).astype(BF16).reshape(plan.joint_src, jr, half)
            )

    def back_pair(i):
        for r in range(rows):
            attend_back(i * rows + r, rows, qkv_back, key_add, query_one, log_totals, grad_context, grad_qkv)

    beside_back = beside(ATTEND_BACK, pairs, steps)
    beside_back[pairs // 2 - 1] += [lambda: joint_terms(0)] + after(JOINT + 1, steps)
    run_beside(pairs, back_pair, beside_back)
    joint_terms(half)
    grads[0:1, :] = col_sum(grad_qkv[0].astype(F32))
    grads[1:2, :] = col_sum(grad_qkv[2].astype(F32))
    run(after(JOINT + 2, steps))

    def input_grad(rs):
        now = acc[rs, :]
        for b in range(3):
            now = now + dot_nt(grad_qkv[b, rs, :], joint_weight(plan, params_back, b))
        acc[rs, :] = now

    size = plan.tokens // 4
    for j in range(4):
        input_grad(pl.ds(j * size, size))
        if j == 3:
            copies["in_grad"].start()
        run(after(INPUT_GRAD + j, steps))

    summed = vec_own.at[bits]
    total_f, total_a = terms_f.at[me], terms_a.at[me]

    @pl.when(me < plan.in_src)
    def _():
        for c in range(4):
            for u in range(6):
                joined_f[pl.ds(6 * c + u, ir, stride=24), :] = total_f[c * ir : (c + 1) * ir, cols[u]].astype(F32)

    @pl.when(me >= plan.in_src)
    def _():
        for u in range(6):
            joined_f[pl.ds(u, plan.rows_f, stride=6), :] = total_f[:, cols[u]].astype(F32)

    @pl.when(me < plan.joint_src)
    def _():
        for b in range(3):
            for u in range(6):
                joined_a[pl.ds(6 * b + u, jr, stride=18), :] = total_a[b * jr : (b + 1) * jr, cols[u]].astype(F32)

    @pl.when(me >= plan.joint_src)
    def _():
        for u in range(6):
            joined_a[pl.ds(u, ra, stride=6), :] = total_a[:, cols[u]].astype(F32)

    head_a, head_f = joined_a.at[0:tail_a], joined_f.at[0:tail_f]

    @pl.when(me > 0)
    def _():
        wire.copy(head_f, out_f, halo_out + 1, me - 1).start()
        wire.copy(head_a, out_a, halo_out, me - 1).start()

    rest_a = pl.ds(plan.block_a, tail_a)
    rest_f = pl.ds(plan.block_f, tail_f)

    @pl.when(me < n - 1)
    def _():
        wire.copy(head_f, out_f, halo_out + 1, me + 1).wait_recv()
        wire.copy(head_a, out_a, halo_out, me + 1).wait_recv()
        joined_f[rest_f, :] = out_f[...]
        joined_a[rest_a, :] = out_a[...]

    @pl.when(me == hub_b)
    def _():
        for u in range(6):
            joined_f[pl.ds(plan.block_f + u, 4, stride=6), :] = summed[5:9, cols[u]]
        joined_f[plan.block_f + gap : plan.block_f + tail_f, :] = out_f[0 : tail_f - gap, :]

    @pl.when(me == n - 1)
    def _():
        joined_f[rest_f, :] = jnp.zeros((tail_f, LANES), F32)
        joined_a[rest_a, :] = jnp.zeros((tail_a, LANES), F32)
        for u in range(6):
            joined_f[pl.ds(plan.block_f + u, 3, stride=6), :] = summed[9:12, cols[u]]
            joined_a[pl.ds(plan.block_a + u, 5, stride=6), :] = summed[0:5, cols[u]]

    ffn_grad[...] = joined_f[pl.ds(plan.shift_f(me), plan.unit_f), :]
    attn_grad[...] = joined_a[pl.ds(plan.shift_a(me), plan.unit_a), :]
    for u in range(6):
        bias_grad[u : u + 1, :] = summed[2:3, cols[u]]
    copies["in_grad"].wait()
    for mover in (scatter_f, scatter_1, scatter_2):
        mover.drain()
    to_all(vec_a, got_a, 0, lambda copy: copy.wait_send())
    to_all(vec_b, got_b, 1, lambda copy: copy.wait_send())

    @pl.when(me < n - 1)
    def _():
        wire.copy(end_a, halo_a, halo_in, me + 1).wait_send()
        wire.copy(end_f, halo_f, halo_in + 1, me + 1).wait_send()

    @pl.when(me > 0)
    def _():
        wire.copy(head_f, out_f, halo_out + 1, me - 1).wait_send()
        wire.copy(head_a, out_a, halo_out, me - 1).wait_send()


def hand_over(*arrays):
    def kernel(*refs):
        for j in range(len(arrays)):
            refs[len(arrays) + j][...] = refs[j][...]

    parts = 2
    specs = []
    for array in arrays:
        count, width = array.shape
        if count % (16 * parts) == 0:
            specs.append(pl.BlockSpec((count // parts, width), lambda i: (i, 0)))
        else:
            specs.append(pl.BlockSpec((count, width), lambda i: (0, 0)))
    return pl.pallas_call(
        kernel,
        name="hand_over",
        grid=(parts,),
        out_shape=[jax.ShapeDtypeStruct(array.shape, array.dtype) for array in arrays],
        in_specs=specs,
        out_specs=specs,
    )(*arrays)


def fused_body(plan, layer_in, pair_ids, pair_lengths, attn_shard, ffn_shard, out_grad):
    n, t, nz = plan.n, plan.tokens, plan.nz
    shape = jax.ShapeDtypeStruct
    bits = n.bit_length() - 1
    turns = HEADS // 2 * plan.rows
    sems = 4 + bits + 2 * gather_count(nz) + 3 * scatter_count(nz)
    low, full = pltpu.VMEM((t, D), BF16), pltpu.VMEM((t, D), F32)
    blocks = pltpu.VMEM((n, plan.rows_f, D), BF16)
    wide = pltpu.VMEM((4, t, D), BF16)
    side = pltpu.VMEM((t, LANES), BF16)
    vmem, far = pl.BlockSpec(memory_space=pltpu.VMEM), pl.BlockSpec(memory_space=pl.ANY)

    def units(count):
        return pltpu.VMEM((count, LANES), F32)

    def low_units(count):
        return pltpu.VMEM((count, LANES), BF16)

    layer_out, in_grad, attn_grad, ffn_grad, bias_grad = pl.pallas_call(
        functools.partial(layer_kernel, plan),
        name="layer",
        out_shape=[
            shape((t, D), BF16),
            shape((t, D), F32),
            shape((plan.unit_a, LANES), F32),
            shape((plan.unit_f, LANES), F32),
            shape((D // LANES, LANES), F32),
            shape((n, plan.rows_a, D), BF16),
            shape((3, t, D), BF16),
            shape((t, D), BF16),
        ],
        in_specs=[far] + [vmem] * 4 + [far],
        out_specs=[far] * 2 + [vmem] * 3 + [far] * 3,
        scratch_shapes=[
            low, blocks, wide, wide, blocks, low, low, low, full, full,
            pltpu.VMEM((t, LANES), F32),
            pltpu.VMEM((turns, 1, 2 * SLOTS), F32),
            side, side,
            pltpu.VMEM((16, D), F32),
            pltpu.VMEM((bits + 1, 16, D), F32),
            pltpu.VMEM((bits, 16, D), F32),
            units(plan.tail_a + -(-plan.unit_a // 8) * 8 + 8),
            units(plan.tail_f + -(-plan.unit_f // 8) * 8 + 8),
            units(plan.tail_a), units(plan.tail_f), units(plan.tail_a), units(plan.tail_f),
            low_units(48), low_units(32), low_units(48), low_units(32),
            units(80), units(plan.tail_a), units(plan.tail_f),
            pltpu.SemaphoreType.DMA((sems,)),
            pltpu.SemaphoreType.DMA((sems,)),
            pltpu.SemaphoreType.DMA((n,)),
            pltpu.SemaphoreType.DMA((2,)),
            pltpu.SemaphoreType.DMA((12,)),
        ]
        + Scatter.rooms(nz, D, *plan.part_f)
        + Scatter.rooms(nz, D // 2, *plan.part_a)
        + Scatter.rooms(nz, D // 2, *plan.part_a),
        compiler_params=pltpu.CompilerParams(
            collective_id=0, has_side_effects=True, vmem_limit_bytes=VMEM_LIMIT
        ),
    )(
        layer_in.reshape(t, D),
        pair_ids,
        jnp.swapaxes(pair_lengths, 1, 2),
        attn_shard.reshape(plan.unit_a, LANES),
        ffn_shard.reshape(plan.unit_f, LANES),
        out_grad.reshape(t, D),
    )[:5]
    layer_out, in_grad, attn_grad, ffn_grad, bias_grad = hand_over(layer_out, in_grad, attn_grad, ffn_grad, bias_grad)
    return (
        layer_out.reshape(layer_in.shape),
        in_grad.reshape(layer_in.shape),
        attn_grad.reshape(-1),
        ffn_grad.reshape(-1),
        bias_grad.reshape(-1),
    )


def unpack_attention(flattened):
    offset = 3 * D * D
    weight_joint = flattened[:offset].reshape(D, 3 * D)
    weight_out = flattened[offset : offset + D * D].reshape(D, D)
    offset = offset + D * D
    vectors = flattened[offset : offset + 5 * D].reshape(5, D)
    return (weight_joint, weight_out, vectors[0], vectors[1], vectors[2], vectors[3], vectors[4])


def unpack_feedforward(flattened):
    offset = D * FF
    weight_in = flattened[:offset].reshape(D, FF)
    bias_in = flattened[offset : offset + FF]
    offset = offset + FF
    weight_back = flattened[offset : offset + FF * D].reshape(FF, D)
    offset = offset + FF * D
    vectors = flattened[offset : offset + 3 * D].reshape(3, D)
    return (weight_in, bias_in, weight_back, vectors[0], vectors[1], vectors[2])


def layer_norm(values, gain_vec, shift_vec):
    row_mean = jnp.mean(values, axis=-1, keepdims=True)
    centred = values - row_mean
    row_var = jnp.mean(centred * centred, axis=-1, keepdims=True)
    return centred * lax.rsqrt(row_var + NORM_EPS) * gain_vec + shift_vec


def exact_gelu(values):
    return jax.nn.gelu(values, approximate=False)


def key_mask(pair_ids, pair_lengths):
    labels = jnp.arange(PAIRS, dtype=jnp.int32)
    member = pair_ids[:, :, None] == labels[None, None, :]
    starts = jnp.sum((pair_ids[:, :, None] < labels[None, None, :]).astype(jnp.int32), axis=1)
    live_len = pair_lengths[:, :, 0] + pair_lengths[:, :, 1]
    slot_start = jnp.sum(jnp.where(member, starts[:, None, :], 0), axis=-1)
    slot_len = jnp.sum(jnp.where(member, live_len[:, None, :], 0), axis=-1)
    places = jnp.arange(pair_ids.shape[1], dtype=jnp.int32)[None, :]
    is_live = places - slot_start < slot_len
    return (pair_ids[:, :, None] == pair_ids[:, None, :]) & is_live[:, None, :]


def contract_rows(one_side, other_side):
    return lax.dot_general(
        one_side, other_side, (((0,), (0,)), ((), ())), preferred_element_type=jnp.float32
    )


def contract_cols(one_side, other_side):
    return lax.dot_general(
        one_side, other_side, (((1,), (1,)), ((), ())), preferred_element_type=jnp.float32
    )


def attend_forward(queries, key_rows, value_rows, key_ok, score_scale):

    def head_block(block_index):
        head_start = block_index * 4
        query_b = lax.dynamic_slice_in_dim(queries, head_start, 4, 2)
        key_b = lax.dynamic_slice_in_dim(key_rows, head_start, 4, 2)
        value_b = lax.dynamic_slice_in_dim(value_rows, head_start, 4, 2)
        scores = (
            jnp.einsum("rqhd,rkhd->rhqk", query_b, key_b, preferred_element_type=jnp.float32)
            * score_scale
        )
        scores = jnp.where(key_ok[:, None], scores, -1e30)
        row_max = jnp.max(scores, axis=-1, keepdims=True)
        raised = jnp.exp(scores - row_max)
        totals = jnp.sum(raised, axis=-1, keepdims=True)
        shares = (raised / totals).astype(jnp.bfloat16)
        context = jnp.einsum("rhqk,rkhd->rqhd", shares, value_b, preferred_element_type=jnp.float32)
        return (context, row_max + jnp.log(totals))

    return lax.map(head_block, jnp.arange(HEADS // 4))


def attend_backward(queries, key_rows, value_rows, grad_context, log_totals, key_ok, score_scale):

    def head_block(operands):
        block_index, log_total = operands
        head_start = block_index * 4
        query_b = lax.dynamic_slice_in_dim(queries, head_start, 4, 2)
        key_b = lax.dynamic_slice_in_dim(key_rows, head_start, 4, 2)
        value_b = lax.dynamic_slice_in_dim(value_rows, head_start, 4, 2)
        grad_block = lax.dynamic_slice_in_dim(grad_context, head_start, 4, 2)
        scores = (
            jnp.einsum("rqhd,rkhd->rhqk", query_b, key_b, preferred_element_type=jnp.float32)
            * score_scale
        )
        shares = jnp.where(key_ok[:, None], jnp.exp(scores - log_total), 0.0)
        grad_shares = jnp.einsum(
            "rqhd,rkhd->rhqk", grad_block, value_b, preferred_element_type=jnp.float32
        )
        inner_sum = jnp.sum(shares * grad_shares, axis=-1, keepdims=True)
        grad_scores = (shares * (grad_shares - inner_sum)).astype(jnp.bfloat16)
        grad_query = (
            jnp.einsum("rhqk,rkhd->rqhd", grad_scores, key_b, preferred_element_type=jnp.float32)
            * score_scale
        )
        grad_key = (
            jnp.einsum("rhqk,rqhd->rkhd", grad_scores, query_b, preferred_element_type=jnp.float32)
            * score_scale
        )
        grad_value = jnp.einsum(
            "rhqk,rqhd->rkhd",
            shares.astype(jnp.bfloat16),
            grad_block,
            preferred_element_type=jnp.float32,
        )
        return (grad_query, grad_key, grad_value)

    gradients = lax.map(head_block, (jnp.arange(HEADS // 4), log_totals))
    return [jnp.moveaxis(piece, 0, 2).reshape(-1, D) for piece in gradients]


def plain_body(layer_in, pair_ids, pair_lengths, attn_shard, ffn_shard, out_grad):
    row_count = layer_in.shape[0]
    tokens = row_count * SLOTS
    score_scale = HEAD_DIM ** (-0.5)
    key_ok = key_mask(pair_ids, pair_lengths)
    att_whole = lax.all_gather(attn_shard, "fsdp", axis=0, tiled=True)
    weight_joint, weight_out, bias_query, bias_value, bias_out, gain_first, shift_first = (
        unpack_attention(att_whole)
    )
    inputs = layer_in.reshape(tokens, D)
    bias_joint = jnp.concatenate([bias_query, jnp.zeros_like(bias_query), bias_value]).astype(
        jnp.float32
    )
    projected = (
        jnp.dot(inputs, weight_joint, preferred_element_type=jnp.float32) + bias_joint
    ).astype(jnp.bfloat16)
    projected = projected.reshape(row_count, SLOTS, 3, HEADS, HEAD_DIM)
    queries = projected[:, :, 0]
    key_rows = projected[:, :, 1]
    value_rows = projected[:, :, 2]
    contexts, log_totals = attend_forward(queries, key_rows, value_rows, key_ok, score_scale)
    context = jnp.moveaxis(contexts, 0, 2).reshape(tokens, D).astype(jnp.bfloat16)
    attn_out = jnp.dot(context, weight_out, preferred_element_type=jnp.float32) + bias_out.astype(
        jnp.float32
    )
    norm_first, first_pull = jax.vjp(
        layer_norm,
        inputs.astype(jnp.float32) + attn_out,
        gain_first.astype(jnp.float32),
        shift_first.astype(jnp.float32),
    )
    norm_first_b = norm_first.astype(jnp.bfloat16)
    feed_whole = lax.all_gather(ffn_shard, "fsdp", axis=0, tiled=True)
    weight_in, bias_in, weight_back, bias_back, gain_second, shift_second = unpack_feedforward(
        feed_whole
    )
    hidden = jnp.dot(norm_first_b, weight_in, preferred_element_type=jnp.float32) + bias_in.astype(
        jnp.float32
    )
    active, gelu_pull = jax.vjp(exact_gelu, hidden)
    active_b = active.astype(jnp.bfloat16)
    ffn_out = jnp.dot(active_b, weight_back, preferred_element_type=jnp.float32) + bias_back.astype(
        jnp.float32
    )
    result, second_pull = jax.vjp(
        layer_norm,
        norm_first + ffn_out,
        gain_second.astype(jnp.float32),
        shift_second.astype(jnp.float32),
    )
    layer_out = result.astype(jnp.bfloat16).reshape(row_count, SLOTS, D)
    feed_back = lax.all_gather(ffn_shard, "fsdp", axis=0, tiled=True)
    weight_in, bias_in, weight_back, bias_back, gain_second, shift_second = unpack_feedforward(
        feed_back
    )
    cotangent = out_grad.reshape(tokens, D).astype(jnp.float32)
    grad_sum_second, grad_gain_second, grad_shift_second = second_pull(cotangent)
    grad_ffn = grad_sum_second.astype(jnp.bfloat16)
    grad_bias_back = jnp.sum(grad_ffn.astype(jnp.float32), axis=0)
    grad_weight_back = contract_rows(active_b, grad_ffn)
    (grad_hidden,) = gelu_pull(contract_cols(grad_ffn, weight_back))
    grad_hidden = grad_hidden.astype(jnp.bfloat16)
    grad_bias_in = jnp.sum(grad_hidden.astype(jnp.float32), axis=0)
    grad_weight_in = contract_rows(norm_first_b, grad_hidden)
    grad_norm_first = grad_sum_second + contract_cols(grad_hidden, weight_in)
    grad_sum_first, grad_gain_first, grad_shift_first = first_pull(grad_norm_first)
    feed_pad = feed_back.shape[0] - (2 * D * FF + FF + 3 * D)
    feed_full = jnp.concatenate(
        [
            grad_weight_in.reshape(-1),
            grad_bias_in,
            grad_weight_back.reshape(-1),
            grad_bias_back,
            grad_gain_second,
            grad_shift_second,
            jnp.zeros((feed_pad,), jnp.float32),
        ]
    )
    ffn_grad = lax.psum_scatter(feed_full, "fsdp", scatter_dimension=0, tiled=True)
    att_back = lax.all_gather(attn_shard, "fsdp", axis=0, tiled=True)
    weight_joint, weight_out, bias_query, bias_value, bias_out, gain_first, shift_first = (
        unpack_attention(att_back)
    )
    grad_attn = grad_sum_first.astype(jnp.bfloat16)
    grad_bias_out = jnp.sum(grad_attn.astype(jnp.float32), axis=0)
    out_bias_grad = lax.psum(grad_bias_out, "fsdp")
    grad_weight_out = contract_rows(context, grad_attn)
    grad_context = (
        contract_cols(grad_attn, weight_out)
        .astype(jnp.bfloat16)
        .reshape(row_count, SLOTS, HEADS, HEAD_DIM)
    )
    grad_query, grad_key, grad_value = attend_backward(
        queries, key_rows, value_rows, grad_context, log_totals, key_ok, score_scale
    )
    grad_projected = jnp.concatenate([grad_query, grad_key, grad_value], axis=-1).astype(
        jnp.bfloat16
    )
    column_sums = jnp.sum(grad_projected.astype(jnp.float32), axis=0)
    grad_weight_joint = contract_rows(inputs, grad_projected)
    in_grad = grad_sum_first + contract_cols(grad_projected, weight_joint)
    att_pad = att_back.shape[0] - (4 * D * D + 5 * D)
    attn_full = jnp.concatenate(
        [
            grad_weight_joint.reshape(-1),
            grad_weight_out.reshape(-1),
            column_sums[:D],
            column_sums[2 * D :],
            grad_bias_out,
            grad_gain_first,
            grad_shift_first,
            jnp.zeros((att_pad,), jnp.float32),
        ]
    )
    attn_grad = lax.psum_scatter(attn_full, "fsdp", scatter_dimension=0, tiled=True)
    return (layer_out, in_grad.reshape(row_count, SLOTS, D), attn_grad, ffn_grad, out_bias_grad)


def body(layer_in, pair_ids, pair_lengths, attn_shard, ffn_shard, out_grad, devices):
    plan = Plan(devices, attn_shard.shape[0], ffn_shard.shape[0], layer_in.shape[0])
    run = functools.partial(fused_body, plan) if plan.fits() else plain_body
    return run(layer_in, pair_ids, pair_lengths, attn_shard, ffn_shard, out_grad)


def solution(mesh):
    placed = (
        P("fsdp", None, None),
        P("fsdp", None),
        P("fsdp", None, None),
        P("fsdp"),
        P("fsdp"),
        P("fsdp", None, None),
    )
    return jax.shard_map(
        functools.partial(body, devices=mesh.shape["fsdp"]),
        mesh=mesh,
        in_specs=placed,
        out_specs=(P("fsdp", None, None), P("fsdp", None, None), P("fsdp"), P("fsdp"), P()),
        check_vma=False,
    )
```

```python
import functools

import jax
import jax.numpy as jnp
from jax import lax
from jax.experimental import pallas as pl
from jax.experimental.pallas import tpu as pltpu
from jax.sharding import PartitionSpec as P

D = 768
HEADS = 12
HEAD_DIM = 64
FF = 3072
SLOTS = 416
PAIRS = 3
LANES = 128
NORM_EPS = 1e-12
F32 = jnp.float32
BF16 = jnp.bfloat16
MESH = pl.DeviceIdType.MESH
VMEM_LIMIT = 62 << 20
FINISH = 11
RELAY, PROJECT, ATTEND, NORM, UP, DOWN, TURN, BACK_WEIGHT, HIDDEN, LEAVE, ATTEND_BACK, JOINT, INPUT_GRAD = range(
    0, 1300, 100
)


def dot_nn(a, b):
    return lax.dot_general(a, b, (((1,), (0,)), ((), ())), preferred_element_type=F32)


def dot_nt(a, b):
    return lax.dot_general(a, b, (((1,), (1,)), ((), ())), preferred_element_type=F32)


def dot_tn(a, b):
    return lax.dot_general(a, b, (((0,), (0,)), ((), ())), preferred_element_type=F32)


def row_mean(v):
    return jnp.sum(v, axis=1, keepdims=True) * (1.0 / D)


def col_sum(v):
    return jnp.sum(v, axis=0, keepdims=True)


class Plan:
    def __init__(self, n, attn_shard_len, ffn_shard_len, row_count):
        self.n = n
        self.nz = n // 8
        self.rows = row_count
        self.tokens = row_count * SLOTS
        self.unit_a = attn_shard_len // LANES
        self.unit_f = ffn_shard_len // LANES
        self.block_a = 4 * D * D // LANES // n
        self.block_f = 2 * D * FF // LANES // n
        self.rows_a = 4 * D // n
        self.rows_f = 2 * FF // n
        self.joint_rows = self.rows_a // 3
        self.joint_src = 3 * n // 4
        self.in_rows = self.rows_f // 4
        self.in_src = n // 2
        self.part_a = (0, self.rows_a, 16, 32)
        self.part_f = (0, self.rows_f, 48, 64)
        self.gap = FF // LANES
        self.at_attn_vec = divmod(4 * D * D // LANES, self.unit_a)
        self.at_bias_in = divmod(D * FF // LANES, self.unit_f)
        self.at_ffn_vec = divmod(2 * D * FF // LANES + self.gap, self.unit_f)

    def shift_a(self, me):
        return me * (self.unit_a - self.block_a)

    def shift_f(self, me):
        return me * (self.unit_f - self.block_f) - jnp.where(me >= self.in_src, self.gap, 0)

    def fits(self):
        n = self.n
        if self.nz != 4 or n % 8 or self.rows_a % 48 or self.rows_f % 64:
            return False
        last_a = (n - 1) * (self.unit_a - self.block_a)
        step_f = self.unit_f - self.block_f
        last_f = max((self.in_src - 1) * step_f, (n - 1) * step_f - self.gap)
        first_f = self.in_src * step_f - self.gap
        self.tail_a = -(-(last_a + 1) // 8) * 8
        self.tail_f = -(-(last_f + 2) // 8) * 8
        vec_a, vec_f = 5 * D // LANES, 3 * D // LANES
        return (
            step_f >= 0
            and self.unit_a >= self.block_a
            and first_f >= 0
            and self.tail_a <= self.block_a
            and self.tail_f <= self.block_f
            and self.at_attn_vec[0] == n - 1
            and self.at_ffn_vec[0] == n - 1
            and self.at_bias_in[0] == self.in_src - 1
            and self.unit_a - self.at_attn_vec[1] <= self.tail_a
            and self.unit_f - self.at_ffn_vec[1] <= self.tail_f
            and self.at_attn_vec[1] + vec_a <= self.unit_a
            and self.at_ffn_vec[1] + vec_f <= self.unit_f
            and self.at_bias_in[1] + self.gap <= self.unit_f
            and self.at_bias_in[1] == self.block_f - (self.in_src - 1) * step_f
        )


class Place:
    def __init__(self, plan):
        self.n, self.nz = plan.n, plan.nz
        me = lax.axis_index("fsdp")
        self.me = me
        self.core = lax.rem(me, 2)
        self.x = lax.rem(me // 2, 2)
        self.y = lax.rem(me // 4, 2)
        self.z = me // 8
        self.sib = me + 1 - 2 * self.core
        self.xn = me + 2 - 4 * self.x
        self.yn = me + 4 - 8 * self.y

    def block(self, column, z, other_core=False):
        x = self.x if column in (0, 2) else 1 - self.x
        y = self.y if column in (0, 1) else 1 - self.y
        core = 1 - self.core if other_core else self.core
        return ((z * 2 + y) * 2 + x) * 2 + core

    def level(self, distance, fn):
        if distance == 0:
            fn(self.z)
            return
        pl.when(self.z >= distance)(lambda: fn(self.z - distance))
        pl.when(self.z + distance < self.nz)(lambda: fn(self.z + distance))

    def onward(self, z, fn):
        pl.when((z <= self.z) & (self.z < self.nz - 1))(lambda: fn(self.me + 8))
        pl.when((z >= self.z) & (self.z > 0))(lambda: fn(self.me - 8))

    def bits(self):
        out = []
        bit = 1
        while bit < self.n:
            out.append(self.me + bit - 2 * bit * lax.rem(self.me // bit, 2))
            bit *= 2
        return out

    def greet(self, hubs):
        sem = pltpu.get_barrier_semaphore()

        def tell(partner):
            pl.semaphore_signal(sem, inc=1, device_id=(partner,), device_id_type=MESH)

        fixed = self.bits()
        for partner in fixed:
            tell(partner)
        z_odd = lax.rem(self.z, 2)
        far_z = (self.z > 0) & (self.z < self.nz - 1)
        far = (self.me > 0) & (self.me < self.n - 1)
        pl.when(far_z)(lambda: tell(self.me - 8 + 16 * z_odd))
        pl.when(far)(lambda: tell(self.me - 1 + 2 * self.core))
        count = len(fixed) + far_z.astype(jnp.int32) + far.astype(jnp.int32)
        for hub in hubs:
            pl.when(self.me != hub)(lambda: tell(hub))
            count = count + jnp.where(self.me == hub, self.n - 1, 0)
        return lambda: pl.semaphore_wait(sem, count)


class Wire:
    def __init__(self, send, recv):
        self.send, self.recv = send, recv
        self.sent = []

    def copy(self, src, dst, number, partner):
        return pltpu.make_async_remote_copy(
            src_ref=src,
            dst_ref=dst,
            send_sem=self.send.at[number],
            recv_sem=self.recv.at[number],
            device_id=(partner,),
            device_id_type=MESH,
        )


def add_over_all(place, wire, base, own, held):
    partners = place.bits()

    def send(s):
        wire.copy(own.at[s], held.at[s], base + s, partners[s]).start()

    def take(s):
        wire.copy(own.at[s], held.at[s], base + s, partners[s]).wait()
        own[s + 1] = own[s] + held[s]

    steps = [lambda: send(0)]
    for s in range(len(partners)):

        def step(s=s):
            take(s)
            if s + 1 < len(partners):
                send(s + 1)

        steps.append(step)
    return steps


def gather_count(nz):
    return 17 * nz + 3


class Gather:
    def __init__(self, place, wire, base, ref, top, rows, late, half):
        self.p, self.w, self.ref = place, wire, ref
        nz = place.nz
        self.early = (top, rows - late)
        self.late = (top + rows - late, late)
        self.first = (top, half)
        self.second = (top + half, rows - late - half)
        at = [base]

        def take(count):
            at[0] += count
            return at[0] - count

        self.line, self.xs, self.ys, self.d1, self.d2 = (take(nz) for _ in range(5))
        self.sib, self.late_line, self.late_sib = (take(4 * nz) for _ in range(3))
        self.px, self.py, self.pd = (take(1) for _ in range(3))

    def move(self, column, z, part, number, partner):
        ref = self.ref.at[self.p.block(column, z), pl.ds(*part)]
        return self.w.copy(ref, ref, number, partner)

    def send(self, *args):
        self.move(*args).start()

    def wait(self, column, z, part, number):
        self.move(column, z, part, number, self.p.sib).wait_recv()

    def to_sib(self, column, z):
        self.send(column, z, self.early, self.sib + column * self.p.nz + z, self.p.sib)

    def spread(self, z):
        p = self.p
        p.onward(z, lambda partner: self.send(0, z, self.early, self.line + z, partner))
        self.send(0, z, self.early, self.xs + z, p.xn)
        self.send(0, z, self.early, self.ys + z, p.yn)
        self.to_sib(0, z)

    def spread_late(self, column, z):
        number = column * self.p.nz + z
        self.p.onward(
            z, lambda partner: self.send(column, z, self.late, self.late_line + number, partner)
        )
        self.send(column, z, self.late, self.late_sib + number, self.p.sib)

    def take_line(self, z):
        self.wait(0, z, self.early, self.line + z)
        self.spread(z)

    def take_x(self, z):
        self.wait(1, z, self.early, self.xs + z)
        self.send(1, z, self.first, self.d1 + z, self.p.yn)
        self.to_sib(1, z)

    def take_y(self, z):
        self.wait(2, z, self.early, self.ys + z)
        self.send(2, z, self.second, self.d2 + z, self.p.xn)
        self.to_sib(2, z)

    def take_corner(self, z):
        self.wait(3, z, self.first, self.d1 + z)
        self.wait(3, z, self.second, self.d2 + z)
        self.to_sib(3, z)

    def take_late(self, z):
        for column in range(4):
            self.wait(column, z, self.late, self.late_line + column * self.p.nz + z)
            self.spread_late(column, z)

    def begin(self):
        self.spread(self.p.z)

    def begin_late(self):
        p = self.p
        self.send(0, p.z, self.late, self.px, p.xn)
        self.send(0, p.z, self.late, self.py, p.yn)

    def late_x(self):
        self.wait(1, self.p.z, self.late, self.px)
        self.send(1, self.p.z, self.late, self.pd, self.p.yn)

    def late_y(self):
        self.wait(2, self.p.z, self.late, self.py)

    def late_corner(self):
        self.wait(3, self.p.z, self.late, self.pd)

    def step(self, kind, number):
        p = self.p
        plane, digit = number // 10, number % 10
        starts = (self.begin, self.begin_late, self.late_x, self.late_y, self.late_corner,
                  lambda: self.spread_late(digit, p.z))
        takes = (self.take_line, self.take_x, self.take_y, self.take_corner, self.take_late)
        if kind == FINISH:
            planes = range(plane, plane + digit)
            return lambda: self.finish(planes)
        if kind < len(starts):
            return lambda: pl.when(p.z == plane)(starts[kind])
        take = takes[kind - len(starts)]
        if digit:
            return lambda: pl.when((p.z == plane - digit) | (p.z == plane + digit))(lambda: take(plane))
        return lambda: take(plane)

    def finish(self, planes):
        p, nz = self.p, self.p.nz

        def one(j, carry):
            for column in range(4):
                ref = self.ref.at[p.block(column, j, True)]
                for part, base in ((self.early, self.sib), (self.late, self.late_sib)):
                    r = ref.at[pl.ds(*part)]
                    self.w.copy(r, r, base + column * nz + j, p.sib).wait_recv()
            return carry

        lax.fori_loop(planes[0], planes[-1] + 1, one, 0)

    def drain(self):
        p, nz = self.p, self.p.nz

        def sent(column, z, part, number):
            self.move(column, z, part, number, p.sib).wait_send()

        sent(0, p.z, self.late, self.px)
        sent(0, p.z, self.late, self.py)
        sent(1, p.z, self.late, self.pd)

        def one(z, carry):
            p.onward(z, lambda partner: sent(0, z, self.early, self.line + z))
            sent(0, z, self.early, self.xs + z)
            sent(0, z, self.early, self.ys + z)
            sent(1, z, self.first, self.d1 + z)
            sent(2, z, self.second, self.d2 + z)
            for column in range(4):
                number = column * nz + z
                sent(column, z, self.early, self.sib + number)
                sent(column, z, self.late, self.late_sib + number)
                p.onward(z, lambda partner: sent(column, z, self.late, self.late_line + number))
            return carry

        lax.fori_loop(0, nz, one, 0)


def gather_count(nz):
    return 17 * nz + 3


ORDER = (
    10030, 10000, 10500, 10010, 10510, 10020, 10120, 0, 10130, 10100, 20030, 20000, 20500, 20020, 20100,
    10110, 10200, 10601, 10501, 20130, 10300, 10621, 10631, 10210, 20010, 10230, 10220, 10611, 10502, 20530,
    10520, 10602, 10622, 10612, 10310, 10632, 10531, 10400, 10512, 10320, 10522, 10430, 10533, 10503, 10521,
    20520, 10603, 10420, 10523, 20200, 20120, 10410, 20501, 10513, 10810, 11002, 10511, 10330, 10633, 10820,
    10720, 11011, 10710, 11001, 10800, 20110, 20230, 10700, 10530, 20400, 20631, 11022, 11021, 10532, 20601,
    10730, 10830, 11012, 11003, 20220, 20521, 20602, 20300, 20621, 20503, 20502, 20310, 11031, 20512, 20330,
    10920, 10910, 20611, 20430, 10900, 20320, 11121, 11111, 20210, 20632, 20533, 11101, 20531, 20522, 100,
    20622, 21001, 102, 20532, 11032, 20510, 20603, 101, 103, 200, 10930, 20420, 20523, 20511, 20612, 20633,
    201, 21002, 11033, 11131, 20410, 20513, 21031, 20700, 21021, 20800, 202, 203, 20710, 20810, 20830,
    21011, 20730, 204, 20900, 20820, 21003, 21032, 205, 300, 20720, 21022, 20910, 301, 21012, 20930, 21102,
    400, 20920, 401, 21033, 21122, 402, 403, 500, 501, 502, 503, 600, 700, 30030, 701, 30020, 30230, 30130,
    30633, 800, 30220, 30120, 30622, 801, 802, 30430, 30330, 30320, 803, 30420, 30632, 804, 805, 806, 30533,
    30621, 807, 30000, 30010, 900, 30100, 901, 30200, 30110, 30603, 902, 30631, 30522, 30210, 30612, 30532,
    30300, 1000, 30400, 30410, 1001, 30602, 30310, 1002, 30630, 30503, 1101, 40001, 40002, 30611, 40003,
    30531, 30730, 1003, 30601, 40101, 30620, 30512, 30720, 40203, 30502, 40201, 40103, 40603, 30830, 1004,
    40403, 30521, 40102, 40401, 30610, 30710, 30820, 40301, 30511, 40303, 40202, 1005, 40302, 40402, 30501,
    1102, 50003, 30600, 40503, 60000, 30920, 50103, 30700, 30810, 30930, 30520, 30530, 50002, 50001, 40602,
    40000, 60001, 50203, 50603, 40502, 50102, 50303, 50403, 1200, 30800, 50101, 40100, 50202, 50602, 30510,
    60002, 50000, 50302, 40601, 30910, 50402, 50503, 50100, 30500, 30900, 50201, 40200, 50401, 50601, 50301,
    50200, 40600, 40700, 60003, 50502, 40501, 50600, 50700, 40300, 40400, 1201, 60004, 50400, 50300, 50501,
    40800, 50800, 1202, 1203, 40500, 40900, 60005, 50900, 50500,
)

class Scatter:
    def __init__(self, place, wire, base, terms, columns, top, rows, late, half, room):
        self.p, self.w, self.terms, self.columns = place, wire, terms, columns
        nz = place.nz
        self.whole = (top, rows)
        self.early = (top, rows - late)
        self.late = (top + rows - late, late)
        self.first = (top, half)
        self.second = (top + half, rows - late - half)
        (self.side, self.in_first, self.in_second, self.in_x, self.in_y, self.in_line, self.in_late,
         self.in_plane) = room
        at = [base]

        def take(count):
            at[0] += count
            return at[0] - count

        self.sib = take(4 * nz)
        self.d1, self.d2, self.xs, self.ys = (take(nz) for _ in range(4))
        self.line = take(nz + 1)
        self.late_line = take(4 * (nz + 1))
        self.plane = take(3)

    @staticmethod
    def rooms(nz, columns, top, rows, late, half):
        def room(count, size):
            return pltpu.VMEM((count, size, columns), BF16)

        early = rows - late
        return [
            room(4 * nz, rows), room(nz, half), room(nz, early - half), room(nz, early), room(nz, early),
            room(nz + 1, early), room(4 * (nz + 1), late), room(3, late),
        ]

    def slot(self, column, z):
        return column * self.p.nz + z

    def term(self, column, z, part, other_core=False):
        return self.terms.at[self.p.block(column, z, other_core), pl.ds(*part), pl.ds(*self.columns)]

    def add(self, target, term):
        count = target.shape[0]
        step = count if count <= 48 else next(s for s in (48, 32, 16) if count % s == 0)

        def some(i, carry):
            rs = pl.ds(pl.multiple_of(i * step, 16), step)
            target[rs, :] = target[rs, :] + term[rs, :]
            return carry

        lax.fori_loop(0, count // step, some, 0)

    def got(self, ref, number):
        self.w.copy(ref, ref, number, self.p.sib).wait_recv()
        return ref

    def send_sib(self, z):
        p = self.p
        for column in (3, 1, 2, 0):
            k = self.slot(column, z)
            self.w.copy(self.term(column, z, self.whole, True), self.side.at[k], self.sib + k, p.sib).start()

    def take_sib(self, column, z):
        k = self.slot(column, z)
        self.add(self.term(column, z, self.whole), self.got(self.side.at[k], self.sib + k))

    def corner(self, z):
        p = self.p
        self.take_sib(3, z)
        self.w.copy(self.term(3, z, self.first), self.in_first.at[z], self.d1 + z, p.yn).start()
        self.w.copy(self.term(3, z, self.second), self.in_second.at[z], self.d2 + z, p.xn).start()

    def take_rest(self, z):
        for column in (1, 2, 0):
            self.take_sib(column, z)

    def side_x(self, z):
        p = self.p
        self.add(self.term(1, z, self.first), self.got(self.in_first.at[z], self.d1 + z))
        self.w.copy(self.term(1, z, self.early), self.in_x.at[z], self.xs + z, p.xn).start()

    def side_y(self, z):
        p = self.p
        self.add(self.term(2, z, self.second), self.got(self.in_second.at[z], self.d2 + z))
        self.w.copy(self.term(2, z, self.early), self.in_y.at[z], self.ys + z, p.yn).start()

    def own(self, z):
        ref = self.term(0, z, self.early)
        self.add(ref, self.got(self.in_x.at[z], self.xs + z))
        self.add(ref, self.got(self.in_y.at[z], self.ys + z))
        self.along(z, ref, self.in_line, self.line, 0)

    def own_late(self, z):
        for column in range(4):
            self.along(z, self.term(column, z, self.late), self.in_late, self.late_line,
                       column * (self.p.nz + 1))

    def along(self, z, ref, room, number, at):
        p, nz = self.p, self.p.nz
        below, above = p.z > 0, p.z < nz - 1

        def take(slot):
            self.add(ref, self.got(room.at[at + slot], number + at + slot))

        def send(slot, partner):
            self.w.copy(ref, room.at[at + slot], number + at + slot, partner).start()

        pl.when((z >= p.z) & below)(lambda: take(z))
        pl.when((z < p.z) & above)(lambda: take(z))
        pl.when((z == p.z) & above)(lambda: take(nz))
        pl.when(z > p.z)(lambda: send(z, p.me + 8))
        pl.when(z < p.z)(lambda: send(jnp.where(z == p.z - 1, nz, z), p.me - 8))

    def plane_corner(self):
        p = self.p
        self.w.copy(self.term(3, p.z, self.late), self.in_plane.at[0], self.plane, p.yn).start()

    def plane_sides(self):
        p = self.p
        self.w.copy(self.term(2, p.z, self.late), self.in_plane.at[2], self.plane + 2, p.yn).start()
        ref = self.term(1, p.z, self.late)
        self.add(ref, self.got(self.in_plane.at[0], self.plane))
        self.w.copy(ref, self.in_plane.at[1], self.plane + 1, p.xn).start()

    def plane_own(self):
        ref = self.term(0, self.p.z, self.late)
        self.add(ref, self.got(self.in_plane.at[1], self.plane + 1))
        self.add(ref, self.got(self.in_plane.at[2], self.plane + 2))

    def step(self, kind, number, by_plane):
        p = self.p
        plane, digit = number // 10, number % 10
        takes = (self.send_sib, self.corner, self.take_rest, self.side_x, self.side_y, self.own, self.own_late)
        ends = (self.plane_corner, self.plane_sides, self.plane_own)
        if kind >= len(takes):
            end = ends[kind - len(takes)]
            return (lambda: pl.when(p.z == plane)(end)) if by_plane else end
        take = takes[kind]
        if not by_plane:
            return lambda: p.level(digit, take)
        if take in (self.own, self.own_late):
            return lambda: pl.when((p.z == plane - digit) | (p.z == plane + digit))(lambda: take(plane))
        return lambda: take(plane)

    def drain(self):
        p, nz = self.p, self.p.nz

        def sent(ref, number):
            self.w.copy(ref, ref, number, p.sib).wait_send()

        for i in range(3):
            sent(self.in_plane.at[i], self.plane + i)

        def one(z, carry):
            for column in range(4):
                k = self.slot(column, z)
                sent(self.side.at[k], self.sib + k)
            sent(self.in_first.at[z], self.d1 + z)
            sent(self.in_second.at[z], self.d2 + z)
            sent(self.in_x.at[z], self.xs + z)
            sent(self.in_y.at[z], self.ys + z)

            def lines(slot):
                sent(self.in_line.at[slot], self.line + slot)
                for column in range(4):
                    at = column * (nz + 1) + slot
                    sent(self.in_late.at[at], self.late_line + at)

            pl.when(z > p.z)(lambda: lines(z))
            pl.when(z < p.z)(lambda: lines(jnp.where(z == p.z - 1, nz, z)))
            return carry

        lax.fori_loop(0, nz, one, 0)


def scatter_count(nz):
    return 4 * nz + 4 * nz + nz + 1 + 4 * (nz + 1) + 3


def build_masks(plan, ids_ref, len_ref, key_add, query_one):
    for r in range(plan.rows):
        ids = jnp.broadcast_to(ids_ref[r : r + 1, :], (LANES, SLOTS))
        label = lax.broadcasted_iota(jnp.int32, (LANES, SLOTS), 0)
        place = lax.broadcasted_iota(jnp.int32, (LANES, SLOTS), 1)
        start = jnp.sum((ids < label).astype(F32), axis=1, keepdims=True)
        lengths = len_ref[r]
        lengths = lengths[0:1, :] + lengths[1:2, :]
        live = jnp.zeros((LANES, SLOTS), jnp.int32)
        for j in range(PAIRS):
            live = jnp.where(label == j, lengths[:, j : j + 1], live)
        same = ids == label
        ok = same & (place.astype(F32) - start < live.astype(F32))
        rs = pl.ds(r * SLOTS, SLOTS)
        key_add[rs, :] = jnp.where(ok | (label >= PAIRS), 0.0, -1e30).T.astype(BF16)
        query_one[rs, :] = same.astype(F32).T.astype(BF16)


def split_heads(v):
    lane = lax.broadcasted_iota(jnp.int32, v.shape, 1)
    zero = jnp.zeros_like(v)
    return jnp.concatenate(
        [jnp.where(lane < HEAD_DIM, v, zero), jnp.where(lane < HEAD_DIM, zero, v)], axis=0
    )


def join_heads(v):
    lane = lax.broadcasted_iota(jnp.int32, (SLOTS, LANES), 1)
    return jnp.where(lane < HEAD_DIM, v[:SLOTS], v[SLOTS:])


def head_pair(i, rows):
    r, p = lax.rem(i, rows), i // rows
    return (
        pl.ds(pl.multiple_of(r * SLOTS, 16), SLOTS),
        pl.ds(pl.multiple_of(p * LANES, LANES), LANES),
    )


def scores_of(rs, cs, qkv, key_add, query_one):
    q, k, one = qkv[0, rs, cs], qkv[1, rs, cs], query_one[rs, :]
    q_side = jnp.concatenate([split_heads(q), jnp.concatenate([one, one], axis=0)], axis=1)
    k_side = jnp.concatenate([k, key_add[rs, :]], axis=1)
    return dot_nt(k_side, q_side), q, k


def attend(i, rows, qkv, key_add, query_one, context, log_totals):
    rs, cs = head_pair(i, rows)
    scores, _, _ = scores_of(rs, cs, qkv, key_add, query_one)
    top = jnp.max(scores, axis=0, keepdims=True)
    raised = jnp.exp(scores - top)
    total = jnp.sum(raised, axis=0, keepdims=True)
    shares = (raised * (1.0 / total)).astype(BF16)
    log_totals[i] = top + jnp.log(total)
    turned = dot_tn(qkv[2, rs, cs], shares)
    row = lax.broadcasted_iota(jnp.int32, (LANES, SLOTS), 0)
    context[rs, cs] = jnp.where(row < HEAD_DIM, turned[:, :SLOTS], turned[:, SLOTS:]).T.astype(BF16)


def attend_back(i, rows, qkv, key_add, query_one, log_totals, grad_context, grad_qkv):
    rs, cs = head_pair(i, rows)
    scores, q, k = scores_of(rs, cs, qkv, key_add, query_one)
    shares = jnp.exp(scores - log_totals[i])
    grad = split_heads(grad_context[rs, cs])
    grad_shares = dot_nt(qkv[2, rs, cs], grad)
    inner = jnp.sum(shares * grad_shares, axis=0, keepdims=True)
    grad_scores = (shares * (grad_shares - inner)).astype(BF16)
    grad_qkv[2, rs, cs] = dot_nn(shares.astype(BF16), grad).astype(BF16)
    grad_qkv[1, rs, cs] = dot_nn(grad_scores, split_heads(q)).astype(BF16)
    grad_qkv[0, rs, cs] = (join_heads(dot_tn(grad_scores, k)) * 0.125).astype(BF16)


def run_beside(count, body, steps):
    def turn(i, carry):
        body(i)
        for j, some in enumerate(steps):
            if some:

                @pl.when(i == j)
                def _(some=some):
                    for step in some:
                        step()

        return carry

    lax.fori_loop(0, count, turn, 0)


def after(code, steps):
    at = ORDER.index(code) + 1
    out = []
    while at < len(ORDER) and ORDER[at] >= 10000:
        out.append(steps[ORDER[at]])
        at += 1
    return out


def beside(kind, count, steps):
    return [after(kind + i, steps) for i in range(count)]


def run(steps):
    for step in steps:
        step()


def joint_weight(plan, ref, b):
    jr = plan.joint_rows
    return ref[0 : plan.joint_src, b * jr : (b + 1) * jr, :].reshape(D, D)


def out_weight(plan, ref):
    return ref[plan.joint_src : plan.n].reshape(D, D)


def in_weight(plan, ref, c):
    ir = plan.in_rows
    return ref[0 : plan.in_src, pl.ds(pl.multiple_of(c * ir, 16), ir), :].reshape(D, D)


def back_weight(plan, ref, c):
    return ref[back_blocks(plan, c)].reshape(D, D)


def back_blocks(plan, c):
    per = (plan.n - plan.in_src) // 4
    return pl.ds(plan.in_src + c * per, per)


def row_slots(r):
    return pl.ds(pl.multiple_of(r * SLOTS, 16), SLOTS)


def token_tiles(plan, size, fn):
    def one(t, carry):
        fn(pl.ds(pl.multiple_of(t * size, 16), size))
        return carry

    lax.fori_loop(0, plan.tokens // size, one, 0)


def gelu_with_slope(h):
    cdf = 0.5 * (1.0 + lax.erf(h * 0.7071067811865476))
    return h * cdf, cdf + h * jnp.exp(-0.5 * h * h) * 0.3989422804014327


def norm_parts(v):
    centred = v - row_mean(v)
    rstd = lax.rsqrt(row_mean(centred * centred) + NORM_EPS)
    return centred * rstd, rstd


def norm_back(grad, xhat, rstd):
    return rstd * (grad - row_mean(grad) - xhat * row_mean(grad * xhat))


def layer_kernel(plan, *refs):
    (x_in, ids, lens, shard_a, shard_f, out_grad_in) = refs[:6]
    (layer_out, in_grad, attn_grad, ffn_grad, bias_grad, params_far, qkv_far, context_far) = refs[6:14]
    (x, weights, active, slope, terms_f, norm_b, grad_hidden, grad_low, acc, xhat, rstd_first, log_totals, key_add,
     query_one, vec, vec_own, vec_held, joined_a, joined_f, halo_a, halo_f, end_a, end_f, vec_a, vec_b, got_a, got_b,
     got, out_a, out_f, send, recv, vec_send, vec_recv, local) = refs[14:49]
    room_f, room_1, room_2 = refs[49:57], refs[57:65], refs[65:73]
    n, nz, rows = plan.n, plan.nz, plan.rows
    place = Place(plan)
    me = place.me
    wire = Wire(send, recv)
    tail_a, tail_f = plan.tail_a, plan.tail_f
    hub_a, hub_b = plan.at_attn_vec[0], plan.at_bias_in[0]
    va, vf, gap = 5 * D // LANES, 3 * D // LANES, plan.gap
    bits = n.bit_length() - 1
    ra, half = plan.rows_a, D // 2
    jr, ir = plan.joint_rows, plan.in_rows
    per = (n - plan.in_src) // 4
    turns = HEADS // 2 * rows
    cols = [pl.ds(u * LANES, LANES) for u in range(6)]
    params = terms_f.at[:, 0:ra, :]
    qkv, context = slope.at[0:3], slope.at[3]
    out_grad = grad_hidden
    params_back = weights.at[:, 0:ra, :]
    terms_a = weights.at[:, ra : 2 * ra, :]
    qkv_back, context_back = active.at[0:3], active.at[3]
    grad_qkv, grad_context = slope.at[0:3], slope.at[3]

    base = [0]

    def numbers(count):
        base[0] += count
        return base[0] - count

    halo_in, halo_out = numbers(2), numbers(2)
    gather_a = Gather(place, wire, numbers(gather_count(nz)), params, *plan.part_a)
    gather_f = Gather(place, wire, numbers(gather_count(nz)), weights, *plan.part_f)
    scatter_f = Scatter(place, wire, numbers(scatter_count(nz)), terms_f, (0, D), *plan.part_f, room_f)
    scatter_1 = Scatter(place, wire, numbers(scatter_count(nz)), weights, (0, half), ra, *plan.part_a[1:], room_1)
    scatter_2 = Scatter(place, wire, numbers(scatter_count(nz)), weights, (half, half), ra, *plan.part_a[1:], room_2)
    vec_steps = add_over_all(place, wire, numbers(bits), vec_own, vec_held)
    movers = (None, gather_a, gather_f, scatter_f, scatter_1, scatter_2)
    steps = {}
    for code in ORDER:
        family, kind, number = code // 10000, code // 100 % 100, code % 100
        if family == 6:
            steps[code] = vec_steps[number]
        elif family:
            by_plane = () if family < 3 else (family == 3,)
            steps[code] = movers[family].step(kind, number, *by_plane)

    copies = {}

    def copy_here(name, src, dst):
        copies[name] = pltpu.make_async_copy(src, dst, local.at[len(copies)])

    copy_here("x", x_in, x)
    copy_here("out_grad", out_grad_in, out_grad)
    copy_here("params", params, params_far)
    copy_here("qkv", qkv, qkv_far)
    copy_here("context", context, context_far)
    copy_here("result", out_grad, layer_out)
    copy_here("params_back", params_far, params_back)
    copy_here("qkv_back", qkv_far, qkv_back)
    copy_here("context_back", context_far, context_back)
    copy_here("in_grad", acc, in_grad)
    entered = place.greet((hub_a, hub_b))
    copies["x"].start()
    copies["out_grad"].start()

    joined_a[tail_a : tail_a + plan.unit_a, :] = shard_a[...].astype(F32)
    joined_f[tail_f : tail_f + plan.unit_f, :] = shard_f[...].astype(F32)
    end_a[...] = joined_a[plan.unit_a : plan.unit_a + tail_a, :]
    end_f[...] = joined_f[plan.unit_f : plan.unit_f + tail_f, :]
    at = tail_a + plan.at_attn_vec[1]
    vec_a[0:va, :] = joined_a[at : at + va, :].astype(BF16)
    at = tail_f + plan.at_ffn_vec[1]
    vec_a[va : va + vf, :] = joined_f[at : at + vf, :].astype(BF16)
    at = tail_f + plan.at_bias_in[1]
    vec_b[...] = jnp.zeros_like(vec_b)
    vec_b[0:gap, :] = joined_f[at : at + gap, :].astype(BF16)
    entered()

    @pl.when(me < n - 1)
    def _():
        wire.copy(end_a, halo_a, halo_in, me + 1).start()
        wire.copy(end_f, halo_f, halo_in + 1, me + 1).start()

    def vec_copy(src, dst, which, partner):
        return pltpu.make_async_remote_copy(
            src_ref=src, dst_ref=dst, send_sem=vec_send.at[partner], recv_sem=vec_recv.at[which],
            device_id=(partner,), device_id_type=MESH,
        )

    def to_all(src, dst, which, fn):
        @pl.when(me == (hub_a, hub_b)[which])
        def _():
            def one(j, carry):
                pl.when(j != me)(lambda: fn(vec_copy(src, dst, which, j)))
                return carry

            lax.fori_loop(0, n, one, 0)

    to_all(vec_a, got_a, 0, lambda copy: copy.start())
    to_all(vec_b, got_b, 1, lambda copy: copy.start())

    @pl.when(me > 0)
    def _():
        wire.copy(end_a, halo_a, halo_in, me - 1).wait_recv()
        joined_a[0:tail_a, :] = halo_a[...]

    start = tail_a - plan.shift_a(me)
    mine = params.at[me]

    @pl.when(me < plan.joint_src)
    def _():
        for b in range(3):
            for u in range(6):
                mine[b * jr : (b + 1) * jr, cols[u]] = joined_a[
                    pl.ds(start + 6 * b + u, jr, stride=18), :
                ].astype(BF16)

    @pl.when(me >= plan.joint_src)
    def _():
        for u in range(6):
            mine[:, cols[u]] = joined_a[pl.ds(start + u, ra, stride=6), :].astype(BF16)

    run([steps[code] for code in ORDER[: ORDER.index(RELAY)]])

    @pl.when(me > 0)
    def _():
        wire.copy(end_f, halo_f, halo_in + 1, me - 1).wait_recv()
        joined_f[0:tail_f, :] = halo_f[...]

    start_f = tail_f - plan.shift_f(me)
    mine_f = weights.at[me]

    @pl.when(me < plan.in_src)
    def _():
        for c in range(4):
            for u in range(6):
                mine_f[c * ir : (c + 1) * ir, cols[u]] = joined_f[
                    pl.ds(start_f + 6 * c + u, ir, stride=24), :
                ].astype(BF16)

    @pl.when(me >= plan.in_src)
    def _():
        for u in range(6):
            mine_f[:, cols[u]] = joined_f[pl.ds(start_f + u, plan.rows_f, stride=6), :].astype(BF16)

    run(after(RELAY, steps))
    build_masks(plan, ids, lens, key_add, query_one)

    @pl.when(me == hub_a)
    def _():
        got_a[...] = vec_a[...]

    @pl.when(me == hub_b)
    def _():
        got_b[...] = vec_b[...]

    @pl.when(me != hub_a)
    def _():
        vec_copy(vec_a, got_a, 0, hub_a).wait_recv()

    @pl.when(me != hub_b)
    def _():
        vec_copy(vec_b, got_b, 1, hub_b).wait_recv()

    got[0 : va + vf, :] = got_a[0 : va + vf, :].astype(F32)
    got[va + vf : va + vf + gap, :] = got_b[0:gap, :].astype(F32)
    vec[...] = jnp.zeros_like(vec)
    for u in range(6):
        vec[0:5, cols[u]] = got[pl.ds(u, 5, stride=6), :]
        vec[9:12, cols[u]] = got[pl.ds(va + u, 3, stride=6), :]
        vec[5:9, cols[u]] = got[pl.ds(va + vf + u, 4, stride=6), :]

    copies["x"].wait()
    scale = jnp.asarray(HEAD_DIM ** (-0.5), BF16)
    held = D // (nz - 1)
    partial = (acc, xhat)
    project = [code for code in ORDER if PROJECT <= code < PROJECT + nz]
    for j, code in enumerate(project):
        z = code - PROJECT
        if z < nz - 1:
            blocks, columns = pl.ds(8 * z, 8), pl.ds(held * z, held)
            for b in range(2):
                now = dot_nn(x[:, columns], params[blocks, b * jr : (b + 1) * jr, :].reshape(held, D))
                if j > 0:
                    now = now + partial[b][...]
                if j < nz - 2:
                    partial[b][...] = now
                elif b == 0:
                    qkv[0] = (now + vec[0:1, :]).astype(BF16) * scale
                else:
                    qkv[1] = now.astype(BF16)
        else:
            qkv[2] = (dot_nn(x[...], joint_weight(plan, params, 2)) + vec[1:2, :]).astype(BF16)
        run(after(code, steps))
    copies["qkv"].start()
    pairs = turns // rows

    def attend_pair(i):
        for r in range(rows):
            attend(i * rows + r, rows, qkv, key_add, query_one, context, log_totals)

    run_beside(pairs, attend_pair, beside(ATTEND, pairs, steps))
    copies["params"].start()
    copies["context"].start()
    gain_first, shift_first, bias_back = vec[3:4, :], vec[4:5, :], vec[9:10, :]
    gain_second, shift_second = vec[10:11, :], vec[11:12, :]

    def norm(t):
        rs = row_slots(t)
        v = x[rs, :].astype(F32) + (dot_nn(context[rs, :], out_weight(plan, params)) + vec[2:3, :])
        now, rstd = norm_parts(v)
        xhat[rs, :] = now
        rstd_first[rs, :] = jnp.broadcast_to(rstd, (rstd.shape[0], LANES))
        v = now * gain_first + shift_first
        norm_b[rs, :] = v.astype(BF16)
        acc[rs, :] = v + bias_back

    run_beside(rows, norm, beside(NORM, rows, steps))

    copies["qkv"].wait()
    copies["context"].wait()

    def up(c):
        hidden = dot_nn(norm_b[...], in_weight(plan, weights, c)) + vec[pl.ds(5 + c, 1), :]
        value, incline = gelu_with_slope(hidden)
        active[c] = value.astype(BF16)
        slope[c] = incline.astype(BF16)

    run_beside(4, up, beside(UP, 4, steps))

    def down(c):
        acc[...] += dot_nn(active[c], back_weight(plan, weights, c))

    run_beside(4, down, beside(DOWN, 4, steps))
    copies["out_grad"].wait()
    grads = vec_own.at[0]
    grads[...] = jnp.zeros(grads.shape, F32)

    def turn(rs):
        now, rstd = norm_parts(acc[rs, :])
        cot = out_grad[rs, :].astype(F32)
        out_grad[rs, :] = (now * gain_second + shift_second).astype(BF16)
        grads[10:11, :] += col_sum(cot * now)
        grads[11:12, :] += col_sum(cot)
        grad = norm_back(cot * gain_second, now, rstd)
        acc[rs, :] = grad
        low = grad.astype(BF16)
        grad_low[rs, :] = low
        grads[9:10, :] += col_sum(low.astype(F32))

    token_tiles(plan, SLOTS, turn)
    copies["result"].start()
    copies["params"].wait()
    gather_a.drain()

    back_order = (2, 3, 0, 1)
    for c in back_order:
        terms_f[back_blocks(plan, c)] = (
            dot_tn(active[c], grad_low[...]).astype(BF16).reshape(per, plan.rows_f, D)
        )
        if c == back_order[1]:
            run(after(BACK_WEIGHT, steps))
    run(after(BACK_WEIGHT + 1, steps))
    copies["context_back"].start()
    copies["qkv_back"].start()
    copies["result"].wait()

    def hidden_back(i):
        c = i // 2

        @pl.when(i == 2 * c)
        def _():
            into_hidden = dot_nt(grad_low[...], back_weight(plan, weights, c))
            grad = (slope[c].astype(F32) * into_hidden).astype(BF16)
            grad_hidden[...] = grad
            grads[pl.ds(5 + c, 1), :] += col_sum(grad.astype(F32))
            acc[...] += dot_nt(grad, in_weight(plan, weights, c))

        @pl.when(i != 2 * c)
        def _():
            in_rows = pl.ds(pl.multiple_of(c * ir, 16), ir)
            terms_f[0 : plan.in_src, in_rows, :] = (
                dot_tn(norm_b[...], grad_hidden[...]).astype(BF16).reshape(plan.in_src, ir, D)
            )

    run_beside(8, hidden_back, beside(HIDDEN, 8, steps))
    gather_f.drain()
    copies["params_back"].start()

    def leave(rs):
        grad, now = acc[rs, :], xhat[rs, :]
        grads[3:4, :] += col_sum(grad * now)
        grads[4:5, :] += col_sum(grad)
        grad = norm_back(grad * gain_first, now, rstd_first[rs, 0:1])
        acc[rs, :] = grad
        grad = grad.astype(BF16)
        grad_low[rs, :] = grad
        grads[2:3, :] += col_sum(grad.astype(F32))

    token_tiles(plan, SLOTS, leave)
    run(after(LEAVE, steps))
    copies["params_back"].wait()

    def into_context(rs):
        grad_context[rs, :] = dot_nt(grad_low[rs, :], out_weight(plan, params_back)).astype(BF16)

    token_tiles(plan, SLOTS, into_context)
    run(after(LEAVE + 1, steps))
    copies["context_back"].wait()
    terms_a[plan.joint_src : n] = (
        dot_tn(context_back[...], grad_low[...]).astype(BF16).reshape(n - plan.joint_src, ra, D)
    )
    copies["qkv_back"].wait()
    run(after(LEAVE + 2, steps))

    def joint_terms(first):
        for b in range(3):
            terms_a[0 : plan.joint_src, b * jr : (b + 1) * jr, first : first + half] = (
                dot_tn(x[...], grad_qkv[b, :, first : first + half]).astype(BF16).reshape(plan.joint_src, jr, half)
            )

    def back_pair(i):
        for r in range(rows):
            attend_back(i * rows + r, rows, qkv_back, key_add, query_one, log_totals, grad_context, grad_qkv)

    beside_back = beside(ATTEND_BACK, pairs, steps)
    beside_back[pairs // 2 - 1] += [lambda: joint_terms(0)] + after(JOINT + 1, steps)
    run_beside(pairs, back_pair, beside_back)
    joint_terms(half)
    grads[0:1, :] = col_sum(grad_qkv[0].astype(F32))
    grads[1:2, :] = col_sum(grad_qkv[2].astype(F32))
    run(after(JOINT + 2, steps))

    def input_grad(rs):
        now = acc[rs, :]
        for b in range(3):
            now = now + dot_nt(grad_qkv[b, rs, :], joint_weight(plan, params_back, b))
        acc[rs, :] = now

    size = plan.tokens // 4
    for j in range(4):
        input_grad(pl.ds(j * size, size))
        if j == 3:
            copies["in_grad"].start()
        run(after(INPUT_GRAD + j, steps))

    summed = vec_own.at[bits]
    total_f, total_a = terms_f.at[me], terms_a.at[me]

    @pl.when(me < plan.in_src)
    def _():
        for c in range(4):
            for u in range(6):
                joined_f[pl.ds(6 * c + u, ir, stride=24), :] = total_f[c * ir : (c + 1) * ir, cols[u]].astype(F32)

    @pl.when(me >= plan.in_src)
    def _():
        for u in range(6):
            joined_f[pl.ds(u, plan.rows_f, stride=6), :] = total_f[:, cols[u]].astype(F32)

    @pl.when(me < plan.joint_src)
    def _():
        for b in range(3):
            for u in range(6):
                joined_a[pl.ds(6 * b + u, jr, stride=18), :] = total_a[b * jr : (b + 1) * jr, cols[u]].astype(F32)

    @pl.when(me >= plan.joint_src)
    def _():
        for u in range(6):
            joined_a[pl.ds(u, ra, stride=6), :] = total_a[:, cols[u]].astype(F32)

    head_a, head_f = joined_a.at[0:tail_a], joined_f.at[0:tail_f]

    @pl.when(me > 0)
    def _():
        wire.copy(head_f, out_f, halo_out + 1, me - 1).start()
        wire.copy(head_a, out_a, halo_out, me - 1).start()

    rest_a = pl.ds(plan.block_a, tail_a)
    rest_f = pl.ds(plan.block_f, tail_f)

    @pl.when(me < n - 1)
    def _():
        wire.copy(head_f, out_f, halo_out + 1, me + 1).wait_recv()
        wire.copy(head_a, out_a, halo_out, me + 1).wait_recv()
        joined_f[rest_f, :] = out_f[...]
        joined_a[rest_a, :] = out_a[...]

    @pl.when(me == hub_b)
    def _():
        for u in range(6):
            joined_f[pl.ds(plan.block_f + u, 4, stride=6), :] = summed[5:9, cols[u]]
        joined_f[plan.block_f + gap : plan.block_f + tail_f, :] = out_f[0 : tail_f - gap, :]

    @pl.when(me == n - 1)
    def _():
        joined_f[rest_f, :] = jnp.zeros((tail_f, LANES), F32)
        joined_a[rest_a, :] = jnp.zeros((tail_a, LANES), F32)
        for u in range(6):
            joined_f[pl.ds(plan.block_f + u, 3, stride=6), :] = summed[9:12, cols[u]]
            joined_a[pl.ds(plan.block_a + u, 5, stride=6), :] = summed[0:5, cols[u]]

    ffn_grad[...] = joined_f[pl.ds(plan.shift_f(me), plan.unit_f), :]
    attn_grad[...] = joined_a[pl.ds(plan.shift_a(me), plan.unit_a), :]
    for u in range(6):
        bias_grad[u : u + 1, :] = summed[2:3, cols[u]]
    copies["in_grad"].wait()
    for mover in (scatter_f, scatter_1, scatter_2):
        mover.drain()
    to_all(vec_a, got_a, 0, lambda copy: copy.wait_send())
    to_all(vec_b, got_b, 1, lambda copy: copy.wait_send())

    @pl.when(me < n - 1)
    def _():
        wire.copy(end_a, halo_a, halo_in, me + 1).wait_send()
        wire.copy(end_f, halo_f, halo_in + 1, me + 1).wait_send()

    @pl.when(me > 0)
    def _():
        wire.copy(head_f, out_f, halo_out + 1, me - 1).wait_send()
        wire.copy(head_a, out_a, halo_out, me - 1).wait_send()


def hand_over(*arrays):
    def kernel(*refs):
        for j in range(len(arrays)):
            refs[len(arrays) + j][...] = refs[j][...]

    parts = 2
    specs = []
    for array in arrays:
        count, width = array.shape
        if count % (16 * parts) == 0:
            specs.append(pl.BlockSpec((count // parts, width), lambda i: (i, 0)))
        else:
            specs.append(pl.BlockSpec((count, width), lambda i: (0, 0)))
    return pl.pallas_call(
        kernel,
        name="hand_over",
        grid=(parts,),
        out_shape=[jax.ShapeDtypeStruct(array.shape, array.dtype) for array in arrays],
        in_specs=specs,
        out_specs=specs,
    )(*arrays)


def fused_body(plan, layer_in, pair_ids, pair_lengths, attn_shard, ffn_shard, out_grad):
    n, t, nz = plan.n, plan.tokens, plan.nz
    shape = jax.ShapeDtypeStruct
    bits = n.bit_length() - 1
    turns = HEADS // 2 * plan.rows
    sems = 4 + bits + 2 * gather_count(nz) + 3 * scatter_count(nz)
    low, full = pltpu.VMEM((t, D), BF16), pltpu.VMEM((t, D), F32)
    blocks = pltpu.VMEM((n, plan.rows_f, D), BF16)
    wide = pltpu.VMEM((4, t, D), BF16)
    side = pltpu.VMEM((t, LANES), BF16)
    vmem, far = pl.BlockSpec(memory_space=pltpu.VMEM), pl.BlockSpec(memory_space=pl.ANY)

    def units(count):
        return pltpu.VMEM((count, LANES), F32)

    def low_units(count):
        return pltpu.VMEM((count, LANES), BF16)

    layer_out, in_grad, attn_grad, ffn_grad, bias_grad = pl.pallas_call(
        functools.partial(layer_kernel, plan),
        name="layer",
        out_shape=[
            shape((t, D), BF16),
            shape((t, D), F32),
            shape((plan.unit_a, LANES), F32),
            shape((plan.unit_f, LANES), F32),
            shape((D // LANES, LANES), F32),
            shape((n, plan.rows_a, D), BF16),
            shape((3, t, D), BF16),
            shape((t, D), BF16),
        ],
        in_specs=[far] + [vmem] * 4 + [far],
        out_specs=[far] * 2 + [vmem] * 3 + [far] * 3,
        scratch_shapes=[
            low, blocks, wide, wide, blocks, low, low, low, full, full,
            pltpu.VMEM((t, LANES), F32),
            pltpu.VMEM((turns, 1, 2 * SLOTS), F32),
            side, side,
            pltpu.VMEM((16, D), F32),
            pltpu.VMEM((bits + 1, 16, D), F32),
            pltpu.VMEM((bits, 16, D), F32),
            units(plan.tail_a + -(-plan.unit_a // 8) * 8 + 40),
            units(plan.tail_f + -(-plan.unit_f // 8) * 8 + 40),
            units(plan.tail_a), units(plan.tail_f), units(plan.tail_a), units(plan.tail_f),
            low_units(48), low_units(32), low_units(48), low_units(32),
            units(104), units(plan.tail_a), units(plan.tail_f),
            pltpu.SemaphoreType.DMA((sems,)),
            pltpu.SemaphoreType.DMA((sems,)),
            pltpu.SemaphoreType.DMA((n,)),
            pltpu.SemaphoreType.DMA((2,)),
            pltpu.SemaphoreType.DMA((12,)),
        ]
        + Scatter.rooms(nz, D, *plan.part_f)
        + Scatter.rooms(nz, D // 2, *plan.part_a)
        + Scatter.rooms(nz, D // 2, *plan.part_a),
        compiler_params=pltpu.CompilerParams(
            collective_id=0, has_side_effects=True, vmem_limit_bytes=VMEM_LIMIT
        ),
    )(
        layer_in.reshape(t, D),
        pair_ids,
        jnp.swapaxes(pair_lengths, 1, 2),
        attn_shard.reshape(plan.unit_a, LANES),
        ffn_shard.reshape(plan.unit_f, LANES),
        out_grad.reshape(t, D),
    )[:5]
    layer_out, in_grad, attn_grad, ffn_grad, bias_grad = hand_over(layer_out, in_grad, attn_grad, ffn_grad, bias_grad)
    return (
        layer_out.reshape(layer_in.shape),
        in_grad.reshape(layer_in.shape),
        attn_grad.reshape(-1),
        ffn_grad.reshape(-1),
        bias_grad.reshape(-1),
    )


def unpack_attention(flattened):
    offset = 3 * D * D
    weight_joint = flattened[:offset].reshape(D, 3 * D)
    weight_out = flattened[offset : offset + D * D].reshape(D, D)
    offset = offset + D * D
    vectors = flattened[offset : offset + 5 * D].reshape(5, D)
    return (weight_joint, weight_out, vectors[0], vectors[1], vectors[2], vectors[3], vectors[4])


def unpack_feedforward(flattened):
    offset = D * FF
    weight_in = flattened[:offset].reshape(D, FF)
    bias_in = flattened[offset : offset + FF]
    offset = offset + FF
    weight_back = flattened[offset : offset + FF * D].reshape(FF, D)
    offset = offset + FF * D
    vectors = flattened[offset : offset + 3 * D].reshape(3, D)
    return (weight_in, bias_in, weight_back, vectors[0], vectors[1], vectors[2])


def layer_norm(values, gain_vec, shift_vec):
    row_mean = jnp.mean(values, axis=-1, keepdims=True)
    centred = values - row_mean
    row_var = jnp.mean(centred * centred, axis=-1, keepdims=True)
    return centred * lax.rsqrt(row_var + NORM_EPS) * gain_vec + shift_vec


def exact_gelu(values):
    return jax.nn.gelu(values, approximate=False)


def key_mask(pair_ids, pair_lengths):
    labels = jnp.arange(PAIRS, dtype=jnp.int32)
    member = pair_ids[:, :, None] == labels[None, None, :]
    starts = jnp.sum((pair_ids[:, :, None] < labels[None, None, :]).astype(jnp.int32), axis=1)
    live_len = pair_lengths[:, :, 0] + pair_lengths[:, :, 1]
    slot_start = jnp.sum(jnp.where(member, starts[:, None, :], 0), axis=-1)
    slot_len = jnp.sum(jnp.where(member, live_len[:, None, :], 0), axis=-1)
    places = jnp.arange(pair_ids.shape[1], dtype=jnp.int32)[None, :]
    is_live = places - slot_start < slot_len
    return (pair_ids[:, :, None] == pair_ids[:, None, :]) & is_live[:, None, :]


def contract_rows(one_side, other_side):
    return lax.dot_general(
        one_side, other_side, (((0,), (0,)), ((), ())), preferred_element_type=jnp.float32
    )


def contract_cols(one_side, other_side):
    return lax.dot_general(
        one_side, other_side, (((1,), (1,)), ((), ())), preferred_element_type=jnp.float32
    )


def attend_forward(queries, key_rows, value_rows, key_ok, score_scale):

    def head_block(block_index):
        head_start = block_index * 4
        query_b = lax.dynamic_slice_in_dim(queries, head_start, 4, 2)
        key_b = lax.dynamic_slice_in_dim(key_rows, head_start, 4, 2)
        value_b = lax.dynamic_slice_in_dim(value_rows, head_start, 4, 2)
        scores = (
            jnp.einsum("rqhd,rkhd->rhqk", query_b, key_b, preferred_element_type=jnp.float32)
            * score_scale
        )
        scores = jnp.where(key_ok[:, None], scores, -1e30)
        row_max = jnp.max(scores, axis=-1, keepdims=True)
        raised = jnp.exp(scores - row_max)
        totals = jnp.sum(raised, axis=-1, keepdims=True)
        shares = (raised / totals).astype(jnp.bfloat16)
        context = jnp.einsum("rhqk,rkhd->rqhd", shares, value_b, preferred_element_type=jnp.float32)
        return (context, row_max + jnp.log(totals))

    return lax.map(head_block, jnp.arange(HEADS // 4))


def attend_backward(queries, key_rows, value_rows, grad_context, log_totals, key_ok, score_scale):

    def head_block(operands):
        block_index, log_total = operands
        head_start = block_index * 4
        query_b = lax.dynamic_slice_in_dim(queries, head_start, 4, 2)
        key_b = lax.dynamic_slice_in_dim(key_rows, head_start, 4, 2)
        value_b = lax.dynamic_slice_in_dim(value_rows, head_start, 4, 2)
        grad_block = lax.dynamic_slice_in_dim(grad_context, head_start, 4, 2)
        scores = (
            jnp.einsum("rqhd,rkhd->rhqk", query_b, key_b, preferred_element_type=jnp.float32)
            * score_scale
        )
        shares = jnp.where(key_ok[:, None], jnp.exp(scores - log_total), 0.0)
        grad_shares = jnp.einsum(
            "rqhd,rkhd->rhqk", grad_block, value_b, preferred_element_type=jnp.float32
        )
        inner_sum = jnp.sum(shares * grad_shares, axis=-1, keepdims=True)
        grad_scores = (shares * (grad_shares - inner_sum)).astype(jnp.bfloat16)
        grad_query = (
            jnp.einsum("rhqk,rkhd->rqhd", grad_scores, key_b, preferred_element_type=jnp.float32)
            * score_scale
        )
        grad_key = (
            jnp.einsum("rhqk,rqhd->rkhd", grad_scores, query_b, preferred_element_type=jnp.float32)
            * score_scale
        )
        grad_value = jnp.einsum(
            "rhqk,rqhd->rkhd",
            shares.astype(jnp.bfloat16),
            grad_block,
            preferred_element_type=jnp.float32,
        )
        return (grad_query, grad_key, grad_value)

    gradients = lax.map(head_block, (jnp.arange(HEADS // 4), log_totals))
    return [jnp.moveaxis(piece, 0, 2).reshape(-1, D) for piece in gradients]


def plain_body(layer_in, pair_ids, pair_lengths, attn_shard, ffn_shard, out_grad):
    row_count = layer_in.shape[0]
    tokens = row_count * SLOTS
    score_scale = HEAD_DIM ** (-0.5)
    key_ok = key_mask(pair_ids, pair_lengths)
    att_whole = lax.all_gather(attn_shard, "fsdp", axis=0, tiled=True)
    weight_joint, weight_out, bias_query, bias_value, bias_out, gain_first, shift_first = (
        unpack_attention(att_whole)
    )
    inputs = layer_in.reshape(tokens, D)
    bias_joint = jnp.concatenate([bias_query, jnp.zeros_like(bias_query), bias_value]).astype(
        jnp.float32
    )
    projected = (
        jnp.dot(inputs, weight_joint, preferred_element_type=jnp.float32) + bias_joint
    ).astype(jnp.bfloat16)
    projected = projected.reshape(row_count, SLOTS, 3, HEADS, HEAD_DIM)
    queries = projected[:, :, 0]
    key_rows = projected[:, :, 1]
    value_rows = projected[:, :, 2]
    contexts, log_totals = attend_forward(queries, key_rows, value_rows, key_ok, score_scale)
    context = jnp.moveaxis(contexts, 0, 2).reshape(tokens, D).astype(jnp.bfloat16)
    attn_out = jnp.dot(context, weight_out, preferred_element_type=jnp.float32) + bias_out.astype(
        jnp.float32
    )
    norm_first, first_pull = jax.vjp(
        layer_norm,
        inputs.astype(jnp.float32) + attn_out,
        gain_first.astype(jnp.float32),
        shift_first.astype(jnp.float32),
    )
    norm_first_b = norm_first.astype(jnp.bfloat16)
    feed_whole = lax.all_gather(ffn_shard, "fsdp", axis=0, tiled=True)
    weight_in, bias_in, weight_back, bias_back, gain_second, shift_second = unpack_feedforward(
        feed_whole
    )
    hidden = jnp.dot(norm_first_b, weight_in, preferred_element_type=jnp.float32) + bias_in.astype(
        jnp.float32
    )
    active, gelu_pull = jax.vjp(exact_gelu, hidden)
    active_b = active.astype(jnp.bfloat16)
    ffn_out = jnp.dot(active_b, weight_back, preferred_element_type=jnp.float32) + bias_back.astype(
        jnp.float32
    )
    result, second_pull = jax.vjp(
        layer_norm,
        norm_first + ffn_out,
        gain_second.astype(jnp.float32),
        shift_second.astype(jnp.float32),
    )
    layer_out = result.astype(jnp.bfloat16).reshape(row_count, SLOTS, D)
    feed_back = lax.all_gather(ffn_shard, "fsdp", axis=0, tiled=True)
    weight_in, bias_in, weight_back, bias_back, gain_second, shift_second = unpack_feedforward(
        feed_back
    )
    cotangent = out_grad.reshape(tokens, D).astype(jnp.float32)
    grad_sum_second, grad_gain_second, grad_shift_second = second_pull(cotangent)
    grad_ffn = grad_sum_second.astype(jnp.bfloat16)
    grad_bias_back = jnp.sum(grad_ffn.astype(jnp.float32), axis=0)
    grad_weight_back = contract_rows(active_b, grad_ffn)
    (grad_hidden,) = gelu_pull(contract_cols(grad_ffn, weight_back))
    grad_hidden = grad_hidden.astype(jnp.bfloat16)
    grad_bias_in = jnp.sum(grad_hidden.astype(jnp.float32), axis=0)
    grad_weight_in = contract_rows(norm_first_b, grad_hidden)
    grad_norm_first = grad_sum_second + contract_cols(grad_hidden, weight_in)
    grad_sum_first, grad_gain_first, grad_shift_first = first_pull(grad_norm_first)
    feed_pad = feed_back.shape[0] - (2 * D * FF + FF + 3 * D)
    feed_full = jnp.concatenate(
        [
            grad_weight_in.reshape(-1),
            grad_bias_in,
            grad_weight_back.reshape(-1),
            grad_bias_back,
            grad_gain_second,
            grad_shift_second,
            jnp.zeros((feed_pad,), jnp.float32),
        ]
    )
    ffn_grad = lax.psum_scatter(feed_full, "fsdp", scatter_dimension=0, tiled=True)
    att_back = lax.all_gather(attn_shard, "fsdp", axis=0, tiled=True)
    weight_joint, weight_out, bias_query, bias_value, bias_out, gain_first, shift_first = (
        unpack_attention(att_back)
    )
    grad_attn = grad_sum_first.astype(jnp.bfloat16)
    grad_bias_out = jnp.sum(grad_attn.astype(jnp.float32), axis=0)
    out_bias_grad = lax.psum(grad_bias_out, "fsdp")
    grad_weight_out = contract_rows(context, grad_attn)
    grad_context = (
        contract_cols(grad_attn, weight_out)
        .astype(jnp.bfloat16)
        .reshape(row_count, SLOTS, HEADS, HEAD_DIM)
    )
    grad_query, grad_key, grad_value = attend_backward(
        queries, key_rows, value_rows, grad_context, log_totals, key_ok, score_scale
    )
    grad_projected = jnp.concatenate([grad_query, grad_key, grad_value], axis=-1).astype(
        jnp.bfloat16
    )
    column_sums = jnp.sum(grad_projected.astype(jnp.float32), axis=0)
    grad_weight_joint = contract_rows(inputs, grad_projected)
    in_grad = grad_sum_first + contract_cols(grad_projected, weight_joint)
    att_pad = att_back.shape[0] - (4 * D * D + 5 * D)
    attn_full = jnp.concatenate(
        [
            grad_weight_joint.reshape(-1),
            grad_weight_out.reshape(-1),
            column_sums[:D],
            column_sums[2 * D :],
            grad_bias_out,
            grad_gain_first,
            grad_shift_first,
            jnp.zeros((att_pad,), jnp.float32),
        ]
    )
    attn_grad = lax.psum_scatter(attn_full, "fsdp", scatter_dimension=0, tiled=True)
    return (layer_out, in_grad.reshape(row_count, SLOTS, D), attn_grad, ffn_grad, out_bias_grad)


def body(layer_in, pair_ids, pair_lengths, attn_shard, ffn_shard, out_grad, devices):
    plan = Plan(devices, attn_shard.shape[0], ffn_shard.shape[0], layer_in.shape[0])
    run = functools.partial(fused_body, plan) if plan.fits() else plain_body
    return run(layer_in, pair_ids, pair_lengths, attn_shard, ffn_shard, out_grad)


def solution(mesh):
    placed = (
        P("fsdp", None, None),
        P("fsdp", None),
        P("fsdp", None, None),
        P("fsdp"),
        P("fsdp"),
        P("fsdp", None, None),
    )
    return jax.shard_map(
        functools.partial(body, devices=mesh.shape["fsdp"]),
        mesh=mesh,
        in_specs=placed,
        out_specs=(P("fsdp", None, None), P("fsdp", None, None), P("fsdp"), P("fsdp"), P()),
        check_vma=False,
    )
```

```python
import functools

import jax
import jax.numpy as jnp
from jax import lax
from jax.experimental import pallas as pl
from jax.experimental.pallas import tpu as pltpu
from jax.sharding import PartitionSpec as P

D = 768
HEADS = 12
HEAD_DIM = 64
FF = 3072
SLOTS = 416
PAIRS = 3
LANES = 128
NORM_EPS = 1e-12
F32 = jnp.float32
BF16 = jnp.bfloat16
MESH = pl.DeviceIdType.MESH
VMEM_LIMIT = 62 << 20
FINISH = 11
RELAY, PROJECT, ATTEND, NORM, UP, DOWN, TURN, BACK_WEIGHT, HIDDEN, LEAVE, ATTEND_BACK, JOINT, INPUT_GRAD = range(
    0, 1300, 100
)


def dot_nn(a, b):
    return lax.dot_general(a, b, (((1,), (0,)), ((), ())), preferred_element_type=F32)


def dot_nt(a, b):
    return lax.dot_general(a, b, (((1,), (1,)), ((), ())), preferred_element_type=F32)


def dot_tn(a, b):
    return lax.dot_general(a, b, (((0,), (0,)), ((), ())), preferred_element_type=F32)


def row_mean(v):
    return jnp.sum(v, axis=1, keepdims=True) * (1.0 / D)


def col_sum(v):
    return jnp.sum(v, axis=0, keepdims=True)


class Plan:
    def __init__(self, n, attn_shard_len, ffn_shard_len, row_count):
        self.n = n
        self.nz = n // 8
        self.rows = row_count
        self.tokens = row_count * SLOTS
        self.unit_a = attn_shard_len // LANES
        self.unit_f = ffn_shard_len // LANES
        self.block_a = 4 * D * D // LANES // n
        self.block_f = 2 * D * FF // LANES // n
        self.rows_a = 4 * D // n
        self.rows_f = 2 * FF // n
        self.joint_rows = self.rows_a // 3
        self.joint_src = 3 * n // 4
        self.in_rows = self.rows_f // 4
        self.in_src = n // 2
        self.part_a = (0, self.rows_a, 16, 32)
        self.part_f = (0, self.rows_f, 48, 64)
        self.gap = FF // LANES
        self.at_attn_vec = divmod(4 * D * D // LANES, self.unit_a)
        self.at_bias_in = divmod(D * FF // LANES, self.unit_f)
        self.at_ffn_vec = divmod(2 * D * FF // LANES + self.gap, self.unit_f)

    def shift_a(self, me):
        return me * (self.unit_a - self.block_a)

    def shift_f(self, me):
        return me * (self.unit_f - self.block_f) - jnp.where(me >= self.in_src, self.gap, 0)

    def fits(self):
        n = self.n
        if self.nz != 4 or n % 8 or self.rows_a % 48 or self.rows_f % 64:
            return False
        last_a = (n - 1) * (self.unit_a - self.block_a)
        step_f = self.unit_f - self.block_f
        last_f = max((self.in_src - 1) * step_f, (n - 1) * step_f - self.gap)
        first_f = self.in_src * step_f - self.gap
        self.tail_a = -(-(last_a + 1) // 8) * 8
        self.tail_f = -(-(last_f + 2) // 8) * 8
        vec_a, vec_f = 5 * D // LANES, 3 * D // LANES
        return (
            step_f >= 0
            and self.unit_a >= self.block_a
            and first_f >= 0
            and self.tail_a <= self.block_a
            and self.tail_f <= self.block_f
            and self.at_attn_vec[0] == n - 1
            and self.at_ffn_vec[0] == n - 1
            and self.at_bias_in[0] == self.in_src - 1
            and self.unit_a - self.at_attn_vec[1] <= self.tail_a
            and self.unit_f - self.at_ffn_vec[1] <= self.tail_f
            and self.at_attn_vec[1] + vec_a <= self.unit_a
            and self.at_ffn_vec[1] + vec_f <= self.unit_f
            and self.at_bias_in[1] + self.gap <= self.unit_f
            and self.at_bias_in[1] == self.block_f - (self.in_src - 1) * step_f
        )


class Place:
    def __init__(self, plan):
        self.n, self.nz = plan.n, plan.nz
        me = lax.axis_index("fsdp")
        self.me = me
        self.core = lax.rem(me, 2)
        self.x = lax.rem(me // 2, 2)
        self.y = lax.rem(me // 4, 2)
        self.z = me // 8
        self.sib = me + 1 - 2 * self.core
        self.xn = me + 2 - 4 * self.x
        self.yn = me + 4 - 8 * self.y

    def block(self, column, z, other_core=False):
        x = self.x if column in (0, 2) else 1 - self.x
        y = self.y if column in (0, 1) else 1 - self.y
        core = 1 - self.core if other_core else self.core
        return ((z * 2 + y) * 2 + x) * 2 + core

    def level(self, distance, fn):
        if distance == 0:
            fn(self.z)
            return
        pl.when(self.z >= distance)(lambda: fn(self.z - distance))
        pl.when(self.z + distance < self.nz)(lambda: fn(self.z + distance))

    def onward(self, z, fn):
        pl.when((z <= self.z) & (self.z < self.nz - 1))(lambda: fn(self.me + 8))
        pl.when((z >= self.z) & (self.z > 0))(lambda: fn(self.me - 8))

    def bits(self):
        out = []
        bit = 1
        while bit < self.n:
            out.append(self.me + bit - 2 * bit * lax.rem(self.me // bit, 2))
            bit *= 2
        return out

    def greet(self, hubs):
        sem = pltpu.get_barrier_semaphore()

        def tell(partner):
            pl.semaphore_signal(sem, inc=1, device_id=(partner,), device_id_type=MESH)

        fixed = self.bits()
        for partner in fixed:
            tell(partner)
        z_odd = lax.rem(self.z, 2)
        far_z = (self.z > 0) & (self.z < self.nz - 1)
        far = (self.me > 0) & (self.me < self.n - 1)
        pl.when(far_z)(lambda: tell(self.me - 8 + 16 * z_odd))
        pl.when(far)(lambda: tell(self.me - 1 + 2 * self.core))
        count = len(fixed) + far_z.astype(jnp.int32) + far.astype(jnp.int32)
        for hub in hubs:
            pl.when(self.me != hub)(lambda: tell(hub))
            count = count + jnp.where(self.me == hub, self.n - 1, 0)
        return lambda: pl.semaphore_wait(sem, count)


class Wire:
    def __init__(self, send, recv):
        self.send, self.recv = send, recv
        self.sent = []

    def copy(self, src, dst, number, partner):
        return pltpu.make_async_remote_copy(
            src_ref=src,
            dst_ref=dst,
            send_sem=self.send.at[number],
            recv_sem=self.recv.at[number],
            device_id=(partner,),
            device_id_type=MESH,
        )


def add_over_all(place, wire, base, own, held):
    partners = place.bits()

    def send(s):
        wire.copy(own.at[s], held.at[s], base + s, partners[s]).start()

    def take(s):
        wire.copy(own.at[s], held.at[s], base + s, partners[s]).wait()
        own[s + 1] = own[s] + held[s]

    steps = [lambda: send(0)]
    for s in range(len(partners)):

        def step(s=s):
            take(s)
            if s + 1 < len(partners):
                send(s + 1)

        steps.append(step)
    return steps


def gather_count(nz):
    return 17 * nz + 3


class Gather:
    def __init__(self, place, wire, base, ref, top, rows, late, half):
        self.p, self.w, self.ref = place, wire, ref
        nz = place.nz
        self.early = (top, rows - late)
        self.late = (top + rows - late, late)
        self.first = (top, half)
        self.second = (top + half, rows - late - half)
        at = [base]

        def take(count):
            at[0] += count
            return at[0] - count

        self.line, self.xs, self.ys, self.d1, self.d2 = (take(nz) for _ in range(5))
        self.sib, self.late_line, self.late_sib = (take(4 * nz) for _ in range(3))
        self.px, self.py, self.pd = (take(1) for _ in range(3))

    def move(self, column, z, part, number, partner):
        ref = self.ref.at[self.p.block(column, z), pl.ds(*part)]
        return self.w.copy(ref, ref, number, partner)

    def send(self, *args):
        self.move(*args).start()

    def wait(self, column, z, part, number):
        self.move(column, z, part, number, self.p.sib).wait_recv()

    def to_sib(self, column, z):
        self.send(column, z, self.early, self.sib + column * self.p.nz + z, self.p.sib)

    def spread(self, z):
        p = self.p
        p.onward(z, lambda partner: self.send(0, z, self.early, self.line + z, partner))
        self.send(0, z, self.early, self.xs + z, p.xn)
        self.send(0, z, self.early, self.ys + z, p.yn)
        self.to_sib(0, z)

    def spread_late(self, column, z):
        number = column * self.p.nz + z
        self.p.onward(
            z, lambda partner: self.send(column, z, self.late, self.late_line + number, partner)
        )
        self.send(column, z, self.late, self.late_sib + number, self.p.sib)

    def take_line(self, z):
        self.wait(0, z, self.early, self.line + z)
        self.spread(z)

    def take_x(self, z):
        self.wait(1, z, self.early, self.xs + z)
        self.send(1, z, self.first, self.d1 + z, self.p.yn)
        self.to_sib(1, z)

    def take_y(self, z):
        self.wait(2, z, self.early, self.ys + z)
        self.send(2, z, self.second, self.d2 + z, self.p.xn)
        self.to_sib(2, z)

    def take_corner(self, z):
        self.wait(3, z, self.first, self.d1 + z)
        self.wait(3, z, self.second, self.d2 + z)
        self.to_sib(3, z)

    def take_late(self, z):
        for column in range(4):
            self.wait(column, z, self.late, self.late_line + column * self.p.nz + z)
            self.spread_late(column, z)

    def begin(self):
        self.spread(self.p.z)

    def begin_late(self):
        p = self.p
        self.send(0, p.z, self.late, self.px, p.xn)
        self.send(0, p.z, self.late, self.py, p.yn)

    def late_x(self):
        self.wait(1, self.p.z, self.late, self.px)
        self.send(1, self.p.z, self.late, self.pd, self.p.yn)

    def late_y(self):
        self.wait(2, self.p.z, self.late, self.py)

    def late_corner(self):
        self.wait(3, self.p.z, self.late, self.pd)

    def step(self, kind, number):
        p = self.p
        plane, digit = number // 10, number % 10
        starts = (self.begin, self.begin_late, self.late_x, self.late_y, self.late_corner,
                  lambda: self.spread_late(digit, p.z))
        takes = (self.take_line, self.take_x, self.take_y, self.take_corner, self.take_late)
        if kind == FINISH:
            planes = range(plane, plane + digit)
            return lambda: self.finish(planes)
        if kind < len(starts):
            return lambda: pl.when(p.z == plane)(starts[kind])
        take = takes[kind - len(starts)]
        if digit:
            return lambda: pl.when((p.z == plane - digit) | (p.z == plane + digit))(lambda: take(plane))
        return lambda: take(plane)

    def finish(self, planes):
        p, nz = self.p, self.p.nz

        def one(j, carry):
            for column in range(4):
                ref = self.ref.at[p.block(column, j, True)]
                for part, base in ((self.early, self.sib), (self.late, self.late_sib)):
                    r = ref.at[pl.ds(*part)]
                    self.w.copy(r, r, base + column * nz + j, p.sib).wait_recv()
            return carry

        lax.fori_loop(planes[0], planes[-1] + 1, one, 0)

    def drain(self):
        p, nz = self.p, self.p.nz

        def sent(column, z, part, number):
            self.move(column, z, part, number, p.sib).wait_send()

        sent(0, p.z, self.late, self.px)
        sent(0, p.z, self.late, self.py)
        sent(1, p.z, self.late, self.pd)

        def one(z, carry):
            p.onward(z, lambda partner: sent(0, z, self.early, self.line + z))
            sent(0, z, self.early, self.xs + z)
            sent(0, z, self.early, self.ys + z)
            sent(1, z, self.first, self.d1 + z)
            sent(2, z, self.second, self.d2 + z)
            for column in range(4):
                number = column * nz + z
                sent(column, z, self.early, self.sib + number)
                sent(column, z, self.late, self.late_sib + number)
                p.onward(z, lambda partner: sent(column, z, self.late, self.late_line + number))
            return carry

        lax.fori_loop(0, nz, one, 0)


def gather_count(nz):
    return 17 * nz + 3


ORDER = (
    10030, 10000, 10500, 10010, 10510, 10020, 10120, 0, 10130, 10100, 20030, 20000, 20500, 20020, 20100,
    10110, 10200, 10601, 10501, 20130, 10300, 10621, 10631, 10210, 20010, 10230, 10220, 10611, 10502, 20530,
    10520, 10602, 10622, 10612, 10310, 10632, 10531, 10400, 10512, 10320, 10522, 10430, 10533, 10503, 10521,
    20520, 10603, 10420, 10523, 20200, 20120, 10410, 20501, 10513, 10810, 11002, 10511, 10330, 10633, 10820,
    10720, 11011, 10710, 11001, 10800, 20110, 20230, 10700, 10530, 20400, 20631, 11022, 11021, 10532, 20601,
    10730, 10830, 11012, 11003, 20220, 20521, 20602, 20300, 20621, 20503, 20502, 20310, 11031, 20512, 20330,
    10920, 10910, 20611, 20430, 10900, 20320, 11121, 11111, 20210, 20632, 20533, 11101, 20531, 20522, 100,
    20622, 21001, 102, 20532, 11032, 20510, 20603, 101, 103, 200, 10930, 20420, 20523, 20511, 20612, 20633,
    201, 21002, 11033, 11131, 20410, 20513, 21031, 20700, 21021, 20800, 202, 203, 20710, 20810, 20830,
    21011, 20730, 204, 20900, 20820, 21003, 21032, 205, 300, 20720, 21022, 20910, 301, 21012, 20930, 21102,
    400, 20920, 401, 21033, 21122, 402, 403, 500, 501, 502, 503, 600, 700, 30030, 701, 30020, 30230, 30130,
    30633, 800, 30220, 30120, 30622, 801, 802, 30430, 30330, 30320, 803, 30420, 30632, 804, 805, 806, 30533,
    30621, 807, 30000, 30010, 900, 30100, 901, 30200, 30110, 30603, 902, 30631, 30522, 30210, 30612, 30532,
    30300, 1000, 30400, 30410, 1001, 30602, 30310, 1002, 30630, 30503, 1101, 40001, 40002, 30611, 40003,
    30531, 30730, 1003, 30601, 40101, 30620, 30512, 30720, 40203, 30502, 40201, 40103, 40603, 30830, 1004,
    40403, 30521, 40102, 40401, 30610, 30710, 30820, 40301, 30511, 40303, 40202, 1005, 40302, 40402, 30501,
    1102, 50003, 30600, 40503, 60000, 30920, 50103, 30700, 30810, 30930, 30520, 30530, 50002, 50001, 40602,
    40000, 60001, 50203, 50603, 40502, 50102, 50303, 50403, 1200, 30800, 50101, 40100, 50202, 50602, 30510,
    60002, 50000, 50302, 40601, 30910, 50402, 50503, 50100, 30500, 30900, 50201, 40200, 50401, 50601, 50301,
    50200, 40600, 40700, 60003, 50502, 40501, 50600, 50700, 40300, 40400, 1201, 60004, 50400, 50300, 50501,
    40800, 50800, 1202, 1203, 40500, 40900, 60005, 50900, 50500,
)

class Scatter:
    def __init__(self, place, wire, base, terms, columns, top, rows, late, half, room):
        self.p, self.w, self.terms, self.columns = place, wire, terms, columns
        nz = place.nz
        self.whole = (top, rows)
        self.early = (top, rows - late)
        self.late = (top + rows - late, late)
        self.first = (top, half)
        self.second = (top + half, rows - late - half)
        (self.side, self.in_first, self.in_second, self.in_x, self.in_y, self.in_line, self.in_late,
         self.in_plane) = room
        at = [base]

        def take(count):
            at[0] += count
            return at[0] - count

        self.sib = take(4 * nz)
        self.d1, self.d2, self.xs, self.ys = (take(nz) for _ in range(4))
        self.line = take(nz + 1)
        self.late_line = take(4 * (nz + 1))
        self.plane = take(3)

    @staticmethod
    def rooms(nz, columns, top, rows, late, half):
        def room(count, size):
            return pltpu.VMEM((count, size, columns), BF16)

        early = rows - late
        return [
            room(4 * nz, rows), room(nz, half), room(nz, early - half), room(nz, early), room(nz, early),
            room(nz + 1, early), room(4 * (nz + 1), late), room(3, late),
        ]

    def slot(self, column, z):
        return column * self.p.nz + z

    def term(self, column, z, part, other_core=False):
        return self.terms.at[self.p.block(column, z, other_core), pl.ds(*part), pl.ds(*self.columns)]

    def add(self, target, term):
        count = target.shape[0]
        step = count if count <= 48 else next(s for s in (48, 32, 16) if count % s == 0)

        def some(i, carry):
            rs = pl.ds(pl.multiple_of(i * step, 16), step)
            target[rs, :] = target[rs, :] + term[rs, :]
            return carry

        lax.fori_loop(0, count // step, some, 0)

    def got(self, ref, number):
        self.w.copy(ref, ref, number, self.p.sib).wait_recv()
        return ref

    def send_sib(self, z):
        p = self.p
        for column in (3, 1, 2, 0):
            k = self.slot(column, z)
            self.w.copy(self.term(column, z, self.whole, True), self.side.at[k], self.sib + k, p.sib).start()

    def take_sib(self, column, z):
        k = self.slot(column, z)
        self.add(self.term(column, z, self.whole), self.got(self.side.at[k], self.sib + k))

    def corner(self, z):
        p = self.p
        self.take_sib(3, z)
        self.w.copy(self.term(3, z, self.first), self.in_first.at[z], self.d1 + z, p.yn).start()
        self.w.copy(self.term(3, z, self.second), self.in_second.at[z], self.d2 + z, p.xn).start()

    def take_rest(self, z):
        for column in (1, 2, 0):
            self.take_sib(column, z)

    def side_x(self, z):
        p = self.p
        self.add(self.term(1, z, self.first), self.got(self.in_first.at[z], self.d1 + z))
        self.w.copy(self.term(1, z, self.early), self.in_x.at[z], self.xs + z, p.xn).start()

    def side_y(self, z):
        p = self.p
        self.add(self.term(2, z, self.second), self.got(self.in_second.at[z], self.d2 + z))
        self.w.copy(self.term(2, z, self.early), self.in_y.at[z], self.ys + z, p.yn).start()

    def own(self, z):
        ref = self.term(0, z, self.early)
        self.add(ref, self.got(self.in_x.at[z], self.xs + z))
        self.add(ref, self.got(self.in_y.at[z], self.ys + z))
        self.along(z, ref, self.in_line, self.line, 0)

    def own_late(self, z):
        for column in range(4):
            self.along(z, self.term(column, z, self.late), self.in_late, self.late_line,
                       column * (self.p.nz + 1))

    def along(self, z, ref, room, number, at):
        p, nz = self.p, self.p.nz
        below, above = p.z > 0, p.z < nz - 1

        def take(slot):
            self.add(ref, self.got(room.at[at + slot], number + at + slot))

        def send(slot, partner):
            self.w.copy(ref, room.at[at + slot], number + at + slot, partner).start()

        pl.when((z >= p.z) & below)(lambda: take(z))
        pl.when((z < p.z) & above)(lambda: take(z))
        pl.when((z == p.z) & above)(lambda: take(nz))
        pl.when(z > p.z)(lambda: send(z, p.me + 8))
        pl.when(z < p.z)(lambda: send(jnp.where(z == p.z - 1, nz, z), p.me - 8))

    def plane_corner(self):
        p = self.p
        self.w.copy(self.term(3, p.z, self.late), self.in_plane.at[0], self.plane, p.yn).start()

    def plane_sides(self):
        p = self.p
        self.w.copy(self.term(2, p.z, self.late), self.in_plane.at[2], self.plane + 2, p.yn).start()
        ref = self.term(1, p.z, self.late)
        self.add(ref, self.got(self.in_plane.at[0], self.plane))
        self.w.copy(ref, self.in_plane.at[1], self.plane + 1, p.xn).start()

    def plane_own(self):
        ref = self.term(0, self.p.z, self.late)
        self.add(ref, self.got(self.in_plane.at[1], self.plane + 1))
        self.add(ref, self.got(self.in_plane.at[2], self.plane + 2))

    def step(self, kind, number, by_plane):
        p = self.p
        plane, digit = number // 10, number % 10
        takes = (self.send_sib, self.corner, self.take_rest, self.side_x, self.side_y, self.own, self.own_late)
        ends = (self.plane_corner, self.plane_sides, self.plane_own)
        if kind >= len(takes):
            end = ends[kind - len(takes)]
            return (lambda: pl.when(p.z == plane)(end)) if by_plane else end
        take = takes[kind]
        if not by_plane:
            return lambda: p.level(digit, take)
        if take in (self.own, self.own_late):
            return lambda: pl.when((p.z == plane - digit) | (p.z == plane + digit))(lambda: take(plane))
        return lambda: take(plane)

    def drain(self):
        p, nz = self.p, self.p.nz

        def sent(ref, number):
            self.w.copy(ref, ref, number, p.sib).wait_send()

        for i in range(3):
            sent(self.in_plane.at[i], self.plane + i)

        def one(z, carry):
            for column in range(4):
                k = self.slot(column, z)
                sent(self.side.at[k], self.sib + k)
            sent(self.in_first.at[z], self.d1 + z)
            sent(self.in_second.at[z], self.d2 + z)
            sent(self.in_x.at[z], self.xs + z)
            sent(self.in_y.at[z], self.ys + z)

            def lines(slot):
                sent(self.in_line.at[slot], self.line + slot)
                for column in range(4):
                    at = column * (nz + 1) + slot
                    sent(self.in_late.at[at], self.late_line + at)

            pl.when(z > p.z)(lambda: lines(z))
            pl.when(z < p.z)(lambda: lines(jnp.where(z == p.z - 1, nz, z)))
            return carry

        lax.fori_loop(0, nz, one, 0)


def scatter_count(nz):
    return 4 * nz + 4 * nz + nz + 1 + 4 * (nz + 1) + 3


def build_masks(plan, ids_ref, len_ref, key_add, query_one):
    for r in range(plan.rows):
        ids = jnp.broadcast_to(ids_ref[r : r + 1, :], (LANES, SLOTS))
        label = lax.broadcasted_iota(jnp.int32, (LANES, SLOTS), 0)
        place = lax.broadcasted_iota(jnp.int32, (LANES, SLOTS), 1)
        start = jnp.sum((ids < label).astype(F32), axis=1, keepdims=True)
        lengths = len_ref[r]
        lengths = lengths[0:1, :] + lengths[1:2, :]
        live = jnp.zeros((LANES, SLOTS), jnp.int32)
        for j in range(PAIRS):
            live = jnp.where(label == j, lengths[:, j : j + 1], live)
        same = ids == label
        ok = same & (place.astype(F32) - start < live.astype(F32))
        rs = pl.ds(r * SLOTS, SLOTS)
        key_add[rs, :] = jnp.where(ok | (label >= PAIRS), 0.0, -1e30).T.astype(BF16)
        query_one[rs, :] = same.astype(F32).T.astype(BF16)


def split_heads(v):
    lane = lax.broadcasted_iota(jnp.int32, v.shape, 1)
    zero = jnp.zeros_like(v)
    return jnp.concatenate(
        [jnp.where(lane < HEAD_DIM, v, zero), jnp.where(lane < HEAD_DIM, zero, v)], axis=0
    )


def join_heads(v):
    lane = lax.broadcasted_iota(jnp.int32, (SLOTS, LANES), 1)
    return jnp.where(lane < HEAD_DIM, v[:SLOTS], v[SLOTS:])


def head_pair(i, rows):
    r, p = lax.rem(i, rows), i // rows
    return (
        pl.ds(pl.multiple_of(r * SLOTS, 16), SLOTS),
        pl.ds(pl.multiple_of(p * LANES, LANES), LANES),
    )


def scores_of(rs, cs, qkv, key_add, query_one):
    q, k, one = qkv[0, rs, cs], qkv[1, rs, cs], query_one[rs, :]
    q_side = jnp.concatenate([split_heads(q), jnp.concatenate([one, one], axis=0)], axis=1)
    k_side = jnp.concatenate([k, key_add[rs, :]], axis=1)
    return dot_nt(k_side, q_side), q, k


def attend(i, rows, qkv, key_add, query_one, context, log_totals):
    rs, cs = head_pair(i, rows)
    scores, _, _ = scores_of(rs, cs, qkv, key_add, query_one)
    top = jnp.max(scores, axis=0, keepdims=True)
    raised = jnp.exp(scores - top)
    total = jnp.sum(raised, axis=0, keepdims=True)
    shares = (raised * (1.0 / total)).astype(BF16)
    log_totals[i] = top + jnp.log(total)
    turned = dot_tn(qkv[2, rs, cs], shares)
    row = lax.broadcasted_iota(jnp.int32, (LANES, SLOTS), 0)
    context[rs, cs] = jnp.where(row < HEAD_DIM, turned[:, :SLOTS], turned[:, SLOTS:]).T.astype(BF16)


def attend_back(i, rows, qkv, key_add, query_one, log_totals, grad_context, grad_qkv):
    rs, cs = head_pair(i, rows)
    scores, q, k = scores_of(rs, cs, qkv, key_add, query_one)
    shares = jnp.exp(scores - log_totals[i])
    grad = split_heads(grad_context[rs, cs])
    grad_shares = dot_nt(qkv[2, rs, cs], grad)
    inner = jnp.sum(shares * grad_shares, axis=0, keepdims=True)
    grad_scores = (shares * (grad_shares - inner)).astype(BF16)
    grad_qkv[2, rs, cs] = dot_nn(shares.astype(BF16), grad).astype(BF16)
    grad_qkv[1, rs, cs] = dot_nn(grad_scores, split_heads(q)).astype(BF16)
    grad_qkv[0, rs, cs] = (join_heads(dot_tn(grad_scores, k)) * 0.125).astype(BF16)


def run_beside(count, body, steps):
    def turn(i, carry):
        body(i)
        for j, some in enumerate(steps):
            if some:

                @pl.when(i == j)
                def _(some=some):
                    for step in some:
                        step()

        return carry

    lax.fori_loop(0, count, turn, 0)


def after(code, steps):
    at = ORDER.index(code) + 1
    out = []
    while at < len(ORDER) and ORDER[at] >= 10000:
        out.append(steps[ORDER[at]])
        at += 1
    return out


def beside(kind, count, steps):
    return [after(kind + i, steps) for i in range(count)]


def run(steps):
    for step in steps:
        step()


def joint_weight(plan, ref, b):
    jr = plan.joint_rows
    return ref[0 : plan.joint_src, b * jr : (b + 1) * jr, :].reshape(D, D)


def out_weight(plan, ref):
    return ref[plan.joint_src : plan.n].reshape(D, D)


def in_weight(plan, ref, c):
    ir = plan.in_rows
    return ref[0 : plan.in_src, pl.ds(pl.multiple_of(c * ir, 16), ir), :].reshape(D, D)


def back_weight(plan, ref, c):
    return ref[back_blocks(plan, c)].reshape(D, D)


def back_blocks(plan, c):
    per = (plan.n - plan.in_src) // 4
    return pl.ds(plan.in_src + c * per, per)


def row_slots(r):
    return pl.ds(pl.multiple_of(r * SLOTS, 16), SLOTS)


def token_tiles(plan, size, fn):
    def one(t, carry):
        fn(pl.ds(pl.multiple_of(t * size, 16), size))
        return carry

    lax.fori_loop(0, plan.tokens // size, one, 0)


def gelu_with_slope(h):
    cdf = 0.5 * (1.0 + lax.erf(h * 0.7071067811865476))
    return h * cdf, cdf + h * jnp.exp(-0.5 * h * h) * 0.3989422804014327


def norm_parts(v):
    centred = v - row_mean(v)
    rstd = lax.rsqrt(row_mean(centred * centred) + NORM_EPS)
    return centred * rstd, rstd


def norm_back(grad, xhat, rstd):
    return rstd * (grad - row_mean(grad) - xhat * row_mean(grad * xhat))


def layer_kernel(plan, *refs):
    (x_in, ids, lens, shard_a, shard_f, out_grad_in) = refs[:6]
    (layer_out, in_grad, attn_grad, ffn_grad, bias_grad, params_far, qkv_far, context_far) = refs[6:14]
    (x, weights, active, slope, terms_f, norm_b, grad_hidden, grad_low, acc, xhat, rstd_first, log_totals, key_add,
     query_one, vec, vec_own, vec_held, joined_a, joined_f, halo_a, halo_f, end_a, end_f, vec_a, vec_b, got_a, got_b,
     got, out_a, out_f, send, recv, vec_send, vec_recv, local) = refs[14:49]
    room_f, room_1, room_2 = refs[49:57], refs[57:65], refs[65:73]
    n, nz, rows = plan.n, plan.nz, plan.rows
    place = Place(plan)
    me = place.me
    wire = Wire(send, recv)
    tail_a, tail_f = plan.tail_a, plan.tail_f
    hub_a, hub_b = plan.at_attn_vec[0], plan.at_bias_in[0]
    va, vf, gap = 5 * D // LANES, 3 * D // LANES, plan.gap
    bits = n.bit_length() - 1
    ra, half = plan.rows_a, D // 2
    jr, ir = plan.joint_rows, plan.in_rows
    per = (n - plan.in_src) // 4
    turns = HEADS // 2 * rows
    cols = [pl.ds(u * LANES, LANES) for u in range(6)]
    params = terms_f.at[:, 0:ra, :]
    qkv, context = slope.at[0:3], slope.at[3]
    out_grad = grad_hidden
    params_back = weights.at[:, 0:ra, :]
    terms_a = weights.at[:, ra : 2 * ra, :]
    qkv_back, context_back = active.at[0:3], active.at[3]
    grad_qkv, grad_context = slope.at[0:3], slope.at[3]

    base = [0]

    def numbers(count):
        base[0] += count
        return base[0] - count

    halo_in, halo_out = numbers(2), numbers(2)
    gather_a = Gather(place, wire, numbers(gather_count(nz)), params, *plan.part_a)
    gather_f = Gather(place, wire, numbers(gather_count(nz)), weights, *plan.part_f)
    scatter_f = Scatter(place, wire, numbers(scatter_count(nz)), terms_f, (0, D), *plan.part_f, room_f)
    scatter_1 = Scatter(place, wire, numbers(scatter_count(nz)), weights, (0, half), ra, *plan.part_a[1:], room_1)
    scatter_2 = Scatter(place, wire, numbers(scatter_count(nz)), weights, (half, half), ra, *plan.part_a[1:], room_2)
    vec_steps = add_over_all(place, wire, numbers(bits), vec_own, vec_held)
    movers = (None, gather_a, gather_f, scatter_f, scatter_1, scatter_2)
    steps = {}
    for code in ORDER:
        family, kind, number = code // 10000, code // 100 % 100, code % 100
        if family == 6:
            steps[code] = vec_steps[number]
        elif family:
            by_plane = () if family < 3 else (family == 3,)
            steps[code] = movers[family].step(kind, number, *by_plane)

    copies = {}

    def copy_here(name, src, dst):
        copies[name] = pltpu.make_async_copy(src, dst, local.at[len(copies)])

    copy_here("x", x_in, x)
    copy_here("out_grad", out_grad_in, out_grad)
    copy_here("params", params, params_far)
    copy_here("qkv", qkv, qkv_far)
    copy_here("context", context, context_far)
    copy_here("result", out_grad, layer_out)
    copy_here("params_back", params_far, params_back)
    copy_here("qkv_back", qkv_far, qkv_back)
    copy_here("context_back", context_far, context_back)
    copy_here("in_grad", acc, in_grad)
    entered = place.greet((hub_a, hub_b))
    copies["x"].start()
    copies["out_grad"].start()

    joined_a[tail_a : tail_a + plan.unit_a, :] = shard_a[...].astype(F32)
    joined_f[tail_f : tail_f + plan.unit_f, :] = shard_f[...].astype(F32)
    end_a[...] = joined_a[plan.unit_a : plan.unit_a + tail_a, :]
    end_f[...] = joined_f[plan.unit_f : plan.unit_f + tail_f, :]
    at = tail_a + plan.at_attn_vec[1]
    vec_a[0:va, :] = joined_a[at : at + va, :].astype(BF16)
    at = tail_f + plan.at_ffn_vec[1]
    vec_a[va : va + vf, :] = joined_f[at : at + vf, :].astype(BF16)
    at = tail_f + plan.at_bias_in[1]
    vec_b[...] = jnp.zeros_like(vec_b)
    vec_b[0:gap, :] = joined_f[at : at + gap, :].astype(BF16)
    entered()

    @pl.when(me < n - 1)
    def _():
        wire.copy(end_a, halo_a, halo_in, me + 1).start()
        wire.copy(end_f, halo_f, halo_in + 1, me + 1).start()

    def vec_copy(src, dst, which, partner):
        return pltpu.make_async_remote_copy(
            src_ref=src, dst_ref=dst, send_sem=vec_send.at[partner], recv_sem=vec_recv.at[which],
            device_id=(partner,), device_id_type=MESH,
        )

    def to_all(src, dst, which, fn):
        @pl.when(me == (hub_a, hub_b)[which])
        def _():
            def one(j, carry):
                pl.when(j != me)(lambda: fn(vec_copy(src, dst, which, j)))
                return carry

            lax.fori_loop(0, n, one, 0)

    to_all(vec_a, got_a, 0, lambda copy: copy.start())
    to_all(vec_b, got_b, 1, lambda copy: copy.start())
    build_masks(plan, ids, lens, key_add, query_one)

    @pl.when(me > 0)
    def _():
        wire.copy(end_a, halo_a, halo_in, me - 1).wait_recv()
        joined_a[0:tail_a, :] = halo_a[...]

    start = tail_a - plan.shift_a(me)
    mine = params.at[me]

    @pl.when(me < plan.joint_src)
    def _():
        for b in range(3):
            for u in range(6):
                mine[b * jr : (b + 1) * jr, cols[u]] = joined_a[
                    pl.ds(start + 6 * b + u, jr, stride=18), :
                ].astype(BF16)

    @pl.when(me >= plan.joint_src)
    def _():
        for u in range(6):
            mine[:, cols[u]] = joined_a[pl.ds(start + u, ra, stride=6), :].astype(BF16)

    run([steps[code] for code in ORDER[: ORDER.index(RELAY)]])

    @pl.when(me > 0)
    def _():
        wire.copy(end_f, halo_f, halo_in + 1, me - 1).wait_recv()
        joined_f[0:tail_f, :] = halo_f[...]

    start_f = tail_f - plan.shift_f(me)
    mine_f = weights.at[me]

    @pl.when(me < plan.in_src)
    def _():
        for c in range(4):
            for u in range(6):
                mine_f[c * ir : (c + 1) * ir, cols[u]] = joined_f[
                    pl.ds(start_f + 6 * c + u, ir, stride=24), :
                ].astype(BF16)

    @pl.when(me >= plan.in_src)
    def _():
        for u in range(6):
            mine_f[:, cols[u]] = joined_f[pl.ds(start_f + u, plan.rows_f, stride=6), :].astype(BF16)

    run(after(RELAY, steps))

    @pl.when(me == hub_a)
    def _():
        got_a[...] = vec_a[...]

    @pl.when(me == hub_b)
    def _():
        got_b[...] = vec_b[...]

    @pl.when(me != hub_a)
    def _():
        vec_copy(vec_a, got_a, 0, hub_a).wait_recv()

    @pl.when(me != hub_b)
    def _():
        vec_copy(vec_b, got_b, 1, hub_b).wait_recv()

    got[0 : va + vf, :] = got_a[0 : va + vf, :].astype(F32)
    got[va + vf : va + vf + gap, :] = got_b[0:gap, :].astype(F32)
    vec[...] = jnp.zeros_like(vec)
    for u in range(6):
        vec[0:5, cols[u]] = got[pl.ds(u, 5, stride=6), :]
        vec[9:12, cols[u]] = got[pl.ds(va + u, 3, stride=6), :]
        vec[5:9, cols[u]] = got[pl.ds(va + vf + u, 4, stride=6), :]

    copies["x"].wait()
    scale = jnp.asarray(HEAD_DIM ** (-0.5), BF16)
    held = D // (nz - 1)
    partial = (acc, xhat)
    project = [code for code in ORDER if PROJECT <= code < PROJECT + nz]
    for j, code in enumerate(project):
        z = code - PROJECT
        if z < nz - 1:
            blocks, columns = pl.ds(8 * z, 8), pl.ds(held * z, held)
            for b in range(2):
                now = dot_nn(x[:, columns], params[blocks, b * jr : (b + 1) * jr, :].reshape(held, D))
                if j > 0:
                    now = now + partial[b][...]
                if j < nz - 2:
                    partial[b][...] = now
                elif b == 0:
                    qkv[0] = (now + vec[0:1, :]).astype(BF16) * scale
                else:
                    qkv[1] = now.astype(BF16)
        else:
            qkv[2] = (dot_nn(x[...], joint_weight(plan, params, 2)) + vec[1:2, :]).astype(BF16)
        run(after(code, steps))
    copies["qkv"].start()
    pairs = turns // rows

    def attend_pair(i):
        for r in range(rows):
            attend(i * rows + r, rows, qkv, key_add, query_one, context, log_totals)

    run_beside(pairs, attend_pair, beside(ATTEND, pairs, steps))
    copies["params"].start()
    copies["context"].start()
    gain_first, shift_first, bias_back = vec[3:4, :], vec[4:5, :], vec[9:10, :]
    gain_second, shift_second = vec[10:11, :], vec[11:12, :]

    def norm(t):
        rs = row_slots(t)
        v = x[rs, :].astype(F32) + (dot_nn(context[rs, :], out_weight(plan, params)) + vec[2:3, :])
        now, rstd = norm_parts(v)
        xhat[rs, :] = now
        rstd_first[rs, :] = jnp.broadcast_to(rstd, (rstd.shape[0], LANES))
        v = now * gain_first + shift_first
        norm_b[rs, :] = v.astype(BF16)
        acc[rs, :] = v + bias_back

    run_beside(rows, norm, beside(NORM, rows, steps))

    copies["qkv"].wait()
    copies["context"].wait()

    def up(c):
        hidden = dot_nn(norm_b[...], in_weight(plan, weights, c)) + vec[pl.ds(5 + c, 1), :]
        value, incline = gelu_with_slope(hidden)
        active[c] = value.astype(BF16)
        slope[c] = incline.astype(BF16)

    run_beside(4, up, beside(UP, 4, steps))

    def down(c):
        acc[...] += dot_nn(active[c], back_weight(plan, weights, c))

    run_beside(4, down, beside(DOWN, 4, steps))
    copies["out_grad"].wait()
    grads = vec_own.at[0]
    grads[...] = jnp.zeros(grads.shape, F32)

    def turn(rs):
        now, rstd = norm_parts(acc[rs, :])
        cot = out_grad[rs, :].astype(F32)
        out_grad[rs, :] = (now * gain_second + shift_second).astype(BF16)
        grads[10:11, :] += col_sum(cot * now)
        grads[11:12, :] += col_sum(cot)
        grad = norm_back(cot * gain_second, now, rstd)
        acc[rs, :] = grad
        low = grad.astype(BF16)
        grad_low[rs, :] = low
        grads[9:10, :] += col_sum(low.astype(F32))

    token_tiles(plan, SLOTS, turn)
    copies["result"].start()
    copies["params"].wait()
    gather_a.drain()

    back_order = (2, 3, 0, 1)
    for c in back_order:
        terms_f[back_blocks(plan, c)] = (
            dot_tn(active[c], grad_low[...]).astype(BF16).reshape(per, plan.rows_f, D)
        )
        if c == back_order[1]:
            run(after(BACK_WEIGHT, steps))
    run(after(BACK_WEIGHT + 1, steps))
    copies["context_back"].start()
    copies["qkv_back"].start()
    copies["result"].wait()

    def hidden_back(i):
        c = i // 2

        @pl.when(i == 2 * c)
        def _():
            into_hidden = dot_nt(grad_low[...], back_weight(plan, weights, c))
            grad = (slope[c].astype(F32) * into_hidden).astype(BF16)
            grad_hidden[...] = grad
            grads[pl.ds(5 + c, 1), :] += col_sum(grad.astype(F32))
            acc[...] += dot_nt(grad, in_weight(plan, weights, c))

        @pl.when(i != 2 * c)
        def _():
            in_rows = pl.ds(pl.multiple_of(c * ir, 16), ir)
            terms_f[0 : plan.in_src, in_rows, :] = (
                dot_tn(norm_b[...], grad_hidden[...]).astype(BF16).reshape(plan.in_src, ir, D)
            )

    run_beside(8, hidden_back, beside(HIDDEN, 8, steps))
    gather_f.drain()
    copies["params_back"].start()

    def leave(rs):
        grad, now = acc[rs, :], xhat[rs, :]
        grads[3:4, :] += col_sum(grad * now)
        grads[4:5, :] += col_sum(grad)
        grad = norm_back(grad * gain_first, now, rstd_first[rs, 0:1])
        acc[rs, :] = grad
        grad = grad.astype(BF16)
        grad_low[rs, :] = grad
        grads[2:3, :] += col_sum(grad.astype(F32))

    token_tiles(plan, SLOTS, leave)
    run(after(LEAVE, steps))
    copies["params_back"].wait()

    def into_context(rs):
        grad_context[rs, :] = dot_nt(grad_low[rs, :], out_weight(plan, params_back)).astype(BF16)

    token_tiles(plan, SLOTS, into_context)
    run(after(LEAVE + 1, steps))
    copies["context_back"].wait()
    terms_a[plan.joint_src : n] = (
        dot_tn(context_back[...], grad_low[...]).astype(BF16).reshape(n - plan.joint_src, ra, D)
    )
    copies["qkv_back"].wait()
    run(after(LEAVE + 2, steps))

    def joint_terms(first):
        for b in range(3):
            terms_a[0 : plan.joint_src, b * jr : (b + 1) * jr, first : first + half] = (
                dot_tn(x[...], grad_qkv[b, :, first : first + half]).astype(BF16).reshape(plan.joint_src, jr, half)
            )

    def back_pair(i):
        for r in range(rows):
            attend_back(i * rows + r, rows, qkv_back, key_add, query_one, log_totals, grad_context, grad_qkv)

    beside_back = beside(ATTEND_BACK, pairs, steps)
    beside_back[pairs // 2 - 1] += [lambda: joint_terms(0)] + after(JOINT + 1, steps)
    run_beside(pairs, back_pair, beside_back)
    joint_terms(half)
    grads[0:1, :] = col_sum(grad_qkv[0].astype(F32))
    grads[1:2, :] = col_sum(grad_qkv[2].astype(F32))
    run(after(JOINT + 2, steps))

    def input_grad(rs):
        now = acc[rs, :]
        for b in range(3):
            now = now + dot_nt(grad_qkv[b, rs, :], joint_weight(plan, params_back, b))
        acc[rs, :] = now

    size = plan.tokens // 4
    for j in range(4):
        input_grad(pl.ds(j * size, size))
        if j == 3:
            copies["in_grad"].start()
        run(after(INPUT_GRAD + j, steps))

    summed = vec_own.at[bits]
    total_f, total_a = terms_f.at[me], terms_a.at[me]

    @pl.when(me < plan.in_src)
    def _():
        for c in range(4):
            for u in range(6):
                joined_f[pl.ds(6 * c + u, ir, stride=24), :] = total_f[c * ir : (c + 1) * ir, cols[u]].astype(F32)

    @pl.when(me >= plan.in_src)
    def _():
        for u in range(6):
            joined_f[pl.ds(u, plan.rows_f, stride=6), :] = total_f[:, cols[u]].astype(F32)

    @pl.when(me < plan.joint_src)
    def _():
        for b in range(3):
            for u in range(6):
                joined_a[pl.ds(6 * b + u, jr, stride=18), :] = total_a[b * jr : (b + 1) * jr, cols[u]].astype(F32)

    @pl.when(me >= plan.joint_src)
    def _():
        for u in range(6):
            joined_a[pl.ds(u, ra, stride=6), :] = total_a[:, cols[u]].astype(F32)

    head_a, head_f = joined_a.at[0:tail_a], joined_f.at[0:tail_f]

    @pl.when(me > 0)
    def _():
        wire.copy(head_f, out_f, halo_out + 1, me - 1).start()
        wire.copy(head_a, out_a, halo_out, me - 1).start()

    rest_a = pl.ds(plan.block_a, tail_a)
    rest_f = pl.ds(plan.block_f, tail_f)

    @pl.when(me < n - 1)
    def _():
        wire.copy(head_f, out_f, halo_out + 1, me + 1).wait_recv()
        wire.copy(head_a, out_a, halo_out, me + 1).wait_recv()
        joined_f[rest_f, :] = out_f[...]
        joined_a[rest_a, :] = out_a[...]

    @pl.when(me == hub_b)
    def _():
        for u in range(6):
            joined_f[pl.ds(plan.block_f + u, 4, stride=6), :] = summed[5:9, cols[u]]
        joined_f[plan.block_f + gap : plan.block_f + tail_f, :] = out_f[0 : tail_f - gap, :]

    @pl.when(me == n - 1)
    def _():
        joined_f[rest_f, :] = jnp.zeros((tail_f, LANES), F32)
        joined_a[rest_a, :] = jnp.zeros((tail_a, LANES), F32)
        for u in range(6):
            joined_f[pl.ds(plan.block_f + u, 3, stride=6), :] = summed[9:12, cols[u]]
            joined_a[pl.ds(plan.block_a + u, 5, stride=6), :] = summed[0:5, cols[u]]

    ffn_grad[...] = joined_f[pl.ds(plan.shift_f(me), plan.unit_f), :]
    attn_grad[...] = joined_a[pl.ds(plan.shift_a(me), plan.unit_a), :]
    for u in range(6):
        bias_grad[u : u + 1, :] = summed[2:3, cols[u]]
    copies["in_grad"].wait()
    for mover in (scatter_f, scatter_1, scatter_2):
        mover.drain()
    to_all(vec_a, got_a, 0, lambda copy: copy.wait_send())
    to_all(vec_b, got_b, 1, lambda copy: copy.wait_send())

    @pl.when(me < n - 1)
    def _():
        wire.copy(end_a, halo_a, halo_in, me + 1).wait_send()
        wire.copy(end_f, halo_f, halo_in + 1, me + 1).wait_send()

    @pl.when(me > 0)
    def _():
        wire.copy(head_f, out_f, halo_out + 1, me - 1).wait_send()
        wire.copy(head_a, out_a, halo_out, me - 1).wait_send()


def hand_over(*arrays):
    def kernel(*refs):
        for j in range(len(arrays)):
            refs[len(arrays) + j][...] = refs[j][...]

    parts = 2
    specs = []
    for array in arrays:
        count, width = array.shape
        if count % (16 * parts) == 0:
            specs.append(pl.BlockSpec((count // parts, width), lambda i: (i, 0)))
        else:
            specs.append(pl.BlockSpec((count, width), lambda i: (0, 0)))
    return pl.pallas_call(
        kernel,
        name="hand_over",
        grid=(parts,),
        out_shape=[jax.ShapeDtypeStruct(array.shape, array.dtype) for array in arrays],
        in_specs=specs,
        out_specs=specs,
    )(*arrays)


def fused_body(plan, layer_in, pair_ids, pair_lengths, attn_shard, ffn_shard, out_grad):
    n, t, nz = plan.n, plan.tokens, plan.nz
    shape = jax.ShapeDtypeStruct
    bits = n.bit_length() - 1
    turns = HEADS // 2 * plan.rows
    sems = 4 + bits + 2 * gather_count(nz) + 3 * scatter_count(nz)
    low, full = pltpu.VMEM((t, D), BF16), pltpu.VMEM((t, D), F32)
    blocks = pltpu.VMEM((n, plan.rows_f, D), BF16)
    wide = pltpu.VMEM((4, t, D), BF16)
    side = pltpu.VMEM((t, LANES), BF16)
    vmem, far = pl.BlockSpec(memory_space=pltpu.VMEM), pl.BlockSpec(memory_space=pl.ANY)

    def units(count):
        return pltpu.VMEM((count, LANES), F32)

    def low_units(count):
        return pltpu.VMEM((count, LANES), BF16)

    layer_out, in_grad, attn_grad, ffn_grad, bias_grad = pl.pallas_call(
        functools.partial(layer_kernel, plan),
        name="layer",
        out_shape=[
            shape((t, D), BF16),
            shape((t, D), F32),
            shape((plan.unit_a, LANES), F32),
            shape((plan.unit_f, LANES), F32),
            shape((D // LANES, LANES), F32),
            shape((n, plan.rows_a, D), BF16),
            shape((3, t, D), BF16),
            shape((t, D), BF16),
        ],
        in_specs=[far] + [vmem] * 4 + [far],
        out_specs=[far] * 2 + [vmem] * 3 + [far] * 3,
        scratch_shapes=[
            low, blocks, wide, wide, blocks, low, low, low, full, full,
            pltpu.VMEM((t, LANES), F32),
            pltpu.VMEM((turns, 1, 2 * SLOTS), F32),
            side, side,
            pltpu.VMEM((16, D), F32),
            pltpu.VMEM((bits + 1, 16, D), F32),
            pltpu.VMEM((bits, 16, D), F32),
            units(plan.tail_a + -(-plan.unit_a // 8) * 8 + 40),
            units(plan.tail_f + -(-plan.unit_f // 8) * 8 + 40),
            units(plan.tail_a), units(plan.tail_f), units(plan.tail_a), units(plan.tail_f),
            low_units(48), low_units(32), low_units(48), low_units(32),
            units(104), units(plan.tail_a), units(plan.tail_f),
            pltpu.SemaphoreType.DMA((sems,)),
            pltpu.SemaphoreType.DMA((sems,)),
            pltpu.SemaphoreType.DMA((n,)),
            pltpu.SemaphoreType.DMA((2,)),
            pltpu.SemaphoreType.DMA((12,)),
        ]
        + Scatter.rooms(nz, D, *plan.part_f)
        + Scatter.rooms(nz, D // 2, *plan.part_a)
        + Scatter.rooms(nz, D // 2, *plan.part_a),
        compiler_params=pltpu.CompilerParams(
            collective_id=0, has_side_effects=True, vmem_limit_bytes=VMEM_LIMIT
        ),
    )(
        layer_in.reshape(t, D),
        pair_ids,
        jnp.swapaxes(pair_lengths, 1, 2),
        attn_shard.reshape(plan.unit_a, LANES),
        ffn_shard.reshape(plan.unit_f, LANES),
        out_grad.reshape(t, D),
    )[:5]
    layer_out, in_grad, attn_grad, ffn_grad, bias_grad = hand_over(layer_out, in_grad, attn_grad, ffn_grad, bias_grad)
    return (
        layer_out.reshape(layer_in.shape),
        in_grad.reshape(layer_in.shape),
        attn_grad.reshape(-1),
        ffn_grad.reshape(-1),
        bias_grad.reshape(-1),
    )


def unpack_attention(flattened):
    offset = 3 * D * D
    weight_joint = flattened[:offset].reshape(D, 3 * D)
    weight_out = flattened[offset : offset + D * D].reshape(D, D)
    offset = offset + D * D
    vectors = flattened[offset : offset + 5 * D].reshape(5, D)
    return (weight_joint, weight_out, vectors[0], vectors[1], vectors[2], vectors[3], vectors[4])


def unpack_feedforward(flattened):
    offset = D * FF
    weight_in = flattened[:offset].reshape(D, FF)
    bias_in = flattened[offset : offset + FF]
    offset = offset + FF
    weight_back = flattened[offset : offset + FF * D].reshape(FF, D)
    offset = offset + FF * D
    vectors = flattened[offset : offset + 3 * D].reshape(3, D)
    return (weight_in, bias_in, weight_back, vectors[0], vectors[1], vectors[2])


def layer_norm(values, gain_vec, shift_vec):
    row_mean = jnp.mean(values, axis=-1, keepdims=True)
    centred = values - row_mean
    row_var = jnp.mean(centred * centred, axis=-1, keepdims=True)
    return centred * lax.rsqrt(row_var + NORM_EPS) * gain_vec + shift_vec


def exact_gelu(values):
    return jax.nn.gelu(values, approximate=False)


def key_mask(pair_ids, pair_lengths):
    labels = jnp.arange(PAIRS, dtype=jnp.int32)
    member = pair_ids[:, :, None] == labels[None, None, :]
    starts = jnp.sum((pair_ids[:, :, None] < labels[None, None, :]).astype(jnp.int32), axis=1)
    live_len = pair_lengths[:, :, 0] + pair_lengths[:, :, 1]
    slot_start = jnp.sum(jnp.where(member, starts[:, None, :], 0), axis=-1)
    slot_len = jnp.sum(jnp.where(member, live_len[:, None, :], 0), axis=-1)
    places = jnp.arange(pair_ids.shape[1], dtype=jnp.int32)[None, :]
    is_live = places - slot_start < slot_len
    return (pair_ids[:, :, None] == pair_ids[:, None, :]) & is_live[:, None, :]


def contract_rows(one_side, other_side):
    return lax.dot_general(
        one_side, other_side, (((0,), (0,)), ((), ())), preferred_element_type=jnp.float32
    )


def contract_cols(one_side, other_side):
    return lax.dot_general(
        one_side, other_side, (((1,), (1,)), ((), ())), preferred_element_type=jnp.float32
    )


def attend_forward(queries, key_rows, value_rows, key_ok, score_scale):

    def head_block(block_index):
        head_start = block_index * 4
        query_b = lax.dynamic_slice_in_dim(queries, head_start, 4, 2)
        key_b = lax.dynamic_slice_in_dim(key_rows, head_start, 4, 2)
        value_b = lax.dynamic_slice_in_dim(value_rows, head_start, 4, 2)
        scores = (
            jnp.einsum("rqhd,rkhd->rhqk", query_b, key_b, preferred_element_type=jnp.float32)
            * score_scale
        )
        scores = jnp.where(key_ok[:, None], scores, -1e30)
        row_max = jnp.max(scores, axis=-1, keepdims=True)
        raised = jnp.exp(scores - row_max)
        totals = jnp.sum(raised, axis=-1, keepdims=True)
        shares = (raised / totals).astype(jnp.bfloat16)
        context = jnp.einsum("rhqk,rkhd->rqhd", shares, value_b, preferred_element_type=jnp.float32)
        return (context, row_max + jnp.log(totals))

    return lax.map(head_block, jnp.arange(HEADS // 4))


def attend_backward(queries, key_rows, value_rows, grad_context, log_totals, key_ok, score_scale):

    def head_block(operands):
        block_index, log_total = operands
        head_start = block_index * 4
        query_b = lax.dynamic_slice_in_dim(queries, head_start, 4, 2)
        key_b = lax.dynamic_slice_in_dim(key_rows, head_start, 4, 2)
        value_b = lax.dynamic_slice_in_dim(value_rows, head_start, 4, 2)
        grad_block = lax.dynamic_slice_in_dim(grad_context, head_start, 4, 2)
        scores = (
            jnp.einsum("rqhd,rkhd->rhqk", query_b, key_b, preferred_element_type=jnp.float32)
            * score_scale
        )
        shares = jnp.where(key_ok[:, None], jnp.exp(scores - log_total), 0.0)
        grad_shares = jnp.einsum(
            "rqhd,rkhd->rhqk", grad_block, value_b, preferred_element_type=jnp.float32
        )
        inner_sum = jnp.sum(shares * grad_shares, axis=-1, keepdims=True)
        grad_scores = (shares * (grad_shares - inner_sum)).astype(jnp.bfloat16)
        grad_query = (
            jnp.einsum("rhqk,rkhd->rqhd", grad_scores, key_b, preferred_element_type=jnp.float32)
            * score_scale
        )
        grad_key = (
            jnp.einsum("rhqk,rqhd->rkhd", grad_scores, query_b, preferred_element_type=jnp.float32)
            * score_scale
        )
        grad_value = jnp.einsum(
            "rhqk,rqhd->rkhd",
            shares.astype(jnp.bfloat16),
            grad_block,
            preferred_element_type=jnp.float32,
        )
        return (grad_query, grad_key, grad_value)

    gradients = lax.map(head_block, (jnp.arange(HEADS // 4), log_totals))
    return [jnp.moveaxis(piece, 0, 2).reshape(-1, D) for piece in gradients]


def plain_body(layer_in, pair_ids, pair_lengths, attn_shard, ffn_shard, out_grad):
    row_count = layer_in.shape[0]
    tokens = row_count * SLOTS
    score_scale = HEAD_DIM ** (-0.5)
    key_ok = key_mask(pair_ids, pair_lengths)
    att_whole = lax.all_gather(attn_shard, "fsdp", axis=0, tiled=True)
    weight_joint, weight_out, bias_query, bias_value, bias_out, gain_first, shift_first = (
        unpack_attention(att_whole)
    )
    inputs = layer_in.reshape(tokens, D)
    bias_joint = jnp.concatenate([bias_query, jnp.zeros_like(bias_query), bias_value]).astype(
        jnp.float32
    )
    projected = (
        jnp.dot(inputs, weight_joint, preferred_element_type=jnp.float32) + bias_joint
    ).astype(jnp.bfloat16)
    projected = projected.reshape(row_count, SLOTS, 3, HEADS, HEAD_DIM)
    queries = projected[:, :, 0]
    key_rows = projected[:, :, 1]
    value_rows = projected[:, :, 2]
    contexts, log_totals = attend_forward(queries, key_rows, value_rows, key_ok, score_scale)
    context = jnp.moveaxis(contexts, 0, 2).reshape(tokens, D).astype(jnp.bfloat16)
    attn_out = jnp.dot(context, weight_out, preferred_element_type=jnp.float32) + bias_out.astype(
        jnp.float32
    )
    norm_first, first_pull = jax.vjp(
        layer_norm,
        inputs.astype(jnp.float32) + attn_out,
        gain_first.astype(jnp.float32),
        shift_first.astype(jnp.float32),
    )
    norm_first_b = norm_first.astype(jnp.bfloat16)
    feed_whole = lax.all_gather(ffn_shard, "fsdp", axis=0, tiled=True)
    weight_in, bias_in, weight_back, bias_back, gain_second, shift_second = unpack_feedforward(
        feed_whole
    )
    hidden = jnp.dot(norm_first_b, weight_in, preferred_element_type=jnp.float32) + bias_in.astype(
        jnp.float32
    )
    active, gelu_pull = jax.vjp(exact_gelu, hidden)
    active_b = active.astype(jnp.bfloat16)
    ffn_out = jnp.dot(active_b, weight_back, preferred_element_type=jnp.float32) + bias_back.astype(
        jnp.float32
    )
    result, second_pull = jax.vjp(
        layer_norm,
        norm_first + ffn_out,
        gain_second.astype(jnp.float32),
        shift_second.astype(jnp.float32),
    )
    layer_out = result.astype(jnp.bfloat16).reshape(row_count, SLOTS, D)
    feed_back = lax.all_gather(ffn_shard, "fsdp", axis=0, tiled=True)
    weight_in, bias_in, weight_back, bias_back, gain_second, shift_second = unpack_feedforward(
        feed_back
    )
    cotangent = out_grad.reshape(tokens, D).astype(jnp.float32)
    grad_sum_second, grad_gain_second, grad_shift_second = second_pull(cotangent)
    grad_ffn = grad_sum_second.astype(jnp.bfloat16)
    grad_bias_back = jnp.sum(grad_ffn.astype(jnp.float32), axis=0)
    grad_weight_back = contract_rows(active_b, grad_ffn)
    (grad_hidden,) = gelu_pull(contract_cols(grad_ffn, weight_back))
    grad_hidden = grad_hidden.astype(jnp.bfloat16)
    grad_bias_in = jnp.sum(grad_hidden.astype(jnp.float32), axis=0)
    grad_weight_in = contract_rows(norm_first_b, grad_hidden)
    grad_norm_first = grad_sum_second + contract_cols(grad_hidden, weight_in)
    grad_sum_first, grad_gain_first, grad_shift_first = first_pull(grad_norm_first)
    feed_pad = feed_back.shape[0] - (2 * D * FF + FF + 3 * D)
    feed_full = jnp.concatenate(
        [
            grad_weight_in.reshape(-1),
            grad_bias_in,
            grad_weight_back.reshape(-1),
            grad_bias_back,
            grad_gain_second,
            grad_shift_second,
            jnp.zeros((feed_pad,), jnp.float32),
        ]
    )
    ffn_grad = lax.psum_scatter(feed_full, "fsdp", scatter_dimension=0, tiled=True)
    att_back = lax.all_gather(attn_shard, "fsdp", axis=0, tiled=True)
    weight_joint, weight_out, bias_query, bias_value, bias_out, gain_first, shift_first = (
        unpack_attention(att_back)
    )
    grad_attn = grad_sum_first.astype(jnp.bfloat16)
    grad_bias_out = jnp.sum(grad_attn.astype(jnp.float32), axis=0)
    out_bias_grad = lax.psum(grad_bias_out, "fsdp")
    grad_weight_out = contract_rows(context, grad_attn)
    grad_context = (
        contract_cols(grad_attn, weight_out)
        .astype(jnp.bfloat16)
        .reshape(row_count, SLOTS, HEADS, HEAD_DIM)
    )
    grad_query, grad_key, grad_value = attend_backward(
        queries, key_rows, value_rows, grad_context, log_totals, key_ok, score_scale
    )
    grad_projected = jnp.concatenate([grad_query, grad_key, grad_value], axis=-1).astype(
        jnp.bfloat16
    )
    column_sums = jnp.sum(grad_projected.astype(jnp.float32), axis=0)
    grad_weight_joint = contract_rows(inputs, grad_projected)
    in_grad = grad_sum_first + contract_cols(grad_projected, weight_joint)
    att_pad = att_back.shape[0] - (4 * D * D + 5 * D)
    attn_full = jnp.concatenate(
        [
            grad_weight_joint.reshape(-1),
            grad_weight_out.reshape(-1),
            column_sums[:D],
            column_sums[2 * D :],
            grad_bias_out,
            grad_gain_first,
            grad_shift_first,
            jnp.zeros((att_pad,), jnp.float32),
        ]
    )
    attn_grad = lax.psum_scatter(attn_full, "fsdp", scatter_dimension=0, tiled=True)
    return (layer_out, in_grad.reshape(row_count, SLOTS, D), attn_grad, ffn_grad, out_bias_grad)


def body(layer_in, pair_ids, pair_lengths, attn_shard, ffn_shard, out_grad, devices):
    plan = Plan(devices, attn_shard.shape[0], ffn_shard.shape[0], layer_in.shape[0])
    run = functools.partial(fused_body, plan) if plan.fits() else plain_body
    return run(layer_in, pair_ids, pair_lengths, attn_shard, ffn_shard, out_grad)


def solution(mesh):
    placed = (
        P("fsdp", None, None),
        P("fsdp", None),
        P("fsdp", None, None),
        P("fsdp"),
        P("fsdp"),
        P("fsdp", None, None),
    )
    return jax.shard_map(
        functools.partial(body, devices=mesh.shape["fsdp"]),
        mesh=mesh,
        in_specs=placed,
        out_specs=(P("fsdp", None, None), P("fsdp", None, None), P("fsdp"), P("fsdp"), P()),
        check_vma=False,
    )
```
